512 devices in a mesh: dp: 32 (over x, y), seq: 16 (over z, core).
Axes of the slice: x: 4, y: 8, z: 8, core: 2. Of those that a mesh axis runs over, the one named last changes fastest.
Arguments:
- encoder_timesteps: bfloat16 [8192, 16, 1536], P(('dp', 'seq')), may hold values from -10 to 10
- tile_parent_sequence: int32 [8192], P(('dp', 'seq')), may hold values from 0 to 15, as said below
- tile_recording_label: int32 [8192], P(('dp', 'seq')), may hold values from 0 to 3
- tile_valid_timesteps: int32 [8192], P(('dp', 'seq')), may hold values from 1 to 16, as said below
- standardize_scaling: float32 [1536], replicated, may hold values from 0.5 to 1.5
- triple_projector: bfloat16 [1536, 2304], P('dp'), may hold values from -0.15625 to 0.15625
- final_projector: bfloat16 [768, 1536], P('dp'), may hold values from -0.21875 to 0.21875
- lowered_maps: bfloat16 [2, 1536, 64], P(None, 'dp'), may hold values from -0.15625 to 0.15625
- raising_maps: bfloat16 [2, 64, 768], P(None, None, 'dp'), may hold values from -0.75 to 0.75
- focus_softness: float32 [8], replicated, may hold values from 2 to 12
- result_adjoint: bfloat16 [8192, 16, 1536], P(('dp', 'seq')), may hold values from -0.015625 to 0.015625
Outputs:
- block_out: bfloat16 [8192, 16, 1536], P(('dp', 'seq'))
- down_gradient: float32 [2, 1536, 64], P(None, 'dp')
- up_gradient: float32 [2, 64, 768], P(None, None, 'dp')
The draws below stay inside these ranges and needn't reach their ends.
Inputs may be any that keep to these rules, and one draw needn't show every extreme that they name: `tile_parent_sequence`: at most 2 panels of one device go to one owner, and in every dp group one owner receives exactly 2 panels from every device of the group. `tile_valid_timesteps`: A clip is the set of panels of one dp group with the same tile_parent_sequence and tile_recording_label; every panel of a clip holds 16 frames except the clip's last panel in order of panel index.
All inputs are finite; a program needn't handle non-finite values.
Results may differ from the reference program's by a relative error of at most 0.028.
Values may be sent and summed in bfloat16 or wider, within the bound.
No kernel may reach another device: no remote copies, remote signals or barrier semaphores. Data moves between devices by JAX's collectives and lax.ppermute only.
A program may use at most 128 MiB of HBM per device.

```python
import math
import jax
import jax.numpy as jnp
from jax import lax

MODEL_DIM = 1536
HALF_FOCI = 8
HD = 96
ADAPTER_RANK = 64
PANEL = 16
PAN_DEV = 16
TAGS = 4
CAP = 2
HEADS_WIDTH = 768
ALL_PAN = 8192
N_DP = 32
N_SEQ = 16


def draw_encoder_timesteps(key, part):
    key = jax.random.fold_in(key, 5)
    column_key = jax.random.fold_in(key, 1)
    value_key = jax.random.fold_in(key, 2)
    column_scale = jnp.exp(jax.random.uniform(column_key, (MODEL_DIM,), jnp.float32, 0.0, math.log(10.0)))
    values = jnp.clip(jax.random.normal(value_key, (ALL_PAN, PANEL, MODEL_DIM), jnp.float32), -4.0, 4.0) * column_scale / 4.0
    return values.astype(jnp.bfloat16)


def packing(key):
    owner_base = jax.random.fold_in(key, 7)
    full_key, other_key, order_key = jax.random.split(owner_base, 3)
    group_count = ALL_PAN // (PAN_DEV * N_SEQ)
    full_owner = jax.random.randint(full_key, (group_count, 1, 1), 0, N_SEQ)
    random_scores = jax.random.randint(other_key, (group_count, N_SEQ, N_SEQ - 1), 0, 1 << 20) * N_SEQ + jnp.arange(N_SEQ - 1)
    other_order = jnp.argsort(random_scores, axis=-1, stable=True)
    other_owner = (full_owner + 1 + other_order) % N_SEQ
    cycle_index = jnp.arange(PAN_DEV - CAP) % (N_SEQ - 1)
    rest_owner = jnp.take(other_owner, cycle_index, axis=2)
    head_owner = jnp.broadcast_to(full_owner, (group_count, N_SEQ, CAP))
    listed = jnp.concatenate([head_owner, rest_owner], axis=2)
    shuffle_scores = jax.random.randint(order_key, (group_count, N_SEQ, PAN_DEV), 0, 1 << 20) * PAN_DEV + jnp.arange(PAN_DEV)
    shuffle_order = jnp.argsort(shuffle_scores, axis=-1, stable=True)
    owners = jnp.take_along_axis(listed, shuffle_order, axis=2).reshape(group_count, N_SEQ * PAN_DEV).astype(jnp.int32)
    tags = jax.random.randint(jax.random.fold_in(key, 11), (group_count, N_SEQ * PAN_DEV), 0, TAGS).astype(jnp.int32)
    clips = owners * TAGS + tags
    group_panels = N_SEQ * PAN_DEV
    index = jnp.arange(group_panels, dtype=jnp.int32)
    same_clip = clips[:, :, None] == clips[:, None, :]
    later = index[None, None, :] > index[None, :, None]
    is_last = jnp.logical_not(jnp.any(same_clip & later, axis=2))
    tail = jax.random.randint(jax.random.fold_in(key, 13), (group_count, group_panels), 1, PANEL + 1)
    lengths = jnp.where(is_last, tail, PANEL)
    first_last = jnp.min(jnp.where(is_last, index[None, :], group_panels), axis=1, keepdims=True)
    lengths = jnp.where(index[None, :] == first_last, 1, lengths)
    lengths = jnp.where(index[None, :] == group_panels - 1, PANEL, lengths)
    return (owners.reshape(ALL_PAN), tags.reshape(ALL_PAN), lengths.reshape(ALL_PAN).astype(jnp.int32))


def draw_tile_parent_sequence(key, part):
    return packing(key)[0]


def draw_tile_recording_label(key, part):
    return packing(key)[1]


def draw_tile_valid_timesteps(key, part):
    return packing(key)[2]


def shard_levels(rng, extent, cuts, smallest, high):
    gain = 1.0
    for position, blocks in cuts:
        draws = jax.random.uniform(jax.random.fold_in(jax.random.fold_in(rng, 6), position), (blocks,), jnp.float32, smallest / len(cuts), high / len(cuts))
        gain = gain * jnp.repeat(jnp.exp(draws), extent[position] // blocks).reshape((-1,) + (1,) * (len(extent) - 1 - position))
    return gain


def noise(key, shape, width, limit, shards=(), held_as=jnp.bfloat16):
    entries = width * jax.random.normal(key, shape, jnp.float32)
    if shards:
        entries = entries * shard_levels(key, shape, shards, -0.22, 0.18)
    return jnp.clip(entries, -limit, limit).astype(held_as)


def setup_inputs(seed: int = 0) -> dict:
    arg_keys = jax.random.split(jax.random.key(seed), 12)
    encoder_timesteps = draw_encoder_timesteps(jax.random.fold_in(arg_keys[11], 71), 0)
    tile_parent_sequence = draw_tile_parent_sequence(jax.random.fold_in(arg_keys[11], 71), 0)
    tile_recording_label = draw_tile_recording_label(jax.random.fold_in(arg_keys[11], 71), 0)
    tile_valid_timesteps = draw_tile_valid_timesteps(jax.random.fold_in(arg_keys[11], 71), 0)
    standardize_scaling = jnp.clip(1.0 + 0.1 * jax.random.normal(arg_keys[4], (MODEL_DIM,), jnp.float32), 0.5, 1.5)
    triple_projector = noise(arg_keys[5], (MODEL_DIM, 3 * HEADS_WIDTH), MODEL_DIM ** -0.5, 0.15625, ((0, 32),))
    final_projector = noise(arg_keys[6], (HEADS_WIDTH, MODEL_DIM), HEADS_WIDTH ** -0.5, 0.21875, ((0, 32),))
    lowered_maps = noise(arg_keys[7], (2, MODEL_DIM, ADAPTER_RANK), MODEL_DIM ** -0.5, 0.15625, ((1, 32),))
    raising_maps = noise(arg_keys[8], (2, ADAPTER_RANK, HEADS_WIDTH), ADAPTER_RANK ** -0.5, 0.75, ((2, 32),))
    focus_softness = jnp.clip(jnp.exp(jax.random.uniform(arg_keys[9], (HALF_FOCI,), jnp.float32, math.log(2.0), math.log(12.0))), 2.0, 12.0)
    result_adjoint = noise(arg_keys[10], (ALL_PAN, PANEL, MODEL_DIM), ((ALL_PAN * PANEL) ** -0.5), 0.015625, ((0, 512),))
    return dict(encoder_timesteps=encoder_timesteps, tile_parent_sequence=tile_parent_sequence, tile_recording_label=tile_recording_label, tile_valid_timesteps=tile_valid_timesteps, standardize_scaling=standardize_scaling, triple_projector=triple_projector, final_projector=final_projector, lowered_maps=lowered_maps, raising_maps=raising_maps, focus_softness=focus_softness, result_adjoint=result_adjoint)


EPS_NORM = 1e-05
EPS_HEAD = 1e-06

def layer_norm(encoder_timesteps, standardize_scaling):
    values = encoder_timesteps.astype(jnp.float32)
    centred = values - lax.optimization_barrier(jnp.mean(values, axis=-1, keepdims=True))
    scaled = centred * lax.rsqrt(lax.optimization_barrier(jnp.mean(centred * centred, axis=-1, keepdims=True)) + EPS_NORM)
    return (scaled * standardize_scaling).astype(jnp.bfloat16)

def slot_matrix(tile_parent_sequence, slots_each, owner_count):
    panels_here = tile_parent_sequence.shape[0]
    owner_hits = (tile_parent_sequence[:, None] == jnp.arange(owner_count, dtype=jnp.int32)[None, :]).astype(jnp.int32)
    earlier = (jnp.arange(panels_here, dtype=jnp.int32)[:, None] > jnp.arange(panels_here, dtype=jnp.int32)[None, :]).astype(jnp.int32)
    before = jnp.dot(earlier, owner_hits)
    slot_rank = lax.optimization_barrier(jnp.sum(before * owner_hits, axis=1))
    slot_place = tile_parent_sequence * slots_each + slot_rank
    return (slot_place[None, :] == jnp.arange(owner_count * slots_each, dtype=jnp.int32)[:, None]).astype(jnp.float32)

def apply_focus(asker_vectors, lookup_vectors, payload_vectors, timestep_labels, timestep_valid, focus_softness):
    row_count = asker_vectors.shape[0]
    focus_number = focus_softness.shape[0]

    def divide_foci(array):
        return jnp.swapaxes(array.reshape(row_count, focus_number, -1), 0, 1)
    diagonal = jnp.arange(row_count)[:, None] == jnp.arange(row_count)[None, :]
    allowed = (timestep_labels[:, None] == timestep_labels[None, :]) & (timestep_valid[None, :] > 0.5) | diagonal

    def single_focus(focus_elements):
        focus_askers, focus_lookups, focus_payloads, logit_softness = focus_elements
        broad_askers = focus_askers.astype(jnp.float32)
        key_wide = focus_lookups.astype(jnp.float32)
        normed_askers = broad_askers * lax.rsqrt(lax.optimization_barrier(jnp.mean(broad_askers * broad_askers, axis=-1, keepdims=True)) + EPS_HEAD)
        normed_lookups = key_wide * lax.rsqrt(lax.optimization_barrier(jnp.mean(key_wide * key_wide, axis=-1, keepdims=True)) + EPS_HEAD)
        focus_logits = jnp.dot(normed_askers, normed_lookups.T, precision=lax.Precision.HIGHEST) * (logit_softness / broad_askers.shape[-1])
        unnormed = jnp.where(allowed, jnp.exp(focus_logits), 0.0)
        weights = (unnormed / lax.optimization_barrier(jnp.sum(unnormed, axis=-1, keepdims=True))).astype(jnp.bfloat16)
        return jnp.dot(weights, focus_payloads, preferred_element_type=jnp.float32)
    mixed_result = lax.map(single_focus, (divide_foci(asker_vectors), divide_foci(lookup_vectors), divide_foci(payload_vectors), focus_softness))
    return jnp.swapaxes(mixed_result, 0, 1).reshape(row_count, -1)

def reference(encoder_timesteps, tile_parent_sequence, tile_recording_label, tile_valid_timesteps, standardize_scaling, triple_projector, final_projector, lowered_maps, raising_maps, focus_softness, result_adjoint):
    head_width = HALF_FOCI * HD
    slot_total = N_SEQ * CAP
    shape_source = (N_SEQ, PAN_DEV, PANEL, -1)

    def one_group(group_items):
        group_frames, group_owner, group_tag, group_live, group_cotangent = group_items
        normalized_rows = layer_norm(group_frames, standardize_scaling).reshape(-1, MODEL_DIM)
        base_proj = jnp.dot(normalized_rows, triple_projector, preferred_element_type=jnp.float32)
        rank_product = jnp.einsum('eg,igp->iep', normalized_rows.astype(jnp.float32), lowered_maps.astype(jnp.float32)).astype(jnp.bfloat16)
        adapter_index = jnp.einsum('dyj,djo->dyo', rank_product.astype(jnp.float32), raising_maps.astype(jnp.float32))
        asker_vectors = (base_proj[:, :head_width] + adapter_index[0]).astype(jnp.bfloat16)
        lookup_vectors = base_proj[:, head_width:2 * head_width].astype(jnp.bfloat16)
        payload_vectors = (base_proj[:, 2 * head_width:] + adapter_index[1]).astype(jnp.bfloat16)
        select = jax.vmap(lambda owner_row: slot_matrix(owner_row, CAP, N_SEQ))(group_owner)

        def to_owners(data):
            packed = jnp.einsum('asp,apfw->asfw', select, data.reshape(shape_source).astype(jnp.float32)).astype(data.dtype)
            packed = packed.reshape(N_SEQ, N_SEQ, CAP, PANEL, -1)
            return jnp.swapaxes(packed, 0, 1).reshape(N_SEQ, slot_total * PANEL, -1)

        def to_sources(data):
            parts = data.reshape(N_SEQ, N_SEQ, CAP, PANEL, -1)
            parts = jnp.swapaxes(parts, 0, 1).reshape(N_SEQ, slot_total, PANEL, -1)
            unpacked = jnp.einsum('asp,asfw->apfw', select, parts.astype(jnp.float32))
            return unpacked.astype(data.dtype).reshape(N_SEQ * PAN_DEV * PANEL, -1)
        positions = jnp.arange(PANEL, dtype=jnp.int32)
        live_source = (positions[None, None, :] < group_live[:, :, None]).astype(jnp.float32)
        tag_source = jnp.broadcast_to(group_tag[:, :, None], live_source.shape).astype(jnp.float32)
        timestep_labels = to_owners(tag_source.reshape(-1, 1))[..., 0]
        timestep_valid = to_owners(live_source.reshape(-1, 1))[..., 0]
        lookup_holder = to_owners(lookup_vectors)

        def run(asker_lowered, payload_lowered):
            return jax.vmap(apply_focus, in_axes=(0, 0, 0, 0, 0, None))(asker_lowered, lookup_holder, payload_lowered, timestep_labels, timestep_valid, focus_softness)
        mixed_result, pullback = jax.vjp(run, to_owners(asker_vectors), to_owners(payload_vectors))
        context_source = to_sources(mixed_result.astype(jnp.bfloat16))
        live_column = live_source.reshape(-1, 1)
        attn_out = jnp.dot(context_source, final_projector, preferred_element_type=jnp.float32)
        block_out = (group_frames.reshape(-1, MODEL_DIM).astype(jnp.float32) + live_column * attn_out).astype(jnp.bfloat16)
        masked = (group_cotangent.reshape(-1, MODEL_DIM).astype(jnp.float32) * live_column).astype(jnp.bfloat16)
        d_context = jnp.dot(masked, final_projector.T, preferred_element_type=jnp.float32).astype(jnp.bfloat16)
        d_query_owner, d_value_owner = pullback(to_owners(d_context).astype(jnp.float32))
        query_gradient = to_sources(d_query_owner)
        value_gradient = to_sources(d_value_owner)
        gradient_pairs = jnp.stack([query_gradient, value_gradient]).astype(jnp.float32)
        up_gradient = jnp.einsum('nfr,nfw->nrw', rank_product.astype(jnp.float32), gradient_pairs)
        inner_gradient = jnp.einsum('ydh,yih->ydi', gradient_pairs, raising_maps.astype(jnp.float32)).astype(jnp.bfloat16)
        down_gradient = jnp.einsum('fd,nfr->ndr', normalized_rows.astype(jnp.float32), inner_gradient.astype(jnp.float32))
        return (block_out.reshape(N_SEQ * PAN_DEV, PANEL, MODEL_DIM), down_gradient, up_gradient)
    group_shape = (N_DP, N_SEQ, PAN_DEV)
    outputs = lax.map(one_group, (encoder_timesteps.reshape(N_DP, N_SEQ, PAN_DEV, PANEL, MODEL_DIM), tile_parent_sequence.reshape(group_shape), tile_recording_label.reshape(group_shape), tile_valid_timesteps.reshape(group_shape), result_adjoint.reshape(N_DP, N_SEQ, PAN_DEV, PANEL, MODEL_DIM)))
    block_out = outputs[0].reshape(ALL_PAN, PANEL, MODEL_DIM)
    return (block_out, lax.optimization_barrier(jnp.sum(outputs[1], axis=0)), lax.optimization_barrier(jnp.sum(outputs[2], axis=0)))
```

```python
import math

import jax
import jax.numpy as jnp
from jax import lax
from jax.experimental import pallas as pl
from jax.experimental.pallas import tpu as pltpu
from jax.sharding import PartitionSpec as P

EPS_NORM = 1e-05
EPS_HEAD = 1e-06
WIDE = 1536
PANELS = 16
LEN = 16
ROWS = PANELS * LEN
OWNERS = 16
SLOTS = 2
PACKED = OWNERS * SLOTS * LEN
HEAD = 96
FOCI = 4
HALF = FOCI * HEAD
RANK = 64
SHARDS = 32
BLOCK = WIDE // SHARDS
UPS = 2 * HALF // SHARDS
GRAD = 80
QKVL = 3 * HALF + 2 * RANK
F32 = jnp.float32
BF16 = jnp.bfloat16
SMEM = pltpu.MemorySpace.SMEM
VMEM = pltpu.MemorySpace.VMEM


def dot(a, b):
    return lax.dot_general(a, b, (((1,), (0,)), ((), ())), preferred_element_type=F32)


def dot_nt(a, b):
    return lax.dot_general(a, b, (((1,), (1,)), ((), ())), preferred_element_type=F32)


def slot_places(owner_ref):
    owners = [owner_ref[p] for p in range(PANELS)]
    places = []
    for p in range(PANELS):
        rank = jnp.int32(0)
        for q in range(p):
            rank = rank + jnp.where(owners[q] == owners[p], 1, 0)
        places.append(owners[p] * SLOTS + rank)
    return places


def spread(scalars, shape, axis):
    index = lax.broadcasted_iota(jnp.int32, shape, axis)
    panel = index // LEN
    values = jnp.zeros(shape, jnp.int32)
    for p in range(PANELS):
        values = jnp.where(panel == p, scalars[p], values)
    return values, index % LEN


def pack_kernel(owner_ref, live_ref, x_ref, adjoint_ref, gain_ref, normed_ref, masked_ref):
    place, step = spread(slot_places(owner_ref), (1, ROWS), 1)
    target = place * LEN + step
    slots = lax.broadcasted_iota(jnp.int32, (PACKED, ROWS), 0)
    select = jnp.where(slots == target, 1.0, 0.0).astype(BF16)
    values = x_ref[...].astype(F32)
    centred = values - jnp.mean(values, axis=-1, keepdims=True)
    scaled = centred * lax.rsqrt(jnp.mean(centred * centred, axis=-1, keepdims=True) + EPS_NORM)
    normed = (scaled * gain_ref[...]).astype(BF16)
    normed_ref[...] = dot(select, normed).astype(BF16).reshape(normed_ref.shape)
    lives, step = spread([live_ref[p] for p in range(PANELS)], (ROWS, 1), 0)
    masked = jnp.where(step < lives, adjoint_ref[...].astype(F32), 0.0).astype(BF16)
    masked_ref[...] = dot(select, masked).astype(BF16).reshape(masked_ref.shape)


def pack(owners, lives, x, adjoint, gain):
    packed = jax.ShapeDtypeStruct((OWNERS, SLOTS * LEN, WIDE), BF16)
    return pl.pallas_call(
        pack_kernel,
        out_shape=(packed, packed),
        in_specs=[pl.BlockSpec(memory_space=SMEM)] * 2 + [pl.BlockSpec(memory_space=VMEM)] * 3,
        out_specs=(pl.BlockSpec(memory_space=VMEM),) * 2,
        compiler_params=pltpu.CompilerParams(vmem_limit_bytes=40 << 20),
        cost_estimate=pl.CostEstimate(
            flops=4 * PACKED * ROWS * WIDE, bytes_accessed=6 * PACKED * WIDE, transcendentals=0
        ),
        name="pack",
    )(owners, lives, x, adjoint, gain)


def pad_rows(values, rows=128):
    return jnp.concatenate([values, jnp.zeros((rows - values.shape[0], values.shape[1]), values.dtype)], axis=0)


def focus_kernel(
    core_ref,
    soft_ref,
    normed_ref,
    masked_ref,
    tag_ref,
    code_ref,
    weight_ref,
    out_a_ref,
    out_b_ref,
    raise_ref,
    context_ref,
    grads_ref,
    base_s,
    query_s,
    key_s,
    value_s,
    cot_s,
    context_s,
    dquery_s,
    dvalue_s,
    down_s,
    up_s,
):
    owner = pl.program_id(0)
    core = core_ref[0]

    @pl.when(owner == 0)
    def _():
        down_s[...] = jnp.zeros_like(down_s)
        up_s[...] = jnp.zeros_like(up_s)

    @pl.loop(0, QKVL // 256)
    def _(n):
        columns = pl.ds(pl.multiple_of(n * 256, 256), 256)
        base_s[:, columns] = dot(normed_ref[...], weight_ref[:, columns])

    low = base_s[:, 3 * HALF :].astype(BF16)
    raising = raise_ref[...].astype(F32).T
    row = lax.broadcasted_iota(jnp.int32, raising.shape, 0)
    raise_q = jnp.where(row < RANK, raising, 0.0).astype(BF16)
    raise_v = jnp.where(row < RANK, 0.0, raising).astype(BF16)
    query = (base_s[:, :HALF] + dot(low, raise_q)).astype(BF16)
    query_s[...] = query.astype(F32).T
    key_s[...] = base_s[:, HALF : 2 * HALF].astype(BF16).astype(F32).T
    value = (base_s[:, 2 * HALF : 3 * HALF] + dot(low, raise_v)).astype(BF16)
    value_s[...] = value.astype(F32).T
    cot = dot_nt(out_a_ref[...], masked_ref[:, : WIDE // 2]) + dot_nt(
        out_b_ref[...], masked_ref[:, WIDE // 2 :]
    )
    cot_s[...] = cot.astype(BF16).astype(F32)

    rows_j = lax.broadcasted_iota(jnp.int32, (PACKED, PACKED), 0)
    rows_i = lax.broadcasted_iota(jnp.int32, (PACKED, PACKED), 1)
    allowed = (tag_ref[0:1, :] == code_ref[...]) | (rows_j == rows_i)
    ones_rows = jnp.where(lax.broadcasted_iota(jnp.int32, (32, PACKED), 0) < 2, 1.0, 0.0)
    sub = lax.broadcasted_iota(jnp.int32, (32, PACKED), 0)

    for h in range(FOCI):
        head = slice(h * HEAD, (h + 1) * HEAD)
        temper = soft_ref[core * FOCI + h] * (1.0 / HEAD)
        q = query_s[head, :]
        rq = lax.rsqrt(jnp.sum(q * q, axis=0, keepdims=True) * (1.0 / HEAD) + EPS_HEAD)
        qn = q * rq
        k = key_s[head, :]
        kn = k * lax.rsqrt(jnp.sum(k * k, axis=0, keepdims=True) * (1.0 / HEAD) + EPS_HEAD)
        kn = pad_rows(kn)
        qs = pad_rows(qn * (temper * math.log2(math.e))).astype(BF16)
        v = jnp.concatenate([value_s[head, :], ones_rows], axis=0)
        scores = dot(kn.T.astype(BF16), qs)
        unnormed = jnp.exp2(jnp.where(allowed, scores, -1e30)).astype(BF16)
        mixed = dot(v.astype(BF16), unnormed)
        inverse = 1.0 / mixed[HEAD : HEAD + 1, :]
        context = mixed[:HEAD, :] * inverse
        context_s[head, :] = context
        dc = (cot_s[head, :] * inverse).astype(BF16)
        shift = jnp.sum(dc.astype(F32) * context, axis=0, keepdims=True)
        shift_top = shift.astype(BF16).astype(F32)
        extra = jnp.where(sub == 0, -shift_top, jnp.where(sub == 1, shift_top - shift, 0.0))
        dc = jnp.concatenate([dc, extra.astype(BF16)], axis=0)
        inner = dot(v.T.astype(BF16), dc)
        dscores = (unnormed.astype(F32) * inner).astype(BF16)
        dqn = dot(kn.astype(BF16), dscores)[:HEAD, :] * temper
        dq = rq * (dqn - qn * (jnp.sum(qn * dqn, axis=0, keepdims=True) * (1.0 / HEAD)))
        dquery_s[head, :] = dq.astype(BF16)
        dv = dot_nt(unnormed, dc)
        dvalue_s[head, :] = dv.T[:HEAD, :].astype(BF16)

    context_ref[...] = context_s[...].T.astype(BF16).reshape(context_ref.shape)
    dquery = dquery_s[...]
    dvalue = dvalue_s[...]
    lane = lax.broadcasted_iota(jnp.int32, (HALF, 2 * RANK), 1)
    up_s[...] += jnp.where(lane < RANK, dot(dquery, low), dot(dvalue, low))
    inner_t = (dot(raise_q, dquery) + dot(raise_v, dvalue)).astype(BF16)
    down_s[...] += dot(inner_t, normed_ref[...])

    @pl.when(owner == 1)
    def _():
        grads_ref[...] = jnp.zeros_like(grads_ref)
        grads_ref[:, :BLOCK, :] = down_s[...].T.astype(BF16).reshape(SHARDS, BLOCK, 2 * RANK)
        for t in range(SHARDS // 2):
            part = pad_rows(up_s[t * UPS : (t + 1) * UPS, :], GRAD - BLOCK).astype(BF16)
            grads_ref[core * (SHARDS // 2) + t, BLOCK:, :] = part


def focus(core, soft, normed, masked, tags, codes, weights, out_a, out_b, raising):
    once = pl.Buffered(1)
    grid = pltpu.PrefetchScalarGridSpec(
        num_scalar_prefetch=1,
        grid=(2,),
        in_specs=[
            pl.BlockSpec(memory_space=SMEM),
            pl.BlockSpec((None, PACKED, WIDE), lambda o, c: (o, 0, 0)),
            pl.BlockSpec((None, PACKED, WIDE), lambda o, c: (o, 0, 0)),
            pl.BlockSpec((None, 8, PACKED), lambda o, c: (o, 0, 0)),
            pl.BlockSpec((None, PACKED, 1), lambda o, c: (o, 0, 0)),
            pl.BlockSpec((WIDE, QKVL), lambda o, c: (0, 0), pipeline_mode=once),
            pl.BlockSpec((HALF, WIDE // 2), lambda o, c: (c[0], 0), pipeline_mode=once),
            pl.BlockSpec((HALF, WIDE // 2), lambda o, c: (c[0], 0), pipeline_mode=once),
            pl.BlockSpec((HALF, 2 * RANK), lambda o, c: (c[0], 0), pipeline_mode=once),
        ],
        out_specs=[
            pl.BlockSpec((OWNERS, None, SLOTS * LEN, HALF), lambda o, c: (0, o, 0, 0)),
            pl.BlockSpec((SHARDS, GRAD, 2 * RANK), lambda o, c: (0, 0, 0)),
        ],
        scratch_shapes=[
            pltpu.VMEM((PACKED, QKVL), F32),
            pltpu.VMEM((HALF, PACKED), F32),
            pltpu.VMEM((HALF, PACKED), F32),
            pltpu.VMEM((HALF, PACKED), F32),
            pltpu.VMEM((HALF, PACKED), F32),
            pltpu.VMEM((HALF, PACKED), F32),
            pltpu.VMEM((HALF, PACKED), BF16),
            pltpu.VMEM((HALF, PACKED), BF16),
            pltpu.VMEM((2 * RANK, WIDE), F32),
            pltpu.VMEM((HALF, 2 * RANK), F32),
        ],
    )
    return pl.pallas_call(
        focus_kernel,
        grid_spec=grid,
        out_shape=(
            jax.ShapeDtypeStruct((OWNERS, 2, SLOTS * LEN, HALF), BF16),
            jax.ShapeDtypeStruct((SHARDS, GRAD, 2 * RANK), BF16),
        ),
        compiler_params=pltpu.CompilerParams(
            vmem_limit_bytes=56 << 20, dimension_semantics=("arbitrary",)
        ),
        cost_estimate=pl.CostEstimate(
            flops=12 << 30, bytes_accessed=16 << 20, transcendentals=2 * FOCI * PACKED * PACKED
        ),
        name="focus",
    )(core, soft, normed, masked, tags, codes, weights, out_a, out_b, raising)


def finish_kernel(owner_ref, live_ref, context_ref, x_ref, out_a_ref, out_b_ref, block_ref):
    place, step = spread(slot_places(owner_ref), (ROWS, 1), 0)
    target = place * LEN + step
    slots = lax.broadcasted_iota(jnp.int32, (ROWS, PACKED), 1)
    select = jnp.where(slots == target, 1.0, 0.0).astype(BF16)
    lives, _ = spread([live_ref[p] for p in range(PANELS)], (ROWS, 1), 0)
    halves = []
    for half in range(2):
        parts = []
        for o in range(OWNERS):
            source = o // 2 * 2 + half
            first = 0 if source == o else SLOTS * LEN
            parts.append(context_ref[source, first : first + SLOTS * LEN, :])
        halves.append(dot(select, jnp.concatenate(parts, axis=0)).astype(BF16))
    for side, ref in enumerate((out_a_ref, out_b_ref)):
        columns = slice(side * WIDE // 2, (side + 1) * WIDE // 2)
        attended = dot(halves[0], ref[:HALF, :]) + dot(halves[1], ref[HALF:, :])
        added = jnp.where(step < lives, attended, 0.0)
        block_ref[:, columns] = (x_ref[:, columns].astype(F32) + added).astype(BF16)


def finish(owners, lives, context, x, out_a, out_b):
    return pl.pallas_call(
        finish_kernel,
        out_shape=jax.ShapeDtypeStruct((ROWS, WIDE), BF16),
        in_specs=[pl.BlockSpec(memory_space=SMEM)] * 2 + [pl.BlockSpec(memory_space=VMEM)] * 4,
        out_specs=pl.BlockSpec(memory_space=VMEM),
        compiler_params=pltpu.CompilerParams(vmem_limit_bytes=40 << 20),
        cost_estimate=pl.CostEstimate(
            flops=2 * ROWS * 2 * HALF * (WIDE + PACKED), bytes_accessed=6 << 20, transcendentals=0
        ),
        name="finish",
    )(owners, lives, context, x, out_a, out_b)


def add_shards_kernel(part_ref, total_ref):
    total = part_ref[0].astype(F32)
    for t in range(1, SHARDS):
        total = total + part_ref[t].astype(F32)
    total = total.astype(BF16)
    for o in range(OWNERS):
        total_ref[o] = total


def add_shards(parts):
    return pl.pallas_call(
        add_shards_kernel,
        out_shape=jax.ShapeDtypeStruct((OWNERS, GRAD, 2 * RANK), BF16),
        in_specs=[pl.BlockSpec(memory_space=VMEM)],
        out_specs=pl.BlockSpec(memory_space=VMEM),
        name="add_shards",
    )(parts)


def add_owners_kernel(part_ref, down_ref, up_ref):
    total = part_ref[0].astype(F32)
    for o in range(1, OWNERS):
        total = total + part_ref[o].astype(F32)
    up = pad_rows(total[BLOCK : BLOCK + UPS, :]).T
    for n in range(2):
        down_ref[n] = total[:BLOCK, n * RANK : (n + 1) * RANK]
        up_ref[n] = up[n * RANK : (n + 1) * RANK, :UPS]


def add_owners(parts):
    return pl.pallas_call(
        add_owners_kernel,
        out_shape=(
            jax.ShapeDtypeStruct((2, BLOCK, RANK), F32),
            jax.ShapeDtypeStruct((2, RANK, UPS), F32),
        ),
        in_specs=[pl.BlockSpec(memory_space=VMEM)],
        out_specs=(pl.BlockSpec(memory_space=VMEM),) * 2,
        name="add_owners",
    )(parts)


def exchange(data, axis):
    return lax.all_to_all(data, axis, split_axis=0, concat_axis=0, tiled=True)


def swap_cores(data):
    pairs = [(s, s ^ 1) for s in range(OWNERS)]
    return lax.ppermute(data, "seq", pairs)


def panel_facts(owners, tags, lives):
    same = owners[:, None] == owners[None, :]
    order = jnp.arange(PANELS, dtype=jnp.int32)
    rank = jnp.sum((same & (order[:, None] > order[None, :])).astype(jnp.int32), axis=1)
    place = owners * SLOTS + rank
    hits = place[None, :] == jnp.arange(OWNERS * SLOTS, dtype=jnp.int32)[:, None]
    facts = [jnp.sum(jnp.where(hits, fact[None, :], 0), axis=1) for fact in (tags, lives)]
    sent = jnp.stack(facts, axis=-1).astype(BF16).reshape(OWNERS // 2, 2, SLOTS * 2)
    both = jnp.stack([sent, sent[:, ::-1]], axis=2).reshape(OWNERS, 2, SLOTS, 2)
    received = exchange(both, "seq").astype(F32)
    received = jnp.swapaxes(received, 0, 1).reshape(2, OWNERS * SLOTS, 1, 2)
    steps = jnp.arange(LEN, dtype=jnp.int32).astype(F32)[None, None, :]
    tag = jnp.broadcast_to(received[..., 0], (2, OWNERS * SLOTS, LEN))
    code = jnp.where(steps < received[..., 1], tag, -1.0)
    rows = jnp.broadcast_to(tag.reshape(2, 1, PACKED), (2, 8, PACKED))
    return rows, code.reshape(2, PACKED, 1)


def on_device(
    encoder_timesteps,
    tile_parent_sequence,
    tile_recording_label,
    tile_valid_timesteps,
    standardize_scaling,
    triple_projector,
    final_projector,
    lowered_maps,
    raising_maps,
    focus_softness,
    result_adjoint,
):
    core = lax.axis_index("seq") % 2
    starts = [n * 2 * HALF for n in range(3)]
    triple = [
        jnp.where(
            core == 0,
            triple_projector[:, first : first + HALF],
            triple_projector[:, first + HALF : first + 2 * HALF],
        )
        for first in starts
    ]
    lowered = jnp.concatenate([lowered_maps[0], lowered_maps[1]], axis=1)
    outward = jnp.concatenate([final_projector[:, : WIDE // 2], final_projector[:, WIDE // 2 :]], axis=0)
    raising = raising_maps.reshape(2 * RANK, UPS).T
    raising = jnp.concatenate([raising, jnp.zeros_like(raising)], axis=0)
    shard = jnp.concatenate([*triple, lowered, outward, raising], axis=1)
    whole = lax.all_gather(shard, "dp", axis=0, tiled=True)

    x = encoder_timesteps.reshape(ROWS, WIDE)
    normed, masked = pack(
        tile_parent_sequence,
        tile_valid_timesteps,
        x,
        result_adjoint.reshape(ROWS, WIDE),
        standardize_scaling.reshape(1, WIDE),
    )
    tag_rows, codes = panel_facts(tile_parent_sequence, tile_recording_label, tile_valid_timesteps)
    normed = exchange(normed, "seq")
    masked = exchange(masked, "seq")
    normed = jnp.stack([normed, swap_cores(normed)]).reshape(2, PACKED, WIDE)
    masked = jnp.stack([masked, swap_cores(masked)]).reshape(2, PACKED, WIDE)

    wide = whole.reshape(SHARDS, BLOCK, -1)
    outs = wide[:, :, QKVL : QKVL + WIDE // 2]
    out_a = outs[:, :UPS].reshape(2 * HALF, WIDE // 2)
    out_b = outs[:, UPS:].reshape(2 * HALF, WIDE // 2)
    raise_all = wide[:, :UPS, QKVL + WIDE // 2 :].reshape(2 * HALF, 2 * RANK)
    context, grads = focus(
        core.reshape(1),
        focus_softness,
        normed,
        masked,
        tag_rows,
        codes,
        whole,
        out_a,
        out_b,
        raise_all,
    )
    context = exchange(context.reshape(OWNERS, 2 * SLOTS * LEN, HALF), "seq")
    grads = exchange(add_shards(exchange(grads, "dp")), "seq")
    shard_down, shard_up = add_owners(grads)
    block_out = finish(tile_parent_sequence, tile_valid_timesteps, context, x, out_a, out_b)
    return block_out.reshape(encoder_timesteps.shape), shard_down, shard_up


def solution(mesh):
    in_specs = (
        P(("dp", "seq"), None, None),
        P(("dp", "seq")),
        P(("dp", "seq")),
        P(("dp", "seq")),
        P(),
        P("dp", None),
        P("dp", None),
        P(None, "dp", None),
        P(None, None, "dp"),
        P(),
        P(("dp", "seq"), None, None),
    )
    out_specs = (P(("dp", "seq"), None, None), P(None, "dp", None), P(None, None, "dp"))
    return jax.shard_map(
        on_device, mesh=mesh, in_specs=in_specs, out_specs=out_specs, check_vma=False
    )
```

```python
import math

import jax
import jax.numpy as jnp
from jax import lax
from jax.experimental import pallas as pl
from jax.experimental.pallas import tpu as pltpu
from jax.sharding import PartitionSpec as P

EPS_NORM = 1e-05
EPS_HEAD = 1e-06
WIDE = 1536
PANELS = 16
LEN = 16
ROWS = PANELS * LEN
OWNERS = 16
SLOTS = 2
PACKED = OWNERS * SLOTS * LEN
HEAD = 96
FOCI = 4
HALF = FOCI * HEAD
RANK = 64
SHARDS = 32
BLOCK = WIDE // SHARDS
UPS = 2 * HALF // SHARDS
GRAD = 2 * UPS
HIDDEN = 2 * HALF
QKVL = 3 * HALF + 2 * RANK
F32 = jnp.float32
BF16 = jnp.bfloat16
SMEM = pltpu.MemorySpace.SMEM
VMEM = pltpu.MemorySpace.VMEM


def dot(a, b):
    return lax.dot_general(a, b, (((1,), (0,)), ((), ())), preferred_element_type=F32)


def dot_nt(a, b):
    return lax.dot_general(a, b, (((1,), (1,)), ((), ())), preferred_element_type=F32)


def slot_places(owner_ref):
    owners = [owner_ref[p] for p in range(PANELS)]
    places = []
    for p in range(PANELS):
        rank = jnp.int32(0)
        for q in range(p):
            rank = rank + jnp.where(owners[q] == owners[p], 1, 0)
        places.append(owners[p] * SLOTS + rank)
    return places


def spread(scalars, shape, axis):
    index = lax.broadcasted_iota(jnp.int32, shape, axis)
    panel = index // LEN
    values = jnp.zeros(shape, jnp.int32)
    for p in range(PANELS):
        values = jnp.where(panel == p, scalars[p], values)
    return values, index % LEN


def pack_kernel(owner_ref, live_ref, x_ref, adjoint_ref, gain_ref, normed_ref, masked_ref):
    place, step = spread(slot_places(owner_ref), (1, ROWS), 1)
    target = place * LEN + step
    slots = lax.broadcasted_iota(jnp.int32, (PACKED, ROWS), 0)
    select = jnp.where(slots == target, 1.0, 0.0).astype(BF16)
    values = x_ref[...].astype(F32)
    centred = values - jnp.mean(values, axis=-1, keepdims=True)
    scaled = centred * lax.rsqrt(jnp.mean(centred * centred, axis=-1, keepdims=True) + EPS_NORM)
    normed = (scaled * gain_ref[...]).astype(BF16)
    normed_ref[...] = dot(select, normed).astype(BF16).reshape(normed_ref.shape)
    lives, step = spread([live_ref[p] for p in range(PANELS)], (ROWS, 1), 0)
    masked = jnp.where(step < lives, adjoint_ref[...].astype(F32), 0.0).astype(BF16)
    masked_ref[...] = dot(select, masked).astype(BF16).reshape(masked_ref.shape)


def pack(owners, lives, x, adjoint, gain):
    packed = jax.ShapeDtypeStruct((OWNERS, SLOTS * LEN, WIDE), BF16)
    return pl.pallas_call(
        pack_kernel,
        out_shape=(packed, packed),
        in_specs=[pl.BlockSpec(memory_space=SMEM)] * 2 + [pl.BlockSpec(memory_space=VMEM)] * 3,
        out_specs=(pl.BlockSpec(memory_space=VMEM),) * 2,
        compiler_params=pltpu.CompilerParams(vmem_limit_bytes=40 << 20),
        cost_estimate=pl.CostEstimate(
            flops=4 * PACKED * ROWS * WIDE, bytes_accessed=6 * PACKED * WIDE, transcendentals=0
        ),
        name="pack",
    )(owners, lives, x, adjoint, gain)


def pad_rows(values, rows=128):
    return jnp.concatenate([values, jnp.zeros((rows - values.shape[0], values.shape[1]), values.dtype)], axis=0)


def owner_copies(sources, landing, sems):
    return [pltpu.make_async_copy(source, landing.at[o], sems.at[o]) for o, source in enumerate(sources)]


def raising_of(raise_s):
    tall = raise_s[...].astype(F32).reshape(SHARDS // 2, BLOCK, 2 * RANK)[:, :UPS]
    raising = tall.reshape(HALF, 2 * RANK).T
    row = lax.broadcasted_iota(jnp.int32, raising.shape, 0)
    raise_q = jnp.where(row < RANK, raising, 0.0).astype(BF16)
    raise_v = jnp.where(row < RANK, 0.0, raising).astype(BF16)
    return raise_q, raise_v


def unit(values):
    scale = lax.rsqrt(jnp.sum(values * values, axis=0, keepdims=True) * (1.0 / HEAD) + EPS_HEAD)
    return values * scale, scale


def forward_kernel(
    core_ref,
    soft_ref,
    tag_ref,
    code_ref,
    mine_ref,
    other_ref,
    whole_ref,
    context_ref,
    weights_ref,
    qkv_ref,
    low_ref,
    mixed_ref,
    inverse_ref,
    normed_s,
    weight_s,
    raise_s,
    base_s,
    row_sems,
    weight_sems,
    raise_sem,
):
    owner = pl.program_id(0)
    core = core_ref[0]
    rows = owner_copies((mine_ref, other_ref), normed_s, row_sems)
    tiles = [
        pltpu.make_async_copy(
            whole_ref.at[:, pl.ds(HIDDEN + n * 256, 256)],
            weight_s.at[:, pl.ds(n * 256, 256)],
            weight_sems.at[n],
        )
        for n in range(QKVL // 256)
    ]
    half = pl.ds(pl.multiple_of(core * (WIDE // 2), WIDE // 2), WIDE // 2)
    raises = pltpu.make_async_copy(
        whole_ref.at[half, pl.ds(HIDDEN + QKVL, 2 * RANK)], raise_s, raise_sem
    )

    @pl.when(owner == 0)
    def _():
        rows[0].start()
        for tile in tiles:
            tile.start()
        raises.start()
        rows[1].start()
        rows[0].wait()

    @pl.when(owner == 1)
    def _():
        rows[1].wait()

    for n, tile in enumerate(tiles):

        @pl.when(owner == 0)
        def _():
            tile.wait()

        columns = slice(n * 256, (n + 1) * 256)
        base_s[:, columns] = dot(normed_s[owner], weight_s[:, columns])

    @pl.when(owner == 0)
    def _():
        raises.wait()

    low = base_s[:, 3 * HALF :].astype(BF16)
    low_ref[...] = low
    raise_q, raise_v = raising_of(raise_s)
    query = (base_s[:, :HALF] + dot(low, raise_q)).astype(BF16).astype(F32).T
    key = base_s[:, HALF : 2 * HALF].astype(BF16).astype(F32).T
    value = (base_s[:, 2 * HALF : 3 * HALF] + dot(low, raise_v)).astype(BF16).astype(F32).T
    qkv_ref[:HALF, :] = query.astype(BF16)
    qkv_ref[HALF : 2 * HALF, :] = key.astype(BF16)
    qkv_ref[2 * HALF :, :] = value.astype(BF16)

    rows_j = lax.broadcasted_iota(jnp.int32, (PACKED, PACKED), 0)
    rows_i = lax.broadcasted_iota(jnp.int32, (PACKED, PACKED), 1)
    allowed = (tag_ref[0:1, :] == code_ref[...]) | (rows_j == rows_i)
    ones_rows = jnp.where(lax.broadcasted_iota(jnp.int32, (32, PACKED), 0) < 2, 1.0, 0.0)

    for h in range(FOCI):
        head = slice(h * HEAD, (h + 1) * HEAD)
        temper = soft_ref[core * FOCI + h] * (1.0 / HEAD)
        qn, _ = unit(query[head, :])
        kn, _ = unit(key[head, :])
        qs = pad_rows(qn * (temper * math.log2(math.e))).astype(BF16)
        v = jnp.concatenate([value[head, :], ones_rows], axis=0)
        scores = dot(pad_rows(kn).T.astype(BF16), qs)
        unnormed = jnp.exp2(jnp.where(allowed, scores, -1e30)).astype(BF16)
        weights_ref[h] = unnormed
        mixed = dot(v.astype(BF16), unnormed)
        inverse = 1.0 / mixed[HEAD : HEAD + 1, :]
        inverse_ref[h : h + 1, :] = inverse
        mixed_ref[head, :] = mixed[:HEAD, :] * inverse

    context_ref[...] = mixed_ref[...].T.astype(BF16).reshape(context_ref.shape)


def forward(core, soft, tags, codes, mine, other, whole):
    anywhere = pl.BlockSpec(memory_space=pl.ANY)
    grid = pltpu.PrefetchScalarGridSpec(
        num_scalar_prefetch=1,
        grid=(2,),
        in_specs=[
            pl.BlockSpec(memory_space=SMEM),
            pl.BlockSpec((None, 8, PACKED), lambda o, c: (o, 0, 0)),
            pl.BlockSpec((None, PACKED, 1), lambda o, c: (o, 0, 0)),
            anywhere,
            anywhere,
            anywhere,
        ],
        out_specs=[
            pl.BlockSpec((OWNERS, None, SLOTS * LEN, HALF), lambda o, c: (0, o, 0, 0)),
            pl.BlockSpec((None, FOCI, PACKED, PACKED), lambda o, c: (o, 0, 0, 0)),
            pl.BlockSpec((None, 3 * HALF, PACKED), lambda o, c: (o, 0, 0)),
            pl.BlockSpec((None, PACKED, 2 * RANK), lambda o, c: (o, 0, 0)),
            pl.BlockSpec((None, HALF, PACKED), lambda o, c: (o, 0, 0)),
            pl.BlockSpec((None, 8, PACKED), lambda o, c: (o, 0, 0)),
        ],
        scratch_shapes=[
            pltpu.VMEM((2, PACKED, WIDE), BF16),
            pltpu.VMEM((WIDE, QKVL), BF16),
            pltpu.VMEM((WIDE // 2, 2 * RANK), BF16),
            pltpu.VMEM((PACKED, QKVL), F32),
            pltpu.SemaphoreType.DMA((2,)),
            pltpu.SemaphoreType.DMA((QKVL // 256,)),
            pltpu.SemaphoreType.DMA,
        ],
    )
    return pl.pallas_call(
        forward_kernel,
        grid_spec=grid,
        out_shape=(
            jax.ShapeDtypeStruct((OWNERS, 2, SLOTS * LEN, HALF), BF16),
            jax.ShapeDtypeStruct((2, FOCI, PACKED, PACKED), BF16),
            jax.ShapeDtypeStruct((2, 3 * HALF, PACKED), BF16),
            jax.ShapeDtypeStruct((2, PACKED, 2 * RANK), BF16),
            jax.ShapeDtypeStruct((2, HALF, PACKED), F32),
            jax.ShapeDtypeStruct((2, 8, PACKED), F32),
        ),
        compiler_params=pltpu.CompilerParams(
            vmem_limit_bytes=48 << 20, dimension_semantics=("arbitrary",)
        ),
        cost_estimate=pl.CostEstimate(
            flops=6 << 30, bytes_accessed=16 << 20, transcendentals=2 * FOCI * PACKED * PACKED
        ),
        name="forward",
    )(core, soft, tags, codes, mine, other, whole)


def backward_kernel(
    core_ref,
    soft_ref,
    weights_ref,
    qkv_ref,
    low_ref,
    mixed_ref,
    inverse_ref,
    mine_ref,
    other_ref,
    masked_mine_ref,
    masked_other_ref,
    whole_ref,
    keep_ref,
    send_ref,
    up_ref,
    normed_s,
    masked_s,
    out_s,
    raise_s,
    cot_s,
    dquery_s,
    dvalue_s,
    down_s,
    up_s,
    row_sems,
    masked_sems,
    out_sem,
    raise_sem,
):
    owner = pl.program_id(0)
    core = core_ref[0]
    rows = owner_copies((mine_ref, other_ref), normed_s, row_sems)
    masks = owner_copies((masked_mine_ref, masked_other_ref), masked_s, masked_sems)
    half = pl.ds(pl.multiple_of(core * (WIDE // 2), WIDE // 2), WIDE // 2)
    outs = pltpu.make_async_copy(whole_ref.at[half, pl.ds(0, HIDDEN)], out_s, out_sem)
    raises = pltpu.make_async_copy(
        whole_ref.at[half, pl.ds(HIDDEN + QKVL, 2 * RANK)], raise_s, raise_sem
    )

    @pl.when(owner == 0)
    def _():
        outs.start()
        masks[0].start()
        rows[0].start()
        raises.start()
        masks[1].start()
        rows[1].start()
        down_s[...] = jnp.zeros_like(down_s)
        up_s[...] = jnp.zeros_like(up_s)
        outs.wait()
        masks[0].wait()

    @pl.when(owner == 1)
    def _():
        masks[1].wait()

    sides = []
    for side in range(2):
        columns = slice(side * WIDE // 2, (side + 1) * WIDE // 2)
        both = dot_nt(out_s[...], masked_s[owner, :, columns])
        both = both.reshape(SHARDS // 2, BLOCK, PACKED)
        sides.append(both[:, side * UPS : (side + 1) * UPS])
    cot_s[...] = (sides[0] + sides[1]).reshape(HALF, PACKED).astype(BF16).astype(F32)

    ones_rows = jnp.where(lax.broadcasted_iota(jnp.int32, (32, PACKED), 0) < 2, 1.0, 0.0)
    sub = lax.broadcasted_iota(jnp.int32, (32, PACKED), 0)

    for h in range(FOCI):
        head = slice(h * HEAD, (h + 1) * HEAD)
        temper = soft_ref[core * FOCI + h] * (1.0 / HEAD)
        qn, rq = unit(qkv_ref[head, :].astype(F32))
        kn, _ = unit(qkv_ref[HALF + h * HEAD : HALF + (h + 1) * HEAD, :].astype(F32))
        value = qkv_ref[2 * HALF + h * HEAD : 2 * HALF + (h + 1) * HEAD, :].astype(F32)
        v = jnp.concatenate([value, ones_rows], axis=0)
        unnormed = weights_ref[h]
        dc = (cot_s[head, :] * inverse_ref[h : h + 1, :]).astype(BF16)
        shift = jnp.sum(dc.astype(F32) * mixed_ref[head, :], axis=0, keepdims=True)
        shift_top = shift.astype(BF16).astype(F32)
        extra = jnp.where(sub == 0, -shift_top, jnp.where(sub == 1, shift_top - shift, 0.0))
        dc = jnp.concatenate([dc, extra.astype(BF16)], axis=0)
        inner = dot(v.T.astype(BF16), dc)
        dscores = (unnormed.astype(F32) * inner).astype(BF16)
        dqn = dot(pad_rows(kn).astype(BF16), dscores)[:HEAD, :] * temper
        dq = rq * (dqn - qn * (jnp.sum(qn * dqn, axis=0, keepdims=True) * (1.0 / HEAD)))
        dquery_s[head, :] = dq.astype(BF16)
        dv = dot_nt(unnormed, dc)
        dvalue_s[head, :] = dv.T[:HEAD, :].astype(BF16)

    @pl.when(owner == 0)
    def _():
        raises.wait()
        rows[0].wait()

    @pl.when(owner == 1)
    def _():
        rows[1].wait()

    low = low_ref[...]
    raise_q, raise_v = raising_of(raise_s)
    dquery = dquery_s[...]
    dvalue = dvalue_s[...]
    lane = lax.broadcasted_iota(jnp.int32, (HALF, 2 * RANK), 1)
    up_s[...] += jnp.where(lane < RANK, dot(dquery, low), dot(dvalue, low))
    inner_t = (dot(raise_q, dquery) + dot(raise_v, dvalue)).astype(BF16)
    down_s[...] += dot(inner_t, normed_s[owner])

    @pl.when(owner == 1)
    def _():
        down = down_s[...].T.reshape(SHARDS, BLOCK, 2 * RANK)
        first = down[:, :UPS].reshape(SHARDS * UPS, 2 * RANK)
        second = down[:, UPS:].reshape(SHARDS * UPS, 2 * RANK)
        keep_ref[...] = jnp.where(core == 0, first, second)
        send_ref[...] = jnp.where(core == 0, second, first).astype(BF16)
        up_ref[...] = up_s[...]


def backward(core, soft, saved, normed, masked, whole):
    anywhere = pl.BlockSpec(memory_space=pl.ANY)
    grid = pltpu.PrefetchScalarGridSpec(
        num_scalar_prefetch=1,
        grid=(2,),
        in_specs=[
            pl.BlockSpec(memory_space=SMEM),
            pl.BlockSpec((None, FOCI, PACKED, PACKED), lambda o, c: (o, 0, 0, 0)),
            pl.BlockSpec((None, 3 * HALF, PACKED), lambda o, c: (o, 0, 0)),
            pl.BlockSpec((None, PACKED, 2 * RANK), lambda o, c: (o, 0, 0)),
            pl.BlockSpec((None, HALF, PACKED), lambda o, c: (o, 0, 0)),
            pl.BlockSpec((None, 8, PACKED), lambda o, c: (o, 0, 0)),
        ]
        + [anywhere] * 5,
        out_specs=[
            pl.BlockSpec((SHARDS * UPS, 2 * RANK), lambda o, c: (0, 0)),
            pl.BlockSpec((SHARDS * UPS, 2 * RANK), lambda o, c: (0, 0)),
            pl.BlockSpec((HALF, 2 * RANK), lambda o, c: (0, 0)),
        ],
        scratch_shapes=[
            pltpu.VMEM((2, PACKED, WIDE), BF16),
            pltpu.VMEM((2, PACKED, WIDE), BF16),
            pltpu.VMEM((WIDE // 2, HIDDEN), BF16),
            pltpu.VMEM((WIDE // 2, 2 * RANK), BF16),
            pltpu.VMEM((HALF, PACKED), F32),
            pltpu.VMEM((HALF, PACKED), BF16),
            pltpu.VMEM((HALF, PACKED), BF16),
            pltpu.VMEM((2 * RANK, WIDE), F32),
            pltpu.VMEM((HALF, 2 * RANK), F32),
            pltpu.SemaphoreType.DMA((2,)),
            pltpu.SemaphoreType.DMA((2,)),
            pltpu.SemaphoreType.DMA,
            pltpu.SemaphoreType.DMA,
        ],
    )
    return pl.pallas_call(
        backward_kernel,
        grid_spec=grid,
        out_shape=(
            jax.ShapeDtypeStruct((SHARDS * UPS, 2 * RANK), F32),
            jax.ShapeDtypeStruct((SHARDS * UPS, 2 * RANK), BF16),
            jax.ShapeDtypeStruct((HALF, 2 * RANK), F32),
        ),
        compiler_params=pltpu.CompilerParams(
            vmem_limit_bytes=48 << 20, dimension_semantics=("arbitrary",)
        ),
        cost_estimate=pl.CostEstimate(flops=8 << 30, bytes_accessed=16 << 20, transcendentals=0),
        name="backward",
    )(core, soft, *saved, *normed, *masked, whole)


def combine_kernel(core_ref, keep_ref, come_ref, up_ref, parts_ref):
    down = keep_ref[...] + come_ref[...].astype(F32)
    up = up_ref[...]
    none = jnp.zeros_like(up)
    low_half = core_ref[0] == 0
    up = jnp.concatenate([jnp.where(low_half, up, none), jnp.where(low_half, none, up)], axis=0)
    shape = (SHARDS, UPS, 2 * RANK)
    parts = jnp.concatenate([down.reshape(shape), up.reshape(shape)], axis=1)
    parts_ref[...] = parts.reshape(parts_ref.shape).astype(BF16)


def combine(core, keep, come, up):
    return pl.pallas_call(
        combine_kernel,
        out_shape=jax.ShapeDtypeStruct((SHARDS * GRAD, 2 * RANK), BF16),
        in_specs=[pl.BlockSpec(memory_space=SMEM)] + [pl.BlockSpec(memory_space=VMEM)] * 3,
        out_specs=pl.BlockSpec(memory_space=VMEM),
        name="combine",
    )(core, keep, come, up)


def finish_kernel(owner_ref, live_ref, context_ref, x_ref, out_a_ref, out_b_ref, block_ref):
    place, step = spread(slot_places(owner_ref), (ROWS, 1), 0)
    target = place * LEN + step
    slots = lax.broadcasted_iota(jnp.int32, (ROWS, PACKED), 1)
    select = jnp.where(slots == target, 1.0, 0.0).astype(BF16)
    lives, _ = spread([live_ref[p] for p in range(PANELS)], (ROWS, 1), 0)
    halves = []
    for half in range(2):
        parts = []
        for o in range(OWNERS):
            source = o // 2 * 2 + half
            first = 0 if source == o else SLOTS * LEN
            parts.append(context_ref[source, first : first + SLOTS * LEN, :])
        halves.append(dot(select, jnp.concatenate(parts, axis=0)).astype(BF16))
    for side, ref in enumerate((out_a_ref, out_b_ref)):
        columns = slice(side * WIDE // 2, (side + 1) * WIDE // 2)
        attended = dot(halves[0], ref[:HALF, :]) + dot(halves[1], ref[HALF:, :])
        added = jnp.where(step < lives, attended, 0.0)
        block_ref[:, columns] = (x_ref[:, columns].astype(F32) + added).astype(BF16)


def finish(owners, lives, context, x, out_a, out_b):
    return pl.pallas_call(
        finish_kernel,
        out_shape=jax.ShapeDtypeStruct((ROWS, WIDE), BF16),
        in_specs=[pl.BlockSpec(memory_space=SMEM)] * 2 + [pl.BlockSpec(memory_space=VMEM)] * 4,
        out_specs=pl.BlockSpec(memory_space=VMEM),
        compiler_params=pltpu.CompilerParams(vmem_limit_bytes=40 << 20),
        cost_estimate=pl.CostEstimate(
            flops=2 * ROWS * 2 * HALF * (WIDE + PACKED), bytes_accessed=6 << 20, transcendentals=0
        ),
        name="finish",
    )(owners, lives, context, x, out_a, out_b)


def add_shards_kernel(part_ref, total_ref):
    total = part_ref[0].astype(F32)
    for t in range(1, SHARDS):
        total = total + part_ref[t].astype(F32)
    total = total.astype(BF16)
    for o in range(OWNERS):
        total_ref[o] = total


def add_shards(parts):
    return pl.pallas_call(
        add_shards_kernel,
        out_shape=jax.ShapeDtypeStruct((OWNERS, GRAD, 2 * RANK), BF16),
        in_specs=[pl.BlockSpec(memory_space=VMEM)],
        out_specs=pl.BlockSpec(memory_space=VMEM),
        name="add_shards",
    )(parts)


def add_owners_kernel(part_ref, down_ref, up_ref):
    downs = [jnp.zeros((UPS, 2 * RANK), F32)] * 2
    up = jnp.zeros((UPS, 2 * RANK), F32)
    for o in range(OWNERS):
        part = part_ref[o].astype(F32)
        downs[o % 2] = downs[o % 2] + part[:UPS, :]
        up = up + part[UPS:, :]
    down = jnp.concatenate(downs, axis=0)
    for n in range(2):
        down_ref[n] = down[:, n * RANK : (n + 1) * RANK]
        up_ref[n] = up[:, n * RANK : (n + 1) * RANK]


def add_owners(parts):
    return pl.pallas_call(
        add_owners_kernel,
        out_shape=(
            jax.ShapeDtypeStruct((2, BLOCK, RANK), F32),
            jax.ShapeDtypeStruct((2, UPS, RANK), F32),
        ),
        in_specs=[pl.BlockSpec(memory_space=VMEM)],
        out_specs=(pl.BlockSpec(memory_space=VMEM),) * 2,
        name="add_owners",
    )(parts)


def exchange(data, axis):
    return lax.all_to_all(data, axis, split_axis=0, concat_axis=0, tiled=True)


def swap_cores(data):
    pairs = [(s, s ^ 1) for s in range(OWNERS)]
    return lax.ppermute(data, "seq", pairs)


def packed_facts(owners, tags, lives):
    same = owners[:, None] == owners[None, :]
    order = jnp.arange(PANELS, dtype=jnp.int32)
    rank = jnp.sum((same & (order[:, None] > order[None, :])).astype(jnp.int32), axis=1)
    place = owners * SLOTS + rank
    hits = place[None, :] == jnp.arange(OWNERS * SLOTS, dtype=jnp.int32)[:, None]
    facts = [jnp.sum(jnp.where(hits, fact[None, :], 0), axis=1) for fact in (tags, lives)]
    sent = jnp.stack(facts, axis=-1).astype(BF16).reshape(OWNERS // 2, 2, SLOTS * 2)
    return jnp.stack([sent, sent[:, ::-1]], axis=2).reshape(OWNERS, 2, SLOTS, 2)


def row_facts(received):
    received = jnp.swapaxes(received.astype(F32), 0, 1).reshape(2, OWNERS * SLOTS, 1, 2)
    steps = jnp.arange(LEN, dtype=jnp.int32).astype(F32)[None, None, :]
    tag = jnp.broadcast_to(received[..., 0], (2, OWNERS * SLOTS, LEN))
    code = jnp.where(steps < received[..., 1], tag, -1.0)
    rows = jnp.broadcast_to(tag.reshape(2, 1, PACKED), (2, 8, PACKED))
    return rows, code.reshape(2, PACKED, 1)


def on_device(
    encoder_timesteps,
    tile_parent_sequence,
    tile_recording_label,
    tile_valid_timesteps,
    standardize_scaling,
    triple_projector,
    final_projector,
    lowered_maps,
    raising_maps,
    focus_softness,
    result_adjoint,
):
    core = lax.axis_index("seq") % 2
    starts = [n * 2 * HALF for n in range(3)]
    triple = [
        jnp.where(
            core == 0,
            triple_projector[:, first : first + HALF],
            triple_projector[:, first + HALF : first + 2 * HALF],
        )
        for first in starts
    ]
    lowered = jnp.concatenate([lowered_maps[0], lowered_maps[1]], axis=1)
    outward = jnp.concatenate([final_projector[:, : WIDE // 2], final_projector[:, WIDE // 2 :]], axis=0)
    raising = raising_maps.reshape(2 * RANK, UPS).T
    raising = jnp.concatenate([raising, jnp.zeros_like(raising)], axis=0)
    shard = jnp.concatenate([outward, *triple, lowered, raising], axis=1)
    whole = lax.all_gather(shard, "dp", axis=0, tiled=True)

    x = encoder_timesteps.reshape(ROWS, WIDE)
    facts = exchange(
        packed_facts(tile_parent_sequence, tile_recording_label, tile_valid_timesteps), "seq"
    )
    normed, masked = pack(
        tile_parent_sequence,
        tile_valid_timesteps,
        x,
        result_adjoint.reshape(ROWS, WIDE),
        standardize_scaling.reshape(1, WIDE),
    )
    normed, facts = lax.optimization_barrier((normed, facts))
    tag_rows, codes = row_facts(facts)
    normed = exchange(normed, "seq")
    normed, masked = lax.optimization_barrier((normed, masked))
    masked = exchange(masked, "seq")
    flat = (PACKED, WIDE)
    normed = (normed.reshape(flat), swap_cores(normed).reshape(flat))
    masked = (masked.reshape(flat), swap_cores(masked).reshape(flat))

    core = core.reshape(1)
    context, *saved = forward(core, focus_softness, tag_rows, codes, *normed, whole)
    whole, context = lax.optimization_barrier((whole, context))
    keep, send, up = backward(core, focus_softness, saved, normed, masked, whole)
    context = exchange(context.reshape(OWNERS, 2 * SLOTS * LEN, HALF), "seq")
    parts = combine(core, keep, swap_cores(send), up)
    outs = whole.reshape(SHARDS, BLOCK, -1)[:, :, :HIDDEN]
    out_a = outs[:, :UPS].reshape(HIDDEN, WIDE // 2)
    out_b = outs[:, UPS:].reshape(HIDDEN, WIDE // 2)
    parts, context = lax.optimization_barrier((parts, context))
    parts = exchange(parts.reshape(SHARDS, GRAD, 2 * RANK), "dp")
    block_out = finish(tile_parent_sequence, tile_valid_timesteps, context, x, out_a, out_b)
    shard_down, shard_up = add_owners(exchange(add_shards(parts), "seq"))
    return block_out.reshape(encoder_timesteps.shape), shard_down, jnp.swapaxes(shard_up, 1, 2)


def solution(mesh):
    in_specs = (
        P(("dp", "seq"), None, None),
        P(("dp", "seq")),
        P(("dp", "seq")),
        P(("dp", "seq")),
        P(),
        P("dp", None),
        P("dp", None),
        P(None, "dp", None),
        P(None, None, "dp"),
        P(),
        P(("dp", "seq"), None, None),
    )
    out_specs = (P(("dp", "seq"), None, None), P(None, "dp", None), P(None, None, "dp"))
    return jax.shard_map(
        on_device, mesh=mesh, in_specs=in_specs, out_specs=out_specs, check_vma=False
    )
```

```python
import math

import jax
import jax.numpy as jnp
from jax import lax
from jax.experimental import pallas as pl
from jax.experimental.pallas import tpu as pltpu
from jax.sharding import Mesh
from jax.sharding import PartitionSpec as P

EPS_NORM = 1e-05
EPS_HEAD = 1e-06
WIDE = 1536
PANELS = 16
LEN = 16
ROWS = PANELS * LEN
OWNERS = 16
SLOTS = 2
PACKED = OWNERS * SLOTS * LEN
HEAD = 96
FOCI = 4
HALF = FOCI * HEAD
RANK = 64
SHARDS = 32
BLOCK = WIDE // SHARDS
UPS = 2 * HALF // SHARDS
GRAD = 2 * UPS
HIDDEN = 2 * HALF
FACTS = 128
X_SIZE = 4
Y_SIZE = 8
X_TURNS = (0, -1, 1, 2)
Y_TURNS = (0, -1, 1, -2, 2, -3, 3)
QKVL = 3 * HALF + 2 * RANK
F32 = jnp.float32
BF16 = jnp.bfloat16
SMEM = pltpu.MemorySpace.SMEM
VMEM = pltpu.MemorySpace.VMEM


def dot(a, b):
    return lax.dot_general(a, b, (((1,), (0,)), ((), ())), preferred_element_type=F32)


def dot_nt(a, b):
    return lax.dot_general(a, b, (((1,), (1,)), ((), ())), preferred_element_type=F32)


def slot_places(owner_ref):
    owners = [owner_ref[p] for p in range(PANELS)]
    places = []
    for p in range(PANELS):
        rank = jnp.int32(0)
        for q in range(p):
            rank = rank + jnp.where(owners[q] == owners[p], 1, 0)
        places.append(owners[p] * SLOTS + rank)
    return places


def spread(scalars, shape, axis):
    index = lax.broadcasted_iota(jnp.int32, shape, axis)
    panel = index // LEN
    values = jnp.zeros(shape, jnp.int32)
    for p in range(PANELS):
        values = jnp.where(panel == p, scalars[p], values)
    return values, index % LEN


def pack_kernel(owner_ref, tag_ref, live_ref, x_ref, gain_ref, packed_ref):
    place, step = spread(slot_places(owner_ref), (1, ROWS), 1)
    target = place * LEN + step
    slots = lax.broadcasted_iota(jnp.int32, (PACKED, ROWS), 0)
    select = jnp.where(slots == target, 1.0, 0.0).astype(BF16)
    values = x_ref[...].astype(F32)
    centred = values - jnp.mean(values, axis=-1, keepdims=True)
    scaled = centred * lax.rsqrt(jnp.mean(centred * centred, axis=-1, keepdims=True) + EPS_NORM)
    normed = (scaled * gain_ref[...]).astype(BF16)
    packed_ref[:, :, :WIDE] = dot(select, normed).astype(BF16).reshape(OWNERS, SLOTS * LEN, WIDE)
    tags, step = spread([tag_ref[p] for p in range(PANELS)], (ROWS, FACTS), 0)
    lives, _ = spread([live_ref[p] for p in range(PANELS)], (ROWS, FACTS), 0)
    lane = lax.broadcasted_iota(jnp.int32, (ROWS, FACTS), 1)
    alive = jnp.where(step < lives, 1, 0)
    facts = jnp.where(lane == 0, tags, jnp.where(lane == 1, alive, 0)).astype(F32).astype(BF16)
    packed_ref[:, :, WIDE:] = dot(select, facts).astype(BF16).reshape(OWNERS, SLOTS * LEN, FACTS)


def pack(owners, tags, lives, x, gain):
    return pl.pallas_call(
        pack_kernel,
        out_shape=jax.ShapeDtypeStruct((OWNERS, SLOTS * LEN, WIDE + FACTS), BF16),
        in_specs=[pl.BlockSpec(memory_space=SMEM)] * 3 + [pl.BlockSpec(memory_space=VMEM)] * 2,
        out_specs=pl.BlockSpec(memory_space=VMEM),
        compiler_params=pltpu.CompilerParams(vmem_limit_bytes=32 << 20),
        cost_estimate=pl.CostEstimate(
            flops=2 * PACKED * ROWS * WIDE, bytes_accessed=4 * PACKED * WIDE, transcendentals=0
        ),
        name="pack",
    )(owners, tags, lives, x, gain)


def cotangent_kernel(owner_ref, live_ref, adjoint_ref, out_a_ref, out_b_ref, packed_ref):
    place, step = spread(slot_places(owner_ref), (1, ROWS), 1)
    target = place * LEN + step
    slots = lax.broadcasted_iota(jnp.int32, (PACKED, ROWS), 0)
    select = jnp.where(slots == target, 1.0, 0.0).astype(BF16)
    lives, step = spread([live_ref[p] for p in range(PANELS)], (ROWS, 1), 0)
    masked = jnp.where(step < lives, adjoint_ref[...].astype(F32), 0.0).astype(BF16)
    cot = dot_nt(masked[:, : WIDE // 2], out_a_ref[...])
    cot = cot + dot_nt(masked[:, WIDE // 2 :], out_b_ref[...])
    cot = dot(select, cot.astype(BF16)).astype(BF16)
    span = SLOTS * LEN
    for o in range(OWNERS):
        columns = slice(o % 2 * HALF, (o % 2 + 1) * HALF)
        for place_in, owner in enumerate((o, o ^ 1)):
            packed_ref[o, place_in * span : (place_in + 1) * span, :] = cot[
                owner * span : (owner + 1) * span, columns
            ]


def cotangent(owners, lives, adjoint, out_a, out_b):
    return pl.pallas_call(
        cotangent_kernel,
        out_shape=jax.ShapeDtypeStruct((OWNERS, 2 * SLOTS * LEN, HALF), BF16),
        in_specs=[pl.BlockSpec(memory_space=SMEM)] * 2 + [pl.BlockSpec(memory_space=VMEM)] * 3,
        out_specs=pl.BlockSpec(memory_space=VMEM),
        compiler_params=pltpu.CompilerParams(vmem_limit_bytes=32 << 20),
        cost_estimate=pl.CostEstimate(
            flops=2 * ROWS * HIDDEN * (WIDE + PACKED), bytes_accessed=6 << 20, transcendentals=0
        ),
        name="cotangent",
    )(owners, lives, adjoint, out_a, out_b)


def pad_rows(values, rows=128):
    return jnp.concatenate([values, jnp.zeros((rows - values.shape[0], values.shape[1]), values.dtype)], axis=0)


def owner_copies(sources, landing, sems):
    return [pltpu.make_async_copy(source, landing.at[o], sems.at[o]) for o, source in enumerate(sources)]


def raising_of(raise_s):
    tall = raise_s[...].astype(F32).reshape(SHARDS // 2, BLOCK, 2 * RANK)[:, :UPS]
    raising = tall.reshape(HALF, 2 * RANK).T
    row = lax.broadcasted_iota(jnp.int32, raising.shape, 0)
    raise_q = jnp.where(row < RANK, raising, 0.0).astype(BF16)
    raise_v = jnp.where(row < RANK, 0.0, raising).astype(BF16)
    return raise_q, raise_v


def unit(values):
    scale = lax.rsqrt(jnp.sum(values * values, axis=0, keepdims=True) * (1.0 / HEAD) + EPS_HEAD)
    return values * scale, scale


def forward_kernel(
    core_ref,
    soft_ref,
    mine_ref,
    other_ref,
    rest_ref,
    block_0_ref,
    block_1_ref,
    block_2_ref,
    block_3_ref,
    block_4_ref,
    block_5_ref,
    block_6_ref,
    far_a_ref,
    far_b_ref,
    context_ref,
    weights_ref,
    qkv_ref,
    low_ref,
    mixed_ref,
    inverse_ref,
    normed_s,
    weight_s,
    raise_s,
    base_s,
    row_sems,
    weight_sems,
    low_sem,
    raise_sem,
):
    owner = pl.program_id(0)
    core = core_ref[0]
    rows = owner_copies((mine_ref, other_ref), normed_s, row_sems)
    place_x, place_y = core_ref[1], core_ref[2]
    blocks = (block_0_ref, block_1_ref, block_2_ref, block_3_ref, block_4_ref, block_5_ref, block_6_ref)
    sources = [
        (blocks[j], i * BLOCK, dx, dy)
        for j, dy in enumerate(Y_TURNS)
        for i, dx in enumerate(X_TURNS)
    ]
    sources += [(far_a_ref, i * BLOCK, X_TURNS[i], Y_SIZE // 2) for i in range(2)]
    sources += [(far_b_ref, i * BLOCK, X_TURNS[2 + i], Y_SIZE // 2) for i in range(2)]
    pieces = []
    for n, (source, first, dx, dy) in enumerate(sources):
        shard = lax.rem(place_x + dx + X_SIZE, X_SIZE) * Y_SIZE + lax.rem(
            place_y + dy + Y_SIZE, Y_SIZE
        )
        target = pl.ds(pl.multiple_of(shard * BLOCK, BLOCK), BLOCK)
        pieces.append(
            pltpu.make_async_copy(
                source.at[pl.ds(first, BLOCK), :],
                weight_s.at[target, pl.ds(0, 3 * HALF)],
                weight_sems.at[n],
            )
        )
    lows = pltpu.make_async_copy(
        rest_ref.at[:, pl.ds(HIDDEN, 2 * RANK)], weight_s.at[:, pl.ds(3 * HALF, 2 * RANK)], low_sem
    )
    half = pl.ds(pl.multiple_of(core * (WIDE // 2), WIDE // 2), WIDE // 2)
    raises = pltpu.make_async_copy(
        rest_ref.at[half, pl.ds(HIDDEN + 2 * RANK, 2 * RANK)], raise_s, raise_sem
    )

    @pl.when(owner == 0)
    def _():
        rows[0].start()
        for piece in pieces:
            piece.start()
        lows.start()
        raises.start()
        rows[1].start()
        rows[0].wait()
        for piece in pieces:
            piece.wait()
        lows.wait()
        raises.wait()

    @pl.when(owner == 1)
    def _():
        rows[1].wait()

    for n in range(QKVL // 256):
        columns = slice(n * 256, (n + 1) * 256)
        base_s[:, columns] = dot(normed_s[owner, :, :WIDE], weight_s[:, columns])

    low = base_s[:, 3 * HALF :].astype(BF16)
    low_ref[...] = low
    raise_q, raise_v = raising_of(raise_s)
    query = (base_s[:, :HALF] + dot(low, raise_q)).astype(BF16).astype(F32).T
    key = base_s[:, HALF : 2 * HALF].astype(BF16).astype(F32).T
    value = (base_s[:, 2 * HALF : 3 * HALF] + dot(low, raise_v)).astype(BF16).astype(F32).T
    qkv_ref[:HALF, :] = query.astype(BF16)
    qkv_ref[HALF : 2 * HALF, :] = key.astype(BF16)
    qkv_ref[2 * HALF :, :] = value.astype(BF16)

    rows_j = lax.broadcasted_iota(jnp.int32, (PACKED, PACKED), 0)
    rows_i = lax.broadcasted_iota(jnp.int32, (PACKED, PACKED), 1)
    facts = normed_s[owner, :, WIDE:].astype(F32)
    codes = jnp.where(facts[:, 1:2] > 0.5, facts[:, 0:1], -1.0)
    allowed = (facts.T[0:1, :] == codes) | (rows_j == rows_i)
    ones_rows = jnp.where(lax.broadcasted_iota(jnp.int32, (32, PACKED), 0) < 2, 1.0, 0.0)

    for h in range(FOCI):
        head = slice(h * HEAD, (h + 1) * HEAD)
        temper = soft_ref[core * FOCI + h] * (1.0 / HEAD)
        qn, _ = unit(query[head, :])
        kn, _ = unit(key[head, :])
        qs = pad_rows(qn * (temper * math.log2(math.e))).astype(BF16)
        v = jnp.concatenate([value[head, :], ones_rows], axis=0)
        scores = dot(pad_rows(kn).T.astype(BF16), qs)
        unnormed = jnp.exp2(jnp.where(allowed, scores, -1e30)).astype(BF16)
        weights_ref[h] = unnormed
        mixed = dot(v.astype(BF16), unnormed)
        inverse = 1.0 / mixed[HEAD : HEAD + 1, :]
        inverse_ref[h : h + 1, :] = inverse
        mixed_ref[head, :] = mixed[:HEAD, :] * inverse

    context_ref[...] = mixed_ref[...].T.astype(BF16).reshape(context_ref.shape)


def forward(core, soft, mine, other, rest, pieces):
    anywhere = pl.BlockSpec(memory_space=pl.ANY)
    grid = pltpu.PrefetchScalarGridSpec(
        num_scalar_prefetch=1,
        grid=(2,),
        in_specs=[
            pl.BlockSpec(memory_space=SMEM),
        ]
        + [anywhere] * (3 + len(pieces)),
        out_specs=[
            pl.BlockSpec((OWNERS, None, SLOTS * LEN, HALF), lambda o, c: (0, o, 0, 0)),
            pl.BlockSpec((None, FOCI, PACKED, PACKED), lambda o, c: (o, 0, 0, 0)),
            pl.BlockSpec((None, 3 * HALF, PACKED), lambda o, c: (o, 0, 0)),
            pl.BlockSpec((None, PACKED, 2 * RANK), lambda o, c: (o, 0, 0)),
            pl.BlockSpec((None, HALF, PACKED), lambda o, c: (o, 0, 0)),
            pl.BlockSpec((None, 8, PACKED), lambda o, c: (o, 0, 0)),
        ],
        scratch_shapes=[
            pltpu.VMEM((2, PACKED, WIDE + FACTS), BF16),
            pltpu.VMEM((WIDE, QKVL), BF16),
            pltpu.VMEM((WIDE // 2, 2 * RANK), BF16),
            pltpu.VMEM((PACKED, QKVL), F32),
            pltpu.SemaphoreType.DMA((2,)),
            pltpu.SemaphoreType.DMA((SHARDS,)),
            pltpu.SemaphoreType.DMA,
            pltpu.SemaphoreType.DMA,
        ],
    )
    return pl.pallas_call(
        forward_kernel,
        grid_spec=grid,
        out_shape=(
            jax.ShapeDtypeStruct((OWNERS, 2, SLOTS * LEN, HALF), BF16),
            jax.ShapeDtypeStruct((2, FOCI, PACKED, PACKED), BF16),
            jax.ShapeDtypeStruct((2, 3 * HALF, PACKED), BF16),
            jax.ShapeDtypeStruct((2, PACKED, 2 * RANK), BF16),
            jax.ShapeDtypeStruct((2, HALF, PACKED), F32),
            jax.ShapeDtypeStruct((2, 8, PACKED), F32),
        ),
        compiler_params=pltpu.CompilerParams(
            vmem_limit_bytes=48 << 20, dimension_semantics=("arbitrary",)
        ),
        cost_estimate=pl.CostEstimate(
            flops=6 << 30, bytes_accessed=16 << 20, transcendentals=2 * FOCI * PACKED * PACKED
        ),
        name="forward",
    )(core, soft, mine, other, rest, *pieces)


def backward_kernel(
    core_ref,
    soft_ref,
    weights_ref,
    qkv_ref,
    low_ref,
    mixed_ref,
    inverse_ref,
    cot_ref,
    mine_ref,
    other_ref,
    rest_ref,
    keep_ref,
    send_ref,
    up_ref,
    normed_s,
    raise_s,
    dquery_s,
    dvalue_s,
    down_s,
    up_s,
    row_sems,
    raise_sem,
):
    owner = pl.program_id(0)
    core = core_ref[0]
    body = pl.ds(0, WIDE)
    rows = owner_copies((mine_ref.at[:, body], other_ref.at[:, body]), normed_s, row_sems)
    half = pl.ds(pl.multiple_of(core * (WIDE // 2), WIDE // 2), WIDE // 2)
    raises = pltpu.make_async_copy(
        rest_ref.at[half, pl.ds(HIDDEN + 2 * RANK, 2 * RANK)], raise_s, raise_sem
    )

    @pl.when(owner == 0)
    def _():
        rows[0].start()
        raises.start()
        rows[1].start()
        down_s[...] = jnp.zeros_like(down_s)
        up_s[...] = jnp.zeros_like(up_s)

    cot = cot_ref[...].reshape(PACKED, HALF).astype(F32).T
    ones_rows = jnp.where(lax.broadcasted_iota(jnp.int32, (32, PACKED), 0) < 2, 1.0, 0.0)
    sub = lax.broadcasted_iota(jnp.int32, (32, PACKED), 0)

    for h in range(FOCI):
        head = slice(h * HEAD, (h + 1) * HEAD)
        temper = soft_ref[core * FOCI + h] * (1.0 / HEAD)
        qn, rq = unit(qkv_ref[head, :].astype(F32))
        kn, _ = unit(qkv_ref[HALF + h * HEAD : HALF + (h + 1) * HEAD, :].astype(F32))
        value = qkv_ref[2 * HALF + h * HEAD : 2 * HALF + (h + 1) * HEAD, :].astype(F32)
        v = jnp.concatenate([value, ones_rows], axis=0)
        unnormed = weights_ref[h]
        dc = (cot[head, :] * inverse_ref[h : h + 1, :]).astype(BF16)
        shift = jnp.sum(dc.astype(F32) * mixed_ref[head, :], axis=0, keepdims=True)
        shift_top = shift.astype(BF16).astype(F32)
        extra = jnp.where(sub == 0, -shift_top, jnp.where(sub == 1, shift_top - shift, 0.0))
        dc = jnp.concatenate([dc, extra.astype(BF16)], axis=0)
        inner = dot(v.T.astype(BF16), dc)
        dscores = (unnormed.astype(F32) * inner).astype(BF16)
        dqn = dot(pad_rows(kn).astype(BF16), dscores)[:HEAD, :] * temper
        dq = rq * (dqn - qn * (jnp.sum(qn * dqn, axis=0, keepdims=True) * (1.0 / HEAD)))
        dquery_s[head, :] = dq.astype(BF16)
        dv = dot_nt(unnormed, dc)
        dvalue_s[head, :] = dv.T[:HEAD, :].astype(BF16)

    @pl.when(owner == 0)
    def _():
        raises.wait()
        rows[0].wait()

    @pl.when(owner == 1)
    def _():
        rows[1].wait()

    low = low_ref[...]
    raise_q, raise_v = raising_of(raise_s)
    dquery = dquery_s[...]
    dvalue = dvalue_s[...]
    lane = lax.broadcasted_iota(jnp.int32, (HALF, 2 * RANK), 1)
    up_s[...] += jnp.where(lane < RANK, dot(dquery, low), dot(dvalue, low))
    inner_t = (dot(raise_q, dquery) + dot(raise_v, dvalue)).astype(BF16)
    down_s[...] += dot(inner_t, normed_s[owner])

    @pl.when(owner == 1)
    def _():
        down = down_s[...].T.reshape(SHARDS, BLOCK, 2 * RANK)
        first = down[:, :UPS].reshape(SHARDS * UPS, 2 * RANK)
        second = down[:, UPS:].reshape(SHARDS * UPS, 2 * RANK)
        keep_ref[...] = jnp.where(core == 0, first, second)
        send_ref[...] = jnp.where(core == 0, second, first).astype(BF16)
        up_ref[...] = up_s[...]


def backward(core, soft, saved, cot, normed, rest):
    anywhere = pl.BlockSpec(memory_space=pl.ANY)
    grid = pltpu.PrefetchScalarGridSpec(
        num_scalar_prefetch=1,
        grid=(2,),
        in_specs=[
            pl.BlockSpec(memory_space=SMEM),
            pl.BlockSpec((None, FOCI, PACKED, PACKED), lambda o, c: (o, 0, 0, 0)),
            pl.BlockSpec((None, 3 * HALF, PACKED), lambda o, c: (o, 0, 0)),
            pl.BlockSpec((None, PACKED, 2 * RANK), lambda o, c: (o, 0, 0)),
            pl.BlockSpec((None, HALF, PACKED), lambda o, c: (o, 0, 0)),
            pl.BlockSpec((None, 8, PACKED), lambda o, c: (o, 0, 0)),
            pl.BlockSpec((OWNERS, SLOTS * LEN, HALF), lambda o, c: (0, o, 0)),
        ]
        + [anywhere] * 3,
        out_specs=[
            pl.BlockSpec((SHARDS * UPS, 2 * RANK), lambda o, c: (0, 0)),
            pl.BlockSpec((SHARDS * UPS, 2 * RANK), lambda o, c: (0, 0)),
            pl.BlockSpec((HALF, 2 * RANK), lambda o, c: (0, 0)),
        ],
        scratch_shapes=[
            pltpu.VMEM((2, PACKED, WIDE), BF16),
            pltpu.VMEM((WIDE // 2, 2 * RANK), BF16),
            pltpu.VMEM((HALF, PACKED), BF16),
            pltpu.VMEM((HALF, PACKED), BF16),
            pltpu.VMEM((2 * RANK, WIDE), F32),
            pltpu.VMEM((HALF, 2 * RANK), F32),
            pltpu.SemaphoreType.DMA((2,)),
            pltpu.SemaphoreType.DMA,
        ],
    )
    return pl.pallas_call(
        backward_kernel,
        grid_spec=grid,
        out_shape=(
            jax.ShapeDtypeStruct((SHARDS * UPS, 2 * RANK), F32),
            jax.ShapeDtypeStruct((SHARDS * UPS, 2 * RANK), BF16),
            jax.ShapeDtypeStruct((HALF, 2 * RANK), F32),
        ),
        compiler_params=pltpu.CompilerParams(
            vmem_limit_bytes=48 << 20, dimension_semantics=("arbitrary",)
        ),
        cost_estimate=pl.CostEstimate(flops=8 << 30, bytes_accessed=16 << 20, transcendentals=0),
        name="backward",
    )(core, soft, *saved, cot, *normed, rest)


def combine_kernel(core_ref, keep_ref, come_ref, up_ref, parts_ref):
    down = keep_ref[...] + come_ref[...].astype(F32)
    up = up_ref[...]
    none = jnp.zeros_like(up)
    low_half = core_ref[0] == 0
    up = jnp.concatenate([jnp.where(low_half, up, none), jnp.where(low_half, none, up)], axis=0)
    shape = (SHARDS, UPS, 2 * RANK)
    parts = jnp.concatenate([down.reshape(shape), up.reshape(shape)], axis=1)
    parts_ref[...] = parts.reshape(parts_ref.shape).astype(BF16)


def combine(core, keep, come, up):
    return pl.pallas_call(
        combine_kernel,
        out_shape=jax.ShapeDtypeStruct((SHARDS * GRAD, 2 * RANK), BF16),
        in_specs=[pl.BlockSpec(memory_space=SMEM)] + [pl.BlockSpec(memory_space=VMEM)] * 3,
        out_specs=pl.BlockSpec(memory_space=VMEM),
        name="combine",
    )(core, keep, come, up)


def finish_kernel(owner_ref, live_ref, context_ref, x_ref, out_a_ref, out_b_ref, block_ref):
    place, step = spread(slot_places(owner_ref), (ROWS, 1), 0)
    target = place * LEN + step
    slots = lax.broadcasted_iota(jnp.int32, (ROWS, PACKED), 1)
    select = jnp.where(slots == target, 1.0, 0.0).astype(BF16)
    lives, _ = spread([live_ref[p] for p in range(PANELS)], (ROWS, 1), 0)
    halves = []
    for half in range(2):
        parts = []
        for o in range(OWNERS):
            source = o // 2 * 2 + half
            first = 0 if source == o else SLOTS * LEN
            parts.append(context_ref[source, first : first + SLOTS * LEN, :])
        halves.append(dot(select, jnp.concatenate(parts, axis=0)).astype(BF16))
    for side, ref in enumerate((out_a_ref, out_b_ref)):
        columns = slice(side * WIDE // 2, (side + 1) * WIDE // 2)
        attended = dot(halves[0], ref[:HALF, :]) + dot(halves[1], ref[HALF:, :])
        added = jnp.where(step < lives, attended, 0.0)
        block_ref[:, columns] = (x_ref[:, columns].astype(F32) + added).astype(BF16)


def finish(owners, lives, context, x, out_a, out_b):
    return pl.pallas_call(
        finish_kernel,
        out_shape=jax.ShapeDtypeStruct((ROWS, WIDE), BF16),
        in_specs=[pl.BlockSpec(memory_space=SMEM)] * 2 + [pl.BlockSpec(memory_space=VMEM)] * 4,
        out_specs=pl.BlockSpec(memory_space=VMEM),
        compiler_params=pltpu.CompilerParams(vmem_limit_bytes=40 << 20),
        cost_estimate=pl.CostEstimate(
            flops=2 * ROWS * 2 * HALF * (WIDE + PACKED), bytes_accessed=6 << 20, transcendentals=0
        ),
        name="finish",
    )(owners, lives, context, x, out_a, out_b)


def add_shards_kernel(part_ref, total_ref):
    total = part_ref[0].astype(F32)
    for t in range(1, SHARDS):
        total = total + part_ref[t].astype(F32)
    total = total.astype(BF16)
    for o in range(OWNERS):
        total_ref[o] = total


def add_shards(parts):
    return pl.pallas_call(
        add_shards_kernel,
        out_shape=jax.ShapeDtypeStruct((OWNERS, GRAD, 2 * RANK), BF16),
        in_specs=[pl.BlockSpec(memory_space=VMEM)],
        out_specs=pl.BlockSpec(memory_space=VMEM),
        name="add_shards",
    )(parts)


def add_owners_kernel(part_ref, down_ref, up_ref):
    downs = [jnp.zeros((UPS, 2 * RANK), F32)] * 2
    up = jnp.zeros((UPS, 2 * RANK), F32)
    for o in range(OWNERS):
        part = part_ref[o].astype(F32)
        downs[o % 2] = downs[o % 2] + part[:UPS, :]
        up = up + part[UPS:, :]
    down = jnp.concatenate(downs, axis=0)
    for n in range(2):
        down_ref[n] = down[:, n * RANK : (n + 1) * RANK]
        up_ref[n] = up[:, n * RANK : (n + 1) * RANK]


def add_owners(parts):
    return pl.pallas_call(
        add_owners_kernel,
        out_shape=(
            jax.ShapeDtypeStruct((2, BLOCK, RANK), F32),
            jax.ShapeDtypeStruct((2, UPS, RANK), F32),
        ),
        in_specs=[pl.BlockSpec(memory_space=VMEM)],
        out_specs=(pl.BlockSpec(memory_space=VMEM),) * 2,
        name="add_owners",
    )(parts)


def exchange(data, axis):
    return lax.all_to_all(data, axis, split_axis=0, concat_axis=0, tiled=True)


def swap_cores(data):
    pairs = [(s, s ^ 1) for s in range(OWNERS)]
    return lax.ppermute(data, "seq", pairs)


def shift(data, turn_x, turn_y):
    pairs = []
    for x in range(X_SIZE):
        for y in range(Y_SIZE):
            to_x, to_y = (x + turn_x) % X_SIZE, (y + turn_y) % Y_SIZE
            pairs.append((x * Y_SIZE + y, to_x * Y_SIZE + to_y))
    return lax.ppermute(data, ("x", "y"), pairs)


def gather_blocks(shard):
    block = [shard] + [shift(shard, -dx, 0) for dx in X_TURNS[1:]]
    block = jnp.concatenate(block, axis=0)
    ups, downs = [block], [block]
    for _ in range(3):
        ups.append(shift(ups[-1], 0, 1))
        downs.append(shift(downs[-1], 0, -1))
    far_a = shift(ups[-1][: 2 * BLOCK], 0, 1)
    far_b = shift(downs[-1][2 * BLOCK :], 0, -1)
    return block, ups[1], downs[1], ups[2], downs[2], ups[3], downs[3], far_a, far_b


def on_device(
    encoder_timesteps,
    tile_parent_sequence,
    tile_recording_label,
    tile_valid_timesteps,
    standardize_scaling,
    triple_projector,
    final_projector,
    lowered_maps,
    raising_maps,
    focus_softness,
    result_adjoint,
):
    core = lax.axis_index("seq") % 2
    starts = [n * 2 * HALF for n in range(3)]
    triple = [
        jnp.where(
            core == 0,
            triple_projector[:, first : first + HALF],
            triple_projector[:, first + HALF : first + 2 * HALF],
        )
        for first in starts
    ]
    pieces = gather_blocks(jnp.concatenate(triple, axis=1))
    outward = jnp.concatenate([final_projector[:, : WIDE // 2], final_projector[:, WIDE // 2 :]], axis=0)
    raising = raising_maps.reshape(2 * RANK, UPS).T
    raising = jnp.concatenate([raising, jnp.zeros_like(raising)], axis=0)
    rest = jnp.concatenate([outward, lowered_maps[0], lowered_maps[1], raising], axis=1)
    rest = lax.all_gather(rest, "y", axis=0, tiled=True)
    rest = lax.all_gather(rest, "x", axis=0, tiled=True)

    x = encoder_timesteps.reshape(ROWS, WIDE)
    packed = pack(
        tile_parent_sequence,
        tile_recording_label,
        tile_valid_timesteps,
        x,
        standardize_scaling.reshape(1, WIDE),
    )
    packed = exchange(packed, "seq")
    outs = rest.reshape(SHARDS, BLOCK, -1)[:, :, :HIDDEN]
    out_a = outs[:, :UPS].reshape(HIDDEN, WIDE // 2)
    out_b = outs[:, UPS:].reshape(HIDDEN, WIDE // 2)
    cot = cotangent(
        tile_parent_sequence,
        tile_valid_timesteps,
        result_adjoint.reshape(ROWS, WIDE),
        out_a,
        out_b,
    )
    cot = exchange(cot, "seq")
    flat = (PACKED, WIDE + FACTS)
    normed = (packed.reshape(flat), swap_cores(packed).reshape(flat))

    places = jnp.stack([core, lax.axis_index("x"), lax.axis_index("y")]).astype(jnp.int32)
    context, *saved = forward(places, focus_softness, *normed, rest, pieces)
    cot, context = lax.optimization_barrier((cot, context))
    keep, send, up = backward(places, focus_softness, saved, cot, normed, rest)
    context = exchange(context.reshape(OWNERS, 2 * SLOTS * LEN, HALF), "seq")
    parts = combine(places, keep, swap_cores(send), up)
    parts, context = lax.optimization_barrier((parts, context))
    parts = exchange(parts.reshape(SHARDS, GRAD, 2 * RANK), ("x", "y"))
    block_out = finish(tile_parent_sequence, tile_valid_timesteps, context, x, out_a, out_b)
    shard_down, shard_up = add_owners(exchange(add_shards(parts), "seq"))
    return block_out.reshape(encoder_timesteps.shape), shard_down, jnp.swapaxes(shard_up, 1, 2)


def solution(mesh):
    grid = Mesh(mesh.devices.reshape(X_SIZE, Y_SIZE, OWNERS), ("x", "y", "seq"))
    rows, shards = ("x", "y", "seq"), ("x", "y")
    in_specs = (
        P(rows, None, None),
        P(rows),
        P(rows),
        P(rows),
        P(),
        P(shards, None),
        P(shards, None),
        P(None, shards, None),
        P(None, None, shards),
        P(),
        P(rows, None, None),
    )
    out_specs = (P(rows, None, None), P(None, shards, None), P(None, None, shards))
    return jax.shard_map(
        on_device, mesh=grid, in_specs=in_specs, out_specs=out_specs, check_vma=False
    )
```

```python
import math

import jax
import jax.numpy as jnp
from jax import lax
from jax.experimental import pallas as pl
from jax.experimental.pallas import tpu as pltpu
from jax.sharding import PartitionSpec as P

EPS_NORM = 1e-05
EPS_HEAD = 1e-06
WIDE = 1536
PANELS = 16
LEN = 16
ROWS = PANELS * LEN
OWNERS = 16
SLOTS = 2
PACKED = OWNERS * SLOTS * LEN
HEAD = 96
FOCI = 4
HALF = FOCI * HEAD
RANK = 64
SHARDS = 32
BLOCK = WIDE // SHARDS
UPS = 2 * HALF // SHARDS
GRAD = 2 * UPS
HIDDEN = 2 * HALF
QUARTER = WIDE // 4
FACTS = 128
QKVL = 3 * HALF + 2 * RANK
F32 = jnp.float32
BF16 = jnp.bfloat16
SMEM = pltpu.MemorySpace.SMEM
VMEM = pltpu.MemorySpace.VMEM


def dot(a, b):
    return lax.dot_general(a, b, (((1,), (0,)), ((), ())), preferred_element_type=F32)


def dot_nt(a, b):
    return lax.dot_general(a, b, (((1,), (1,)), ((), ())), preferred_element_type=F32)


def slot_places(owner_ref):
    owners = [owner_ref[p] for p in range(PANELS)]
    places = []
    for p in range(PANELS):
        rank = jnp.int32(0)
        for q in range(p):
            rank = rank + jnp.where(owners[q] == owners[p], 1, 0)
        places.append(owners[p] * SLOTS + rank)
    return places


def spread(scalars, shape, axis):
    index = lax.broadcasted_iota(jnp.int32, shape, axis)
    panel = index // LEN
    values = jnp.zeros(shape, jnp.int32)
    for p in range(PANELS):
        values = jnp.where(panel == p, scalars[p], values)
    return values, index % LEN


def pack_kernel(owner_ref, tag_ref, live_ref, x_ref, gain_ref, packed_ref):
    place, step = spread(slot_places(owner_ref), (1, ROWS), 1)
    target = place * LEN + step
    slots = lax.broadcasted_iota(jnp.int32, (PACKED, ROWS), 0)
    select = jnp.where(slots == target, 1.0, 0.0).astype(BF16)
    values = x_ref[...].astype(F32)
    centred = values - jnp.mean(values, axis=-1, keepdims=True)
    scaled = centred * lax.rsqrt(jnp.mean(centred * centred, axis=-1, keepdims=True) + EPS_NORM)
    normed = (scaled * gain_ref[...]).astype(BF16)
    packed_ref[:, :, :WIDE] = dot(select, normed).astype(BF16).reshape(OWNERS, SLOTS * LEN, WIDE)
    tags, step = spread([tag_ref[p] for p in range(PANELS)], (ROWS, FACTS), 0)
    lives, _ = spread([live_ref[p] for p in range(PANELS)], (ROWS, FACTS), 0)
    lane = lax.broadcasted_iota(jnp.int32, (ROWS, FACTS), 1)
    alive = jnp.where(step < lives, 1, 0)
    facts = jnp.where(lane == 0, tags, jnp.where(lane == 1, alive, 0)).astype(F32).astype(BF16)
    packed_ref[:, :, WIDE:] = dot(select, facts).astype(BF16).reshape(OWNERS, SLOTS * LEN, FACTS)


def pack(owners, tags, lives, x, gain):
    return pl.pallas_call(
        pack_kernel,
        out_shape=jax.ShapeDtypeStruct((OWNERS, SLOTS * LEN, WIDE + FACTS), BF16),
        in_specs=[pl.BlockSpec(memory_space=SMEM)] * 3 + [pl.BlockSpec(memory_space=VMEM)] * 2,
        out_specs=pl.BlockSpec(memory_space=VMEM),
        compiler_params=pltpu.CompilerParams(vmem_limit_bytes=32 << 20),
        cost_estimate=pl.CostEstimate(
            flops=2 * PACKED * ROWS * WIDE, bytes_accessed=4 * PACKED * WIDE, transcendentals=0
        ),
        name="pack",
    )(owners, tags, lives, x, gain)


def pack_masked_kernel(owner_ref, live_ref, adjoint_ref, packed_ref):
    place, step = spread(slot_places(owner_ref), (1, ROWS), 1)
    target = place * LEN + step
    slots = lax.broadcasted_iota(jnp.int32, (PACKED, ROWS), 0)
    select = jnp.where(slots == target, 1.0, 0.0).astype(BF16)
    lives, step = spread([live_ref[p] for p in range(PANELS)], (ROWS, 1), 0)
    masked = jnp.where(step < lives, adjoint_ref[...].astype(F32), 0.0).astype(BF16)
    packed_ref[...] = dot(select, masked).astype(BF16).reshape(packed_ref.shape)


def pack_masked(owners, lives, adjoint):
    return pl.pallas_call(
        pack_masked_kernel,
        out_shape=jax.ShapeDtypeStruct((OWNERS, SLOTS * LEN, WIDE), BF16),
        in_specs=[pl.BlockSpec(memory_space=SMEM)] * 2 + [pl.BlockSpec(memory_space=VMEM)],
        out_specs=pl.BlockSpec(memory_space=VMEM),
        compiler_params=pltpu.CompilerParams(vmem_limit_bytes=32 << 20),
        cost_estimate=pl.CostEstimate(
            flops=2 * PACKED * ROWS * WIDE, bytes_accessed=4 * PACKED * WIDE, transcendentals=0
        ),
        name="pack_masked",
    )(owners, lives, adjoint)


def pad_rows(values, rows=128):
    return jnp.concatenate([values, jnp.zeros((rows - values.shape[0], values.shape[1]), values.dtype)], axis=0)


def owner_copies(sources, landing, sems):
    return [pltpu.make_async_copy(source, landing.at[o], sems.at[o]) for o, source in enumerate(sources)]


def raising_of(raise_s):
    tall = raise_s[...].astype(F32).reshape(SHARDS // 2, BLOCK, 2 * RANK)[:, :UPS]
    raising = tall.reshape(HALF, 2 * RANK).T
    row = lax.broadcasted_iota(jnp.int32, raising.shape, 0)
    raise_q = jnp.where(row < RANK, raising, 0.0).astype(BF16)
    raise_v = jnp.where(row < RANK, 0.0, raising).astype(BF16)
    return raise_q, raise_v


def unit(values):
    scale = lax.rsqrt(jnp.sum(values * values, axis=0, keepdims=True) * (1.0 / HEAD) + EPS_HEAD)
    return values * scale, scale


def forward_kernel(
    core_ref,
    soft_ref,
    mine_ref,
    other_ref,
    whole_ref,
    context_ref,
    weights_ref,
    qkv_ref,
    low_ref,
    mixed_ref,
    inverse_ref,
    normed_s,
    weight_s,
    raise_s,
    base_s,
    row_sems,
    weight_sems,
    raise_sem,
):
    owner = pl.program_id(0)
    core = core_ref[0]
    rows = owner_copies((mine_ref, other_ref), normed_s, row_sems)
    tiles = [
        pltpu.make_async_copy(
            whole_ref.at[:, pl.ds(n * 256, 256)],
            weight_s.at[:, pl.ds(n * 256, 256)],
            weight_sems.at[n],
        )
        for n in range(QKVL // 256)
    ]
    half = pl.ds(pl.multiple_of(core * (WIDE // 2), WIDE // 2), WIDE // 2)
    raises = pltpu.make_async_copy(
        whole_ref.at[half, pl.ds(QKVL, 2 * RANK)], raise_s, raise_sem
    )

    @pl.when(owner == 0)
    def _():
        rows[0].start()
        for tile in tiles:
            tile.start()
        raises.start()
        rows[1].start()
        rows[0].wait()

    @pl.when(owner == 1)
    def _():
        rows[1].wait()

    for n, tile in enumerate(tiles):

        @pl.when(owner == 0)
        def _():
            tile.wait()

        columns = slice(n * 256, (n + 1) * 256)
        base_s[:, columns] = dot(normed_s[owner, :, :WIDE], weight_s[:, columns])

    @pl.when(owner == 0)
    def _():
        raises.wait()

    low = base_s[:, 3 * HALF :].astype(BF16)
    low_ref[...] = low
    raise_q, raise_v = raising_of(raise_s)
    query = (base_s[:, :HALF] + dot(low, raise_q)).astype(BF16).astype(F32).T
    key = base_s[:, HALF : 2 * HALF].astype(BF16).astype(F32).T
    value = (base_s[:, 2 * HALF : 3 * HALF] + dot(low, raise_v)).astype(BF16).astype(F32).T
    qkv_ref[:HALF, :] = query.astype(BF16)
    qkv_ref[HALF : 2 * HALF, :] = key.astype(BF16)
    qkv_ref[2 * HALF :, :] = value.astype(BF16)

    rows_j = lax.broadcasted_iota(jnp.int32, (PACKED, PACKED), 0)
    rows_i = lax.broadcasted_iota(jnp.int32, (PACKED, PACKED), 1)
    facts = normed_s[owner, :, WIDE:].astype(F32)
    codes = jnp.where(facts[:, 1:2] > 0.5, facts[:, 0:1], -1.0)
    allowed = (facts.T[0:1, :] == codes) | (rows_j == rows_i)
    ones_rows = jnp.where(lax.broadcasted_iota(jnp.int32, (32, PACKED), 0) < 2, 1.0, 0.0)

    for h in range(FOCI):
        head = slice(h * HEAD, (h + 1) * HEAD)
        temper = soft_ref[core * FOCI + h] * (1.0 / HEAD)
        qn, _ = unit(query[head, :])
        kn, _ = unit(key[head, :])
        qs = pad_rows(qn * (temper * math.log2(math.e))).astype(BF16)
        v = jnp.concatenate([value[head, :], ones_rows], axis=0)
        scores = dot(pad_rows(kn).T.astype(BF16), qs)
        unnormed = jnp.exp2(jnp.where(allowed, scores, -1e30)).astype(BF16)
        weights_ref[h] = unnormed
        mixed = dot(v.astype(BF16), unnormed)
        inverse = 1.0 / mixed[HEAD : HEAD + 1, :]
        inverse_ref[h : h + 1, :] = inverse
        mixed_ref[head, :] = mixed[:HEAD, :] * inverse

    context_ref[...] = mixed_ref[...].T.astype(BF16).reshape(context_ref.shape)


def forward(core, soft, mine, other, whole):
    anywhere = pl.BlockSpec(memory_space=pl.ANY)
    grid = pltpu.PrefetchScalarGridSpec(
        num_scalar_prefetch=1,
        grid=(2,),
        in_specs=[
            pl.BlockSpec(memory_space=SMEM),
        ]
        + [anywhere] * 3,
        out_specs=[
            pl.BlockSpec((OWNERS, None, SLOTS * LEN, HALF), lambda o, c: (0, o, 0, 0)),
            pl.BlockSpec((None, FOCI, PACKED, PACKED), lambda o, c: (o, 0, 0, 0)),
            pl.BlockSpec((None, 3 * HALF, PACKED), lambda o, c: (o, 0, 0)),
            pl.BlockSpec((None, PACKED, 2 * RANK), lambda o, c: (o, 0, 0)),
            pl.BlockSpec((None, HALF, PACKED), lambda o, c: (o, 0, 0)),
            pl.BlockSpec((None, 8, PACKED), lambda o, c: (o, 0, 0)),
        ],
        scratch_shapes=[
            pltpu.VMEM((2, PACKED, WIDE + FACTS), BF16),
            pltpu.VMEM((WIDE, QKVL), BF16),
            pltpu.VMEM((WIDE // 2, 2 * RANK), BF16),
            pltpu.VMEM((PACKED, QKVL), F32),
            pltpu.SemaphoreType.DMA((2,)),
            pltpu.SemaphoreType.DMA((QKVL // 256,)),
            pltpu.SemaphoreType.DMA,
        ],
    )
    return pl.pallas_call(
        forward_kernel,
        grid_spec=grid,
        out_shape=(
            jax.ShapeDtypeStruct((OWNERS, 2, SLOTS * LEN, HALF), BF16),
            jax.ShapeDtypeStruct((2, FOCI, PACKED, PACKED), BF16),
            jax.ShapeDtypeStruct((2, 3 * HALF, PACKED), BF16),
            jax.ShapeDtypeStruct((2, PACKED, 2 * RANK), BF16),
            jax.ShapeDtypeStruct((2, HALF, PACKED), F32),
            jax.ShapeDtypeStruct((2, 8, PACKED), F32),
        ),
        compiler_params=pltpu.CompilerParams(
            vmem_limit_bytes=48 << 20, dimension_semantics=("arbitrary",)
        ),
        cost_estimate=pl.CostEstimate(
            flops=6 << 30, bytes_accessed=16 << 20, transcendentals=2 * FOCI * PACKED * PACKED
        ),
        name="forward",
    )(core, soft, mine, other, whole)


def backward_kernel(
    core_ref,
    soft_ref,
    weights_ref,
    qkv_ref,
    low_ref,
    mixed_ref,
    inverse_ref,
    mine_ref,
    other_ref,
    masked_mine_ref,
    masked_other_ref,
    whole_ref,
    out_other_ref,
    keep_ref,
    send_ref,
    up_ref,
    normed_s,
    masked_s,
    out_s,
    raise_s,
    cot_s,
    dquery_s,
    dvalue_s,
    down_s,
    up_s,
    row_sems,
    masked_sems,
    out_sems,
    raise_sem,
):
    owner = pl.program_id(0)
    core = core_ref[0]
    body = pl.ds(0, WIDE)
    rows = owner_copies((mine_ref.at[:, body], other_ref.at[:, body]), normed_s, row_sems)
    masks = owner_copies((masked_mine_ref, masked_other_ref), masked_s, masked_sems)
    half = pl.ds(pl.multiple_of(core * (WIDE // 2), WIDE // 2), WIDE // 2)
    raises = pltpu.make_async_copy(
        whole_ref.at[half, pl.ds(QKVL, 2 * RANK)], raise_s, raise_sem
    )
    outs = owner_copies(
        (whole_ref.at[half, pl.ds(QKVL + 2 * RANK, QUARTER)], out_other_ref.at[half, :]),
        out_s,
        out_sems,
    )

    @pl.when(owner == 0)
    def _():
        masks[0].start()
        outs[0].start()
        outs[1].start()
        rows[0].start()
        raises.start()
        masks[1].start()
        rows[1].start()
        down_s[...] = jnp.zeros_like(down_s)
        up_s[...] = jnp.zeros_like(up_s)
        masks[0].wait()
        outs[0].wait()
        outs[1].wait()

    @pl.when(owner == 1)
    def _():
        masks[1].wait()

    total = jnp.zeros((SHARDS // 2, UPS, PACKED), F32)
    for n, side in enumerate((core, 1 - core)):
        for q in range(2):
            first = pl.multiple_of(side * (WIDE // 2) + q * QUARTER, QUARTER)
            both = dot_nt(out_s[n], masked_s[owner, :, pl.ds(first, QUARTER)])
            total = total + both.reshape(SHARDS // 2, BLOCK, PACKED)[:, q * UPS : (q + 1) * UPS]
    cot_s[...] = total.reshape(HALF, PACKED).astype(BF16).astype(F32)

    ones_rows = jnp.where(lax.broadcasted_iota(jnp.int32, (32, PACKED), 0) < 2, 1.0, 0.0)
    sub = lax.broadcasted_iota(jnp.int32, (32, PACKED), 0)

    for h in range(FOCI):
        head = slice(h * HEAD, (h + 1) * HEAD)
        temper = soft_ref[core * FOCI + h] * (1.0 / HEAD)
        qn, rq = unit(qkv_ref[head, :].astype(F32))
        kn, _ = unit(qkv_ref[HALF + h * HEAD : HALF + (h + 1) * HEAD, :].astype(F32))
        value = qkv_ref[2 * HALF + h * HEAD : 2 * HALF + (h + 1) * HEAD, :].astype(F32)
        v = jnp.concatenate([value, ones_rows], axis=0)
        unnormed = weights_ref[h]
        dc = (cot_s[head, :] * inverse_ref[h : h + 1, :]).astype(BF16)
        shift = jnp.sum(dc.astype(F32) * mixed_ref[head, :], axis=0, keepdims=True)
        shift_top = shift.astype(BF16).astype(F32)
        extra = jnp.where(sub == 0, -shift_top, jnp.where(sub == 1, shift_top - shift, 0.0))
        dc = jnp.concatenate([dc, extra.astype(BF16)], axis=0)
        inner = dot(v.T.astype(BF16), dc)
        dscores = (unnormed.astype(F32) * inner).astype(BF16)
        dqn = dot(pad_rows(kn).astype(BF16), dscores)[:HEAD, :] * temper
        dq = rq * (dqn - qn * (jnp.sum(qn * dqn, axis=0, keepdims=True) * (1.0 / HEAD)))
        dquery_s[head, :] = dq.astype(BF16)
        dv = dot_nt(unnormed, dc)
        dvalue_s[head, :] = dv.T[:HEAD, :].astype(BF16)

    @pl.when(owner == 0)
    def _():
        raises.wait()
        rows[0].wait()

    @pl.when(owner == 1)
    def _():
        rows[1].wait()

    low = low_ref[...]
    raise_q, raise_v = raising_of(raise_s)
    dquery = dquery_s[...]
    dvalue = dvalue_s[...]
    lane = lax.broadcasted_iota(jnp.int32, (HALF, 2 * RANK), 1)
    up_s[...] += jnp.where(lane < RANK, dot(dquery, low), dot(dvalue, low))
    inner_t = (dot(raise_q, dquery) + dot(raise_v, dvalue)).astype(BF16)
    down_s[...] += dot(inner_t, normed_s[owner])

    @pl.when(owner == 1)
    def _():
        down = down_s[...].T.reshape(SHARDS, BLOCK, 2 * RANK)
        first = down[:, :UPS].reshape(SHARDS * UPS, 2 * RANK)
        second = down[:, UPS:].reshape(SHARDS * UPS, 2 * RANK)
        keep_ref[...] = jnp.where(core == 0, first, second)
        send_ref[...] = jnp.where(core == 0, second, first).astype(BF16)
        up_ref[...] = up_s[...]


def backward(core, soft, saved, normed, masked, whole, out_other):
    anywhere = pl.BlockSpec(memory_space=pl.ANY)
    grid = pltpu.PrefetchScalarGridSpec(
        num_scalar_prefetch=1,
        grid=(2,),
        in_specs=[
            pl.BlockSpec(memory_space=SMEM),
            pl.BlockSpec((None, FOCI, PACKED, PACKED), lambda o, c: (o, 0, 0, 0)),
            pl.BlockSpec((None, 3 * HALF, PACKED), lambda o, c: (o, 0, 0)),
            pl.BlockSpec((None, PACKED, 2 * RANK), lambda o, c: (o, 0, 0)),
            pl.BlockSpec((None, HALF, PACKED), lambda o, c: (o, 0, 0)),
            pl.BlockSpec((None, 8, PACKED), lambda o, c: (o, 0, 0)),
        ]
        + [anywhere] * 6,
        out_specs=[
            pl.BlockSpec((SHARDS * UPS, 2 * RANK), lambda o, c: (0, 0)),
            pl.BlockSpec((SHARDS * UPS, 2 * RANK), lambda o, c: (0, 0)),
            pl.BlockSpec((HALF, 2 * RANK), lambda o, c: (0, 0)),
        ],
        scratch_shapes=[
            pltpu.VMEM((2, PACKED, WIDE), BF16),
            pltpu.VMEM((2, PACKED, WIDE), BF16),
            pltpu.VMEM((2, WIDE // 2, QUARTER), BF16),
            pltpu.VMEM((WIDE // 2, 2 * RANK), BF16),
            pltpu.VMEM((HALF, PACKED), F32),
            pltpu.VMEM((HALF, PACKED), BF16),
            pltpu.VMEM((HALF, PACKED), BF16),
            pltpu.VMEM((2 * RANK, WIDE), F32),
            pltpu.VMEM((HALF, 2 * RANK), F32),
            pltpu.SemaphoreType.DMA((2,)),
            pltpu.SemaphoreType.DMA((2,)),
            pltpu.SemaphoreType.DMA((2,)),
            pltpu.SemaphoreType.DMA,
        ],
    )
    return pl.pallas_call(
        backward_kernel,
        grid_spec=grid,
        out_shape=(
            jax.ShapeDtypeStruct((SHARDS * UPS, 2 * RANK), F32),
            jax.ShapeDtypeStruct((SHARDS * UPS, 2 * RANK), BF16),
            jax.ShapeDtypeStruct((HALF, 2 * RANK), F32),
        ),
        compiler_params=pltpu.CompilerParams(
            vmem_limit_bytes=48 << 20, dimension_semantics=("arbitrary",)
        ),
        cost_estimate=pl.CostEstimate(flops=8 << 30, bytes_accessed=16 << 20, transcendentals=0),
        name="backward",
    )(core, soft, *saved, *normed, *masked, whole, out_other)


def combine_kernel(core_ref, keep_ref, come_ref, up_ref, parts_ref):
    down = keep_ref[...] + come_ref[...].astype(F32)
    up = up_ref[...]
    none = jnp.zeros_like(up)
    low_half = core_ref[0] == 0
    up = jnp.concatenate([jnp.where(low_half, up, none), jnp.where(low_half, none, up)], axis=0)
    shape = (SHARDS, UPS, 2 * RANK)
    parts = jnp.concatenate([down.reshape(shape), up.reshape(shape)], axis=1)
    parts_ref[...] = parts.reshape(parts_ref.shape).astype(BF16)


def combine(core, keep, come, up):
    return pl.pallas_call(
        combine_kernel,
        out_shape=jax.ShapeDtypeStruct((SHARDS * GRAD, 2 * RANK), BF16),
        in_specs=[pl.BlockSpec(memory_space=SMEM)] + [pl.BlockSpec(memory_space=VMEM)] * 3,
        out_specs=pl.BlockSpec(memory_space=VMEM),
        compiler_params=pltpu.CompilerParams(vmem_limit_bytes=8 << 20),
        name="combine",
    )(core, keep, come, up)


def finish_kernel(core_ref, owner_ref, live_ref, context_ref, x_ref, *refs):
    *out_refs, block_ref = refs
    core = core_ref[0]
    place, step = spread(slot_places(owner_ref), (ROWS, 1), 0)
    target = place * LEN + step
    slots = lax.broadcasted_iota(jnp.int32, (ROWS, PACKED), 1)
    select = jnp.where(slots == target, 1.0, 0.0).astype(BF16)
    lives, _ = spread([live_ref[p] for p in range(PANELS)], (ROWS, 1), 0)
    halves = []
    for half in range(2):
        parts = []
        for o in range(OWNERS):
            source = o // 2 * 2 + half
            first = 0 if source == o else SLOTS * LEN
            parts.append(context_ref[source, first : first + SLOTS * LEN, :])
        halves.append(dot(select, jnp.concatenate(parts, axis=0)).astype(BF16))
    for n, ref in enumerate(out_refs):
        side = core if n < 2 else 1 - core
        first = pl.multiple_of(side * (WIDE // 2) + n % 2 * QUARTER, QUARTER)
        columns = pl.ds(first, QUARTER)
        attended = dot(halves[0], ref[:HALF, :]) + dot(halves[1], ref[HALF:, :])
        added = jnp.where(step < lives, attended, 0.0)
        block_ref[:, columns] = (x_ref[:, columns].astype(F32) + added).astype(BF16)


def finish(core, owners, lives, context, x, outs):
    return pl.pallas_call(
        finish_kernel,
        out_shape=jax.ShapeDtypeStruct((ROWS, WIDE), BF16),
        in_specs=[pl.BlockSpec(memory_space=SMEM)] * 3 + [pl.BlockSpec(memory_space=VMEM)] * 6,
        out_specs=pl.BlockSpec(memory_space=VMEM),
        compiler_params=pltpu.CompilerParams(vmem_limit_bytes=40 << 20),
        cost_estimate=pl.CostEstimate(
            flops=2 * ROWS * 2 * HALF * (WIDE + PACKED), bytes_accessed=6 << 20, transcendentals=0
        ),
        name="finish",
    )(core, owners, lives, context, x, *outs)


def add_shards_kernel(part_ref, total_ref):
    total = part_ref[0].astype(F32)
    for t in range(1, SHARDS):
        total = total + part_ref[t].astype(F32)
    total = total.astype(BF16)
    for o in range(OWNERS):
        total_ref[o] = total


def add_shards(parts):
    return pl.pallas_call(
        add_shards_kernel,
        out_shape=jax.ShapeDtypeStruct((OWNERS, GRAD, 2 * RANK), BF16),
        in_specs=[pl.BlockSpec(memory_space=VMEM)],
        out_specs=pl.BlockSpec(memory_space=VMEM),
        compiler_params=pltpu.CompilerParams(vmem_limit_bytes=8 << 20),
        name="add_shards",
    )(parts)


def add_owners_kernel(part_ref, down_ref, up_ref):
    downs = [jnp.zeros((UPS, 2 * RANK), F32)] * 2
    up = jnp.zeros((UPS, 2 * RANK), F32)
    for o in range(OWNERS):
        part = part_ref[o].astype(F32)
        downs[o % 2] = downs[o % 2] + part[:UPS, :]
        up = up + part[UPS:, :]
    down = jnp.concatenate(downs, axis=0)
    for n in range(2):
        down_ref[n] = down[:, n * RANK : (n + 1) * RANK]
        up_ref[n] = up[:, n * RANK : (n + 1) * RANK]


def add_owners(parts):
    return pl.pallas_call(
        add_owners_kernel,
        out_shape=(
            jax.ShapeDtypeStruct((2, BLOCK, RANK), F32),
            jax.ShapeDtypeStruct((2, UPS, RANK), F32),
        ),
        in_specs=[pl.BlockSpec(memory_space=VMEM)],
        out_specs=(pl.BlockSpec(memory_space=VMEM),) * 2,
        compiler_params=pltpu.CompilerParams(vmem_limit_bytes=8 << 20),
        name="add_owners",
    )(parts)


def exchange(data, axis):
    return lax.all_to_all(data, axis, split_axis=0, concat_axis=0, tiled=True)


def swap_cores(data):
    pairs = [(s, s ^ 1) for s in range(OWNERS)]
    return lax.ppermute(data, "seq", pairs)


def on_device(
    encoder_timesteps,
    tile_parent_sequence,
    tile_recording_label,
    tile_valid_timesteps,
    standardize_scaling,
    triple_projector,
    final_projector,
    lowered_maps,
    raising_maps,
    focus_softness,
    result_adjoint,
):
    core = lax.axis_index("seq") % 2
    def own(left, right):
        return jnp.where(core == 0, left, right)

    starts = [n * 2 * HALF for n in range(3)]
    triple = [
        own(
            triple_projector[:, first : first + HALF],
            triple_projector[:, first + HALF : first + 2 * HALF],
        )
        for first in starts
    ]
    raising = raising_maps.reshape(2 * RANK, UPS).T
    raising = jnp.concatenate([raising, jnp.zeros_like(raising)], axis=0)
    quarters = [final_projector[:, n * QUARTER : (n + 1) * QUARTER] for n in range(4)]
    outward = jnp.concatenate([own(quarters[0], quarters[2]), own(quarters[1], quarters[3])], axis=0)
    shard = jnp.concatenate([*triple, lowered_maps[0], lowered_maps[1], raising, outward], axis=1)
    whole = lax.all_gather(shard, "dp", axis=0, tiled=True)

    x = encoder_timesteps.reshape(ROWS, WIDE)
    packed = pack(
        tile_parent_sequence,
        tile_recording_label,
        tile_valid_timesteps,
        x,
        standardize_scaling.reshape(1, WIDE),
    )
    packed, adjoint = lax.optimization_barrier((packed, result_adjoint.reshape(ROWS, WIDE)))
    masked = pack_masked(tile_parent_sequence, tile_valid_timesteps, adjoint)
    packed = exchange(packed, "seq")
    packed, masked = lax.optimization_barrier((packed, masked))
    masked = exchange(masked, "seq")
    normed = [part.reshape(PACKED, WIDE + FACTS) for part in (packed, swap_cores(packed))]
    masked = [part.reshape(PACKED, WIDE) for part in (masked, swap_cores(masked))]

    core = core.reshape(1)
    out_own = whole[:, QKVL + 2 * RANK :]
    out_other = swap_cores(out_own)
    context, *saved = forward(core, focus_softness, *normed, whole)
    out_own, out_later, context = lax.optimization_barrier((out_own, out_other, context))
    keep, send, up = backward(core, focus_softness, saved, normed, masked, whole, out_other)
    context = exchange(context.reshape(OWNERS, 2 * SLOTS * LEN, HALF), "seq")
    parts = combine(core, keep, swap_cores(send), up)
    outs = []
    for part in (out_own, out_later):
        part = part.reshape(SHARDS, BLOCK, QUARTER)
        outs += [part[:, :UPS].reshape(HIDDEN, QUARTER), part[:, UPS:].reshape(HIDDEN, QUARTER)]
    parts, context = lax.optimization_barrier((parts, context))
    parts = exchange(parts.reshape(SHARDS, GRAD, 2 * RANK), "dp")
    block_out = finish(core, tile_parent_sequence, tile_valid_timesteps, context, x, outs)
    shard_down, shard_up = add_owners(exchange(add_shards(parts), "seq"))
    return block_out.reshape(encoder_timesteps.shape), shard_down, jnp.swapaxes(shard_up, 1, 2)


def solution(mesh):
    in_specs = (
        P(("dp", "seq"), None, None),
        P(("dp", "seq")),
        P(("dp", "seq")),
        P(("dp", "seq")),
        P(),
        P("dp", None),
        P("dp", None),
        P(None, "dp", None),
        P(None, None, "dp"),
        P(),
        P(("dp", "seq"), None, None),
    )
    out_specs = (P(("dp", "seq"), None, None), P(None, "dp", None), P(None, None, "dp"))
    return jax.shard_map(
        on_device, mesh=mesh, in_specs=in_specs, out_specs=out_specs, check_vma=False
    )
```

```python
import math

import jax
import jax.numpy as jnp
from jax import lax
from jax.experimental import pallas as pl
from jax.experimental.pallas import tpu as pltpu
from jax.sharding import PartitionSpec as P

EPS_NORM = 1e-05
EPS_HEAD = 1e-06
WIDE = 1536
PANELS = 16
LEN = 16
ROWS = PANELS * LEN
OWNERS = 16
SLOTS = 2
PACKED = OWNERS * SLOTS * LEN
HEAD = 96
FOCI = 4
HALF = FOCI * HEAD
RANK = 64
SHARDS = 32
BLOCK = WIDE // SHARDS
UPS = 2 * HALF // SHARDS
GRAD = 2 * UPS
HIDDEN = 2 * HALF
FACTS = 128
X_SIZE = 4
Y_SIZE = 8
X_TURNS = (0, -1, 1, 2)
Y_TURNS = (0, -1, 1, -2, 2, -3, 3)
QKVL = 3 * HALF + 2 * RANK
F32 = jnp.float32
BF16 = jnp.bfloat16
SMEM = pltpu.MemorySpace.SMEM
VMEM = pltpu.MemorySpace.VMEM


def dot(a, b):
    return lax.dot_general(a, b, (((1,), (0,)), ((), ())), preferred_element_type=F32)


def dot_nt(a, b):
    return lax.dot_general(a, b, (((1,), (1,)), ((), ())), preferred_element_type=F32)


def slot_places(owner_ref):
    owners = [owner_ref[p] for p in range(PANELS)]
    places = []
    for p in range(PANELS):
        rank = jnp.int32(0)
        for q in range(p):
            rank = rank + jnp.where(owners[q] == owners[p], 1, 0)
        places.append(owners[p] * SLOTS + rank)
    return places


def spread(scalars, shape, axis):
    index = lax.broadcasted_iota(jnp.int32, shape, axis)
    panel = index // LEN
    values = jnp.zeros(shape, jnp.int32)
    for p in range(PANELS):
        values = jnp.where(panel == p, scalars[p], values)
    return values, index % LEN


def pack_kernel(owner_ref, tag_ref, live_ref, x_ref, gain_ref, packed_ref):
    place, step = spread(slot_places(owner_ref), (1, ROWS), 1)
    target = place * LEN + step
    slots = lax.broadcasted_iota(jnp.int32, (PACKED, ROWS), 0)
    select = jnp.where(slots == target, 1.0, 0.0).astype(BF16)
    values = x_ref[...].astype(F32)
    centred = values - jnp.mean(values, axis=-1, keepdims=True)
    scaled = centred * lax.rsqrt(jnp.mean(centred * centred, axis=-1, keepdims=True) + EPS_NORM)
    normed = (scaled * gain_ref[...]).astype(BF16)
    packed_ref[:, :, :WIDE] = dot(select, normed).astype(BF16).reshape(OWNERS, SLOTS * LEN, WIDE)
    tags, step = spread([tag_ref[p] for p in range(PANELS)], (ROWS, FACTS), 0)
    lives, _ = spread([live_ref[p] for p in range(PANELS)], (ROWS, FACTS), 0)
    lane = lax.broadcasted_iota(jnp.int32, (ROWS, FACTS), 1)
    alive = jnp.where(step < lives, 1, 0)
    facts = jnp.where(lane == 0, tags, jnp.where(lane == 1, alive, 0)).astype(F32).astype(BF16)
    packed_ref[:, :, WIDE:] = dot(select, facts).astype(BF16).reshape(OWNERS, SLOTS * LEN, FACTS)


def pack(owners, tags, lives, x, gain):
    return pl.pallas_call(
        pack_kernel,
        out_shape=jax.ShapeDtypeStruct((OWNERS, SLOTS * LEN, WIDE + FACTS), BF16),
        in_specs=[pl.BlockSpec(memory_space=SMEM)] * 3 + [pl.BlockSpec(memory_space=VMEM)] * 2,
        out_specs=pl.BlockSpec(memory_space=VMEM),
        compiler_params=pltpu.CompilerParams(vmem_limit_bytes=32 << 20),
        cost_estimate=pl.CostEstimate(
            flops=2 * PACKED * ROWS * WIDE, bytes_accessed=4 * PACKED * WIDE, transcendentals=0
        ),
        name="pack",
    )(owners, tags, lives, x, gain)


def cotangent_kernel(
    core_ref,
    owner_ref,
    live_ref,
    adjoint_ref,
    block_0_ref,
    block_1_ref,
    block_2_ref,
    block_3_ref,
    block_4_ref,
    block_5_ref,
    block_6_ref,
    far_a_ref,
    far_b_ref,
    packed_ref,
    out_a_ref,
    out_b_ref,
    whole_s,
    piece_sems,
):
    place_x, place_y = core_ref[1], core_ref[2]
    blocks = (block_0_ref, block_1_ref, block_2_ref, block_3_ref, block_4_ref, block_5_ref, block_6_ref)
    sources = [
        (blocks[j], i * BLOCK, dx, dy)
        for j, dy in enumerate(Y_TURNS)
        for i, dx in enumerate(X_TURNS)
    ]
    sources += [(far_a_ref, i * BLOCK, X_TURNS[i], Y_SIZE // 2) for i in range(2)]
    sources += [(far_b_ref, i * BLOCK, X_TURNS[2 + i], Y_SIZE // 2) for i in range(2)]
    pieces = []
    for n, (source, first, dx, dy) in enumerate(sources):
        shard = lax.rem(place_x + dx + X_SIZE, X_SIZE) * Y_SIZE + lax.rem(
            place_y + dy + Y_SIZE, Y_SIZE
        )
        target = pl.ds(pl.multiple_of(shard * BLOCK, BLOCK), BLOCK)
        pieces.append(
            pltpu.make_async_copy(
                source.at[pl.ds(first, BLOCK), :],
                whole_s.at[target, :],
                piece_sems.at[n],
            )
        )
    for piece in pieces:
        piece.start()
    place, step = spread(slot_places(owner_ref), (1, ROWS), 1)
    target = place * LEN + step
    slots = lax.broadcasted_iota(jnp.int32, (PACKED, ROWS), 0)
    select = jnp.where(slots == target, 1.0, 0.0).astype(BF16)
    lives, step = spread([live_ref[p] for p in range(PANELS)], (ROWS, 1), 0)
    masked = jnp.where(step < lives, adjoint_ref[...].astype(F32), 0.0).astype(BF16)
    for piece in pieces:
        piece.wait()
    tall = whole_s[...].astype(F32).reshape(SHARDS, BLOCK, WIDE // 2)
    out_a = tall[:, :UPS].reshape(HIDDEN, WIDE // 2).astype(BF16)
    out_b = tall[:, UPS:].reshape(HIDDEN, WIDE // 2).astype(BF16)
    out_a_ref[...] = out_a
    out_b_ref[...] = out_b
    cot = dot_nt(masked[:, : WIDE // 2], out_a) + dot_nt(masked[:, WIDE // 2 :], out_b)
    cot = dot(select, cot.astype(BF16)).astype(BF16)
    span = SLOTS * LEN
    for o in range(OWNERS):
        columns = slice(o % 2 * HALF, (o % 2 + 1) * HALF)
        for place_in, owner in enumerate((o, o ^ 1)):
            packed_ref[o, place_in * span : (place_in + 1) * span, :] = cot[
                owner * span : (owner + 1) * span, columns
            ]


def cotangent(places, owners, lives, adjoint, pieces):
    half = jax.ShapeDtypeStruct((HIDDEN, WIDE // 2), BF16)
    return pl.pallas_call(
        cotangent_kernel,
        out_shape=(jax.ShapeDtypeStruct((OWNERS, 2 * SLOTS * LEN, HALF), BF16), half, half),
        in_specs=[pl.BlockSpec(memory_space=SMEM)] * 3
        + [pl.BlockSpec(memory_space=VMEM)]
        + [pl.BlockSpec(memory_space=pl.ANY)] * len(pieces),
        out_specs=(pl.BlockSpec(memory_space=VMEM),) * 3,
        scratch_shapes=[
            pltpu.VMEM((WIDE, WIDE // 2), BF16),
            pltpu.SemaphoreType.DMA((SHARDS,)),
        ],
        compiler_params=pltpu.CompilerParams(vmem_limit_bytes=32 << 20),
        cost_estimate=pl.CostEstimate(
            flops=2 * ROWS * HIDDEN * (WIDE + PACKED), bytes_accessed=8 << 20, transcendentals=0
        ),
        name="cotangent",
    )(places, owners, lives, adjoint, *pieces)


def pad_rows(values, rows=128):
    return jnp.concatenate([values, jnp.zeros((rows - values.shape[0], values.shape[1]), values.dtype)], axis=0)


def owner_copies(sources, landing, sems):
    return [pltpu.make_async_copy(source, landing.at[o], sems.at[o]) for o, source in enumerate(sources)]


def raising_of(raise_s):
    tall = raise_s[...].astype(F32).reshape(SHARDS // 2, BLOCK, 2 * RANK)[:, :UPS]
    raising = tall.reshape(HALF, 2 * RANK).T
    row = lax.broadcasted_iota(jnp.int32, raising.shape, 0)
    raise_q = jnp.where(row < RANK, raising, 0.0).astype(BF16)
    raise_v = jnp.where(row < RANK, 0.0, raising).astype(BF16)
    return raise_q, raise_v


def unit(values):
    scale = lax.rsqrt(jnp.sum(values * values, axis=0, keepdims=True) * (1.0 / HEAD) + EPS_HEAD)
    return values * scale, scale


def forward_kernel(
    core_ref,
    soft_ref,
    mine_ref,
    other_ref,
    whole_ref,
    context_ref,
    weights_ref,
    qkv_ref,
    low_ref,
    mixed_ref,
    inverse_ref,
    normed_s,
    weight_s,
    raise_s,
    base_s,
    row_sems,
    weight_sems,
    raise_sem,
):
    owner = pl.program_id(0)
    core = core_ref[0]
    rows = owner_copies((mine_ref, other_ref), normed_s, row_sems)
    tiles = [
        pltpu.make_async_copy(
            whole_ref.at[:, pl.ds(n * 256, 256)],
            weight_s.at[:, pl.ds(n * 256, 256)],
            weight_sems.at[n],
        )
        for n in range(QKVL // 256)
    ]
    half = pl.ds(pl.multiple_of(core * (WIDE // 2), WIDE // 2), WIDE // 2)
    raises = pltpu.make_async_copy(
        whole_ref.at[half, pl.ds(QKVL, 2 * RANK)], raise_s, raise_sem
    )

    @pl.when(owner == 0)
    def _():
        rows[0].start()
        for tile in tiles:
            tile.start()
        raises.start()
        rows[1].start()
        rows[0].wait()

    @pl.when(owner == 1)
    def _():
        rows[1].wait()

    for n, tile in enumerate(tiles):

        @pl.when(owner == 0)
        def _():
            tile.wait()

        columns = slice(n * 256, (n + 1) * 256)
        base_s[:, columns] = dot(normed_s[owner, :, :WIDE], weight_s[:, columns])

    @pl.when(owner == 0)
    def _():
        raises.wait()

    low = base_s[:, 3 * HALF :].astype(BF16)
    low_ref[...] = low
    raise_q, raise_v = raising_of(raise_s)
    query = (base_s[:, :HALF] + dot(low, raise_q)).astype(BF16).astype(F32).T
    key = base_s[:, HALF : 2 * HALF].astype(BF16).astype(F32).T
    value = (base_s[:, 2 * HALF : 3 * HALF] + dot(low, raise_v)).astype(BF16).astype(F32).T
    qkv_ref[:HALF, :] = query.astype(BF16)
    qkv_ref[HALF : 2 * HALF, :] = key.astype(BF16)
    qkv_ref[2 * HALF :, :] = value.astype(BF16)

    rows_j = lax.broadcasted_iota(jnp.int32, (PACKED, PACKED), 0)
    rows_i = lax.broadcasted_iota(jnp.int32, (PACKED, PACKED), 1)
    facts = normed_s[owner, :, WIDE:].astype(F32)
    codes = jnp.where(facts[:, 1:2] > 0.5, facts[:, 0:1], -1.0)
    allowed = (facts.T[0:1, :] == codes) | (rows_j == rows_i)
    ones_rows = jnp.where(lax.broadcasted_iota(jnp.int32, (32, PACKED), 0) < 2, 1.0, 0.0)

    for h in range(FOCI):
        head = slice(h * HEAD, (h + 1) * HEAD)
        temper = soft_ref[core * FOCI + h] * (1.0 / HEAD)
        qn, _ = unit(query[head, :])
        kn, _ = unit(key[head, :])
        qs = pad_rows(qn * (temper * math.log2(math.e))).astype(BF16)
        v = jnp.concatenate([value[head, :], ones_rows], axis=0)
        scores = dot(pad_rows(kn).T.astype(BF16), qs)
        unnormed = jnp.exp2(jnp.where(allowed, scores, -1e30)).astype(BF16)
        weights_ref[h] = unnormed
        mixed = dot(v.astype(BF16), unnormed)
        inverse = 1.0 / mixed[HEAD : HEAD + 1, :]
        inverse_ref[h : h + 1, :] = inverse
        mixed_ref[head, :] = mixed[:HEAD, :] * inverse

    context_ref[...] = mixed_ref[...].T.astype(BF16).reshape(context_ref.shape)


def forward(core, soft, mine, other, whole):
    anywhere = pl.BlockSpec(memory_space=pl.ANY)
    grid = pltpu.PrefetchScalarGridSpec(
        num_scalar_prefetch=1,
        grid=(2,),
        in_specs=[
            pl.BlockSpec(memory_space=SMEM),
        ]
        + [anywhere] * 3,
        out_specs=[
            pl.BlockSpec((OWNERS, None, SLOTS * LEN, HALF), lambda o, c: (0, o, 0, 0)),
            pl.BlockSpec((None, FOCI, PACKED, PACKED), lambda o, c: (o, 0, 0, 0)),
            pl.BlockSpec((None, 3 * HALF, PACKED), lambda o, c: (o, 0, 0)),
            pl.BlockSpec((None, PACKED, 2 * RANK), lambda o, c: (o, 0, 0)),
            pl.BlockSpec((None, HALF, PACKED), lambda o, c: (o, 0, 0)),
            pl.BlockSpec((None, 8, PACKED), lambda o, c: (o, 0, 0)),
        ],
        scratch_shapes=[
            pltpu.VMEM((2, PACKED, WIDE + FACTS), BF16),
            pltpu.VMEM((WIDE, QKVL), BF16),
            pltpu.VMEM((WIDE // 2, 2 * RANK), BF16),
            pltpu.VMEM((PACKED, QKVL), F32),
            pltpu.SemaphoreType.DMA((2,)),
            pltpu.SemaphoreType.DMA((QKVL // 256,)),
            pltpu.SemaphoreType.DMA,
        ],
    )
    return pl.pallas_call(
        forward_kernel,
        grid_spec=grid,
        out_shape=(
            jax.ShapeDtypeStruct((OWNERS, 2, SLOTS * LEN, HALF), BF16),
            jax.ShapeDtypeStruct((2, FOCI, PACKED, PACKED), BF16),
            jax.ShapeDtypeStruct((2, 3 * HALF, PACKED), BF16),
            jax.ShapeDtypeStruct((2, PACKED, 2 * RANK), BF16),
            jax.ShapeDtypeStruct((2, HALF, PACKED), F32),
            jax.ShapeDtypeStruct((2, 8, PACKED), F32),
        ),
        compiler_params=pltpu.CompilerParams(
            vmem_limit_bytes=48 << 20, dimension_semantics=("arbitrary",)
        ),
        cost_estimate=pl.CostEstimate(
            flops=6 << 30, bytes_accessed=16 << 20, transcendentals=2 * FOCI * PACKED * PACKED
        ),
        name="forward",
    )(core, soft, mine, other, whole)


def backward_kernel(
    core_ref,
    soft_ref,
    weights_ref,
    qkv_ref,
    low_ref,
    mixed_ref,
    inverse_ref,
    cot_ref,
    mine_ref,
    other_ref,
    whole_ref,
    keep_ref,
    send_ref,
    up_ref,
    normed_s,
    raise_s,
    dquery_s,
    dvalue_s,
    down_s,
    up_s,
    row_sems,
    raise_sem,
):
    owner = pl.program_id(0)
    core = core_ref[0]
    body = pl.ds(0, WIDE)
    rows = owner_copies((mine_ref.at[:, body], other_ref.at[:, body]), normed_s, row_sems)
    half = pl.ds(pl.multiple_of(core * (WIDE // 2), WIDE // 2), WIDE // 2)
    raises = pltpu.make_async_copy(
        whole_ref.at[half, pl.ds(QKVL, 2 * RANK)], raise_s, raise_sem
    )

    @pl.when(owner == 0)
    def _():
        rows[0].start()
        raises.start()
        rows[1].start()
        down_s[...] = jnp.zeros_like(down_s)
        up_s[...] = jnp.zeros_like(up_s)

    cot = cot_ref[...].reshape(PACKED, HALF).astype(F32).T
    ones_rows = jnp.where(lax.broadcasted_iota(jnp.int32, (32, PACKED), 0) < 2, 1.0, 0.0)
    sub = lax.broadcasted_iota(jnp.int32, (32, PACKED), 0)

    for h in range(FOCI):
        head = slice(h * HEAD, (h + 1) * HEAD)
        temper = soft_ref[core * FOCI + h] * (1.0 / HEAD)
        qn, rq = unit(qkv_ref[head, :].astype(F32))
        kn, _ = unit(qkv_ref[HALF + h * HEAD : HALF + (h + 1) * HEAD, :].astype(F32))
        value = qkv_ref[2 * HALF + h * HEAD : 2 * HALF + (h + 1) * HEAD, :].astype(F32)
        v = jnp.concatenate([value, ones_rows], axis=0)
        unnormed = weights_ref[h]
        dc = (cot[head, :] * inverse_ref[h : h + 1, :]).astype(BF16)
        shift = jnp.sum(dc.astype(F32) * mixed_ref[head, :], axis=0, keepdims=True)
        shift_top = shift.astype(BF16).astype(F32)
        extra = jnp.where(sub == 0, -shift_top, jnp.where(sub == 1, shift_top - shift, 0.0))
        dc = jnp.concatenate([dc, extra.astype(BF16)], axis=0)
        inner = dot(v.T.astype(BF16), dc)
        dscores = (unnormed.astype(F32) * inner).astype(BF16)
        dqn = dot(pad_rows(kn).astype(BF16), dscores)[:HEAD, :] * temper
        dq = rq * (dqn - qn * (jnp.sum(qn * dqn, axis=0, keepdims=True) * (1.0 / HEAD)))
        dquery_s[head, :] = dq.astype(BF16)
        dv = dot_nt(unnormed, dc)
        dvalue_s[head, :] = dv.T[:HEAD, :].astype(BF16)

    @pl.when(owner == 0)
    def _():
        raises.wait()
        rows[0].wait()

    @pl.when(owner == 1)
    def _():
        rows[1].wait()

    low = low_ref[...]
    raise_q, raise_v = raising_of(raise_s)
    dquery = dquery_s[...]
    dvalue = dvalue_s[...]
    lane = lax.broadcasted_iota(jnp.int32, (HALF, 2 * RANK), 1)
    up_s[...] += jnp.where(lane < RANK, dot(dquery, low), dot(dvalue, low))
    inner_t = (dot(raise_q, dquery) + dot(raise_v, dvalue)).astype(BF16)
    down_s[...] += dot(inner_t, normed_s[owner])

    @pl.when(owner == 1)
    def _():
        down = down_s[...].T.reshape(SHARDS, BLOCK, 2 * RANK)
        first = down[:, :UPS].reshape(SHARDS * UPS, 2 * RANK)
        second = down[:, UPS:].reshape(SHARDS * UPS, 2 * RANK)
        keep_ref[...] = jnp.where(core == 0, first, second)
        send_ref[...] = jnp.where(core == 0, second, first).astype(BF16)
        up_ref[...] = up_s[...]


def backward(core, soft, saved, cot, normed, whole):
    anywhere = pl.BlockSpec(memory_space=pl.ANY)
    grid = pltpu.PrefetchScalarGridSpec(
        num_scalar_prefetch=1,
        grid=(2,),
        in_specs=[
            pl.BlockSpec(memory_space=SMEM),
            pl.BlockSpec((None, FOCI, PACKED, PACKED), lambda o, c: (o, 0, 0, 0)),
            pl.BlockSpec((None, 3 * HALF, PACKED), lambda o, c: (o, 0, 0)),
            pl.BlockSpec((None, PACKED, 2 * RANK), lambda o, c: (o, 0, 0)),
            pl.BlockSpec((None, HALF, PACKED), lambda o, c: (o, 0, 0)),
            pl.BlockSpec((None, 8, PACKED), lambda o, c: (o, 0, 0)),
            pl.BlockSpec((OWNERS, SLOTS * LEN, HALF), lambda o, c: (0, o, 0)),
        ]
        + [anywhere] * 3,
        out_specs=[
            pl.BlockSpec((SHARDS * UPS, 2 * RANK), lambda o, c: (0, 0)),
            pl.BlockSpec((SHARDS * UPS, 2 * RANK), lambda o, c: (0, 0)),
            pl.BlockSpec((HALF, 2 * RANK), lambda o, c: (0, 0)),
        ],
        scratch_shapes=[
            pltpu.VMEM((2, PACKED, WIDE), BF16),
            pltpu.VMEM((WIDE // 2, 2 * RANK), BF16),
            pltpu.VMEM((HALF, PACKED), BF16),
            pltpu.VMEM((HALF, PACKED), BF16),
            pltpu.VMEM((2 * RANK, WIDE), F32),
            pltpu.VMEM((HALF, 2 * RANK), F32),
            pltpu.SemaphoreType.DMA((2,)),
            pltpu.SemaphoreType.DMA,
        ],
    )
    return pl.pallas_call(
        backward_kernel,
        grid_spec=grid,
        out_shape=(
            jax.ShapeDtypeStruct((SHARDS * UPS, 2 * RANK), F32),
            jax.ShapeDtypeStruct((SHARDS * UPS, 2 * RANK), BF16),
            jax.ShapeDtypeStruct((HALF, 2 * RANK), F32),
        ),
        compiler_params=pltpu.CompilerParams(
            vmem_limit_bytes=48 << 20, dimension_semantics=("arbitrary",)
        ),
        cost_estimate=pl.CostEstimate(flops=8 << 30, bytes_accessed=16 << 20, transcendentals=0),
        name="backward",
    )(core, soft, *saved, cot, *normed, whole)


def combine_kernel(core_ref, keep_ref, come_ref, up_ref, parts_ref):
    down = keep_ref[...] + come_ref[...].astype(F32)
    up = up_ref[...]
    none = jnp.zeros_like(up)
    low_half = core_ref[0] == 0
    up = jnp.concatenate([jnp.where(low_half, up, none), jnp.where(low_half, none, up)], axis=0)
    shape = (SHARDS, UPS, 2 * RANK)
    parts = jnp.concatenate([down.reshape(shape), up.reshape(shape)], axis=1)
    parts_ref[...] = parts.reshape(parts_ref.shape).astype(BF16)


def combine(core, keep, come, up):
    return pl.pallas_call(
        combine_kernel,
        out_shape=jax.ShapeDtypeStruct((SHARDS * GRAD, 2 * RANK), BF16),
        in_specs=[pl.BlockSpec(memory_space=SMEM)] + [pl.BlockSpec(memory_space=VMEM)] * 3,
        out_specs=pl.BlockSpec(memory_space=VMEM),
        compiler_params=pltpu.CompilerParams(vmem_limit_bytes=8 << 20),
        name="combine",
    )(core, keep, come, up)


def finish_kernel(owner_ref, live_ref, context_ref, x_ref, out_a_ref, out_b_ref, block_ref):
    place, step = spread(slot_places(owner_ref), (ROWS, 1), 0)
    target = place * LEN + step
    slots = lax.broadcasted_iota(jnp.int32, (ROWS, PACKED), 1)
    select = jnp.where(slots == target, 1.0, 0.0).astype(BF16)
    lives, _ = spread([live_ref[p] for p in range(PANELS)], (ROWS, 1), 0)
    halves = []
    for half in range(2):
        parts = []
        for o in range(OWNERS):
            source = o // 2 * 2 + half
            first = 0 if source == o else SLOTS * LEN
            parts.append(context_ref[source, first : first + SLOTS * LEN, :])
        halves.append(dot(select, jnp.concatenate(parts, axis=0)).astype(BF16))
    for side, ref in enumerate((out_a_ref, out_b_ref)):
        columns = slice(side * WIDE // 2, (side + 1) * WIDE // 2)
        attended = dot(halves[0], ref[:HALF, :]) + dot(halves[1], ref[HALF:, :])
        added = jnp.where(step < lives, attended, 0.0)
        block_ref[:, columns] = (x_ref[:, columns].astype(F32) + added).astype(BF16)


def finish(owners, lives, context, x, out_a, out_b):
    return pl.pallas_call(
        finish_kernel,
        out_shape=jax.ShapeDtypeStruct((ROWS, WIDE), BF16),
        in_specs=[pl.BlockSpec(memory_space=SMEM)] * 2 + [pl.BlockSpec(memory_space=VMEM)] * 4,
        out_specs=pl.BlockSpec(memory_space=VMEM),
        compiler_params=pltpu.CompilerParams(vmem_limit_bytes=40 << 20),
        cost_estimate=pl.CostEstimate(
            flops=2 * ROWS * 2 * HALF * (WIDE + PACKED), bytes_accessed=6 << 20, transcendentals=0
        ),
        name="finish",
    )(owners, lives, context, x, out_a, out_b)


def add_shards_kernel(part_ref, total_ref):
    total = part_ref[0].astype(F32)
    for t in range(1, SHARDS):
        total = total + part_ref[t].astype(F32)
    total = total.astype(BF16)
    for o in range(OWNERS):
        total_ref[o] = total


def add_shards(parts):
    return pl.pallas_call(
        add_shards_kernel,
        out_shape=jax.ShapeDtypeStruct((OWNERS, GRAD, 2 * RANK), BF16),
        in_specs=[pl.BlockSpec(memory_space=VMEM)],
        out_specs=pl.BlockSpec(memory_space=VMEM),
        compiler_params=pltpu.CompilerParams(vmem_limit_bytes=8 << 20),
        name="add_shards",
    )(parts)


def add_owners_kernel(part_ref, down_ref, up_ref):
    downs = [jnp.zeros((UPS, 2 * RANK), F32)] * 2
    up = jnp.zeros((UPS, 2 * RANK), F32)
    for o in range(OWNERS):
        part = part_ref[o].astype(F32)
        downs[o % 2] = downs[o % 2] + part[:UPS, :]
        up = up + part[UPS:, :]
    down = jnp.concatenate(downs, axis=0)
    for n in range(2):
        down_ref[n] = down[:, n * RANK : (n + 1) * RANK]
        up_ref[n] = up[:, n * RANK : (n + 1) * RANK]


def add_owners(parts):
    return pl.pallas_call(
        add_owners_kernel,
        out_shape=(
            jax.ShapeDtypeStruct((2, BLOCK, RANK), F32),
            jax.ShapeDtypeStruct((2, UPS, RANK), F32),
        ),
        in_specs=[pl.BlockSpec(memory_space=VMEM)],
        out_specs=(pl.BlockSpec(memory_space=VMEM),) * 2,
        compiler_params=pltpu.CompilerParams(vmem_limit_bytes=8 << 20),
        name="add_owners",
    )(parts)


def exchange(data, axis):
    return lax.all_to_all(data, axis, split_axis=0, concat_axis=0, tiled=True)


def swap_cores(data):
    pairs = [(s, s ^ 1) for s in range(OWNERS)]
    return lax.ppermute(data, "seq", pairs)


def shift(data, turn_x, turn_y):
    pairs = []
    for x in range(X_SIZE):
        for y in range(Y_SIZE):
            to_x, to_y = (x + turn_x) % X_SIZE, (y + turn_y) % Y_SIZE
            pairs.append((x * Y_SIZE + y, to_x * Y_SIZE + to_y))
    return lax.ppermute(data, "dp", pairs)


def ring_start(shard):
    return jnp.concatenate([shard] + [shift(shard, -dx, 0) for dx in X_TURNS[1:]], axis=0)


def ring_steps(ups, downs, steps):
    ups, downs = list(ups), list(downs)
    for _ in range(steps):
        ups.append(shift(ups[-1], 0, 1))
        downs.append(shift(downs[-1], 0, -1))
    return ups, downs


def ring_end(ups, downs):
    return shift(ups[-1][: 2 * BLOCK], 0, 1), shift(downs[-1][2 * BLOCK :], 0, -1)


def on_device(
    encoder_timesteps,
    tile_parent_sequence,
    tile_recording_label,
    tile_valid_timesteps,
    standardize_scaling,
    triple_projector,
    final_projector,
    lowered_maps,
    raising_maps,
    focus_softness,
    result_adjoint,
):
    core = lax.axis_index("seq") % 2
    def own(left, right):
        return jnp.where(core == 0, left, right)

    starts = [n * 2 * HALF for n in range(3)]
    triple = [
        own(
            triple_projector[:, first : first + HALF],
            triple_projector[:, first + HALF : first + 2 * HALF],
        )
        for first in starts
    ]
    raising = raising_maps.reshape(2 * RANK, UPS).T
    raising = jnp.concatenate([raising, jnp.zeros_like(raising)], axis=0)
    narrow = jnp.concatenate([*triple, lowered_maps[0], lowered_maps[1], raising], axis=1)
    whole = lax.all_gather(narrow, "dp", axis=0, tiled=True)
    outward = jnp.concatenate([final_projector[:, : WIDE // 2], final_projector[:, WIDE // 2 :]], axis=0)

    x = encoder_timesteps.reshape(ROWS, WIDE)
    packed = pack(
        tile_parent_sequence,
        tile_recording_label,
        tile_valid_timesteps,
        x,
        standardize_scaling.reshape(1, WIDE),
    )
    packed, outward = lax.optimization_barrier((packed, outward))
    packed = exchange(packed, "seq")
    block = ring_start(outward)
    ups, downs = ring_steps([block], [block], 3)
    far_a, far_b = ring_end(ups, downs)
    packed, far_a, far_b = lax.optimization_barrier((packed, far_a, far_b))
    pieces = (block, ups[1], downs[1], ups[2], downs[2], ups[3], downs[3], far_a, far_b)
    dp = lax.axis_index("dp")
    places = jnp.stack([core, dp // Y_SIZE, dp % Y_SIZE]).astype(jnp.int32)
    cot, out_a, out_b = cotangent(
        places,
        tile_parent_sequence,
        tile_valid_timesteps,
        result_adjoint.reshape(ROWS, WIDE),
        pieces,
    )
    cot = exchange(cot, "seq")
    normed = [part.reshape(PACKED, WIDE + FACTS) for part in (packed, swap_cores(packed))]
    context, *saved = forward(places, focus_softness, *normed, whole)
    cot, context = lax.optimization_barrier((cot, context))
    keep, send, up = backward(places, focus_softness, saved, cot, normed, whole)
    context = exchange(context.reshape(OWNERS, 2 * SLOTS * LEN, HALF), "seq")
    parts = combine(places, keep, swap_cores(send), up)
    parts, context = lax.optimization_barrier((parts, context))
    parts = exchange(parts.reshape(SHARDS, GRAD, 2 * RANK), "dp")
    block_out = finish(tile_parent_sequence, tile_valid_timesteps, context, x, out_a, out_b)
    shard_down, shard_up = add_owners(exchange(add_shards(parts), "seq"))
    return block_out.reshape(encoder_timesteps.shape), shard_down, jnp.swapaxes(shard_up, 1, 2)


def solution(mesh):
    in_specs = (
        P(("dp", "seq"), None, None),
        P(("dp", "seq")),
        P(("dp", "seq")),
        P(("dp", "seq")),
        P(),
        P("dp", None),
        P("dp", None),
        P(None, "dp", None),
        P(None, None, "dp"),
        P(),
        P(("dp", "seq"), None, None),
    )
    out_specs = (P(("dp", "seq"), None, None), P(None, "dp", None), P(None, None, "dp"))
    return jax.shard_map(
        on_device, mesh=mesh, in_specs=in_specs, out_specs=out_specs, check_vma=False
    )
```

```python
import math

import jax
import jax.numpy as jnp
from jax import lax
from jax.experimental import pallas as pl
from jax.experimental.pallas import tpu as pltpu
from jax.sharding import PartitionSpec as P

EPS_NORM = 1e-05
EPS_HEAD = 1e-06
WIDE = 1536
PANELS = 16
LEN = 16
ROWS = PANELS * LEN
OWNERS = 16
SLOTS = 2
PACKED = OWNERS * SLOTS * LEN
HEAD = 96
FOCI = 4
HALF = FOCI * HEAD
RANK = 64
SHARDS = 32
BLOCK = WIDE // SHARDS
UPS = 2 * HALF // SHARDS
GRAD = 2 * UPS
HIDDEN = 2 * HALF
QUARTER = WIDE // 4
FACTS = 128
QKVL = 3 * HALF + 2 * RANK
F32 = jnp.float32
BF16 = jnp.bfloat16
SMEM = pltpu.MemorySpace.SMEM
VMEM = pltpu.MemorySpace.VMEM


def dot(a, b):
    return lax.dot_general(a, b, (((1,), (0,)), ((), ())), preferred_element_type=F32)


def dot_nt(a, b):
    return lax.dot_general(a, b, (((1,), (1,)), ((), ())), preferred_element_type=F32)


def slot_places(owner_ref):
    owners = [owner_ref[p] for p in range(PANELS)]
    places = []
    for p in range(PANELS):
        rank = jnp.int32(0)
        for q in range(p):
            rank = rank + jnp.where(owners[q] == owners[p], 1, 0)
        places.append(owners[p] * SLOTS + rank)
    return places


def spread(scalars, shape, axis):
    index = lax.broadcasted_iota(jnp.int32, shape, axis)
    panel = index // LEN
    values = jnp.zeros(shape, jnp.int32)
    for p in range(PANELS):
        values = jnp.where(panel == p, scalars[p], values)
    return values, index % LEN


def pack_kernel(owner_ref, tag_ref, live_ref, x_ref, gain_ref, packed_ref):
    place, step = spread(slot_places(owner_ref), (1, ROWS), 1)
    target = place * LEN + step
    slots = lax.broadcasted_iota(jnp.int32, (PACKED, ROWS), 0)
    select = jnp.where(slots == target, 1.0, 0.0).astype(BF16)
    values = x_ref[...].astype(F32)
    centred = values - jnp.mean(values, axis=-1, keepdims=True)
    scaled = centred * lax.rsqrt(jnp.mean(centred * centred, axis=-1, keepdims=True) + EPS_NORM)
    normed = (scaled * gain_ref[...]).astype(BF16)
    packed_ref[:, :, :WIDE] = dot(select, normed).astype(BF16).reshape(OWNERS, SLOTS * LEN, WIDE)
    tags, step = spread([tag_ref[p] for p in range(PANELS)], (ROWS, FACTS), 0)
    lives, _ = spread([live_ref[p] for p in range(PANELS)], (ROWS, FACTS), 0)
    lane = lax.broadcasted_iota(jnp.int32, (ROWS, FACTS), 1)
    alive = jnp.where(step < lives, 1, 0)
    facts = jnp.where(lane == 0, tags, jnp.where(lane == 1, alive, 0)).astype(F32).astype(BF16)
    packed_ref[:, :, WIDE:] = dot(select, facts).astype(BF16).reshape(OWNERS, SLOTS * LEN, FACTS)


def pack(owners, tags, lives, x, gain):
    return pl.pallas_call(
        pack_kernel,
        out_shape=jax.ShapeDtypeStruct((OWNERS, SLOTS * LEN, WIDE + FACTS), BF16),
        in_specs=[pl.BlockSpec(memory_space=SMEM)] * 3 + [pl.BlockSpec(memory_space=VMEM)] * 2,
        out_specs=pl.BlockSpec(memory_space=VMEM),
        compiler_params=pltpu.CompilerParams(vmem_limit_bytes=32 << 20),
        cost_estimate=pl.CostEstimate(
            flops=2 * PACKED * ROWS * WIDE, bytes_accessed=4 * PACKED * WIDE, transcendentals=0
        ),
        name="pack",
    )(owners, tags, lives, x, gain)


def shard_kernel(core_ref, triple_ref, lowered_ref, raising_ref, final_ref, shard_ref):
    core = core_ref[0]
    for n in range(3):
        first = pl.multiple_of(n * HIDDEN + core * HALF, HALF)
        shard_ref[:, n * HALF : (n + 1) * HALF] = triple_ref[:, pl.ds(first, HALF)]
    lowered = [lowered_ref[n].astype(F32) for n in range(2)]
    shard_ref[:, 3 * HALF : QKVL] = jnp.concatenate(lowered, axis=1).astype(BF16)
    raising = jnp.concatenate([raising_ref[n].astype(F32) for n in range(2)], axis=1)
    shard_ref[:, QKVL : QKVL + 2 * RANK] = pad_rows(raising, BLOCK).astype(BF16)
    quarters = []
    for q in range(2):
        first = pl.multiple_of(core * (WIDE // 2) + q * QUARTER, QUARTER)
        quarters.append(final_ref[:, pl.ds(first, QUARTER)].astype(F32))
    shard_ref[:, QKVL + 2 * RANK :] = jnp.concatenate(quarters, axis=0).astype(BF16)


def make_shard(core, triple, lowered, raising, final):
    return pl.pallas_call(
        shard_kernel,
        out_shape=jax.ShapeDtypeStruct((BLOCK, QKVL + 2 * RANK + QUARTER), BF16),
        in_specs=[pl.BlockSpec(memory_space=SMEM)] + [pl.BlockSpec(memory_space=VMEM)] * 4,
        out_specs=pl.BlockSpec(memory_space=VMEM),
        compiler_params=pltpu.CompilerParams(vmem_limit_bytes=60 << 20),
        name="make_shard",
    )(core, triple, lowered, raising, final)


def pack_masked_kernel(owner_ref, live_ref, adjoint_ref, packed_ref):
    place, step = spread(slot_places(owner_ref), (1, ROWS), 1)
    target = place * LEN + step
    slots = lax.broadcasted_iota(jnp.int32, (PACKED, ROWS), 0)
    select = jnp.where(slots == target, 1.0, 0.0).astype(BF16)
    lives, step = spread([live_ref[p] for p in range(PANELS)], (ROWS, 1), 0)
    masked = jnp.where(step < lives, adjoint_ref[...].astype(F32), 0.0).astype(BF16)
    packed_ref[...] = dot(select, masked).astype(BF16).reshape(packed_ref.shape)


def pack_masked(owners, lives, adjoint):
    return pl.pallas_call(
        pack_masked_kernel,
        out_shape=jax.ShapeDtypeStruct((OWNERS, SLOTS * LEN, WIDE), BF16),
        in_specs=[pl.BlockSpec(memory_space=SMEM)] * 2 + [pl.BlockSpec(memory_space=VMEM)],
        out_specs=pl.BlockSpec(memory_space=VMEM),
        compiler_params=pltpu.CompilerParams(vmem_limit_bytes=32 << 20),
        cost_estimate=pl.CostEstimate(
            flops=2 * PACKED * ROWS * WIDE, bytes_accessed=4 * PACKED * WIDE, transcendentals=0
        ),
        name="pack_masked",
    )(owners, lives, adjoint)


def pad_rows(values, rows=128):
    return jnp.concatenate([values, jnp.zeros((rows - values.shape[0], values.shape[1]), values.dtype)], axis=0)


def owner_copies(sources, landing, sems):
    return [pltpu.make_async_copy(source, landing.at[o], sems.at[o]) for o, source in enumerate(sources)]


def raising_of(raise_s):
    tall = raise_s[...].astype(F32).reshape(SHARDS // 2, BLOCK, 2 * RANK)[:, :UPS]
    raising = tall.reshape(HALF, 2 * RANK).T
    row = lax.broadcasted_iota(jnp.int32, raising.shape, 0)
    raise_q = jnp.where(row < RANK, raising, 0.0).astype(BF16)
    raise_v = jnp.where(row < RANK, 0.0, raising).astype(BF16)
    return raise_q, raise_v


def unit(values):
    scale = lax.rsqrt(jnp.sum(values * values, axis=0, keepdims=True) * (1.0 / HEAD) + EPS_HEAD)
    return values * scale, scale


def forward_kernel(
    core_ref,
    soft_ref,
    mine_ref,
    other_ref,
    whole_ref,
    context_ref,
    out_ref,
    weights_ref,
    qkv_ref,
    low_ref,
    mixed_ref,
    inverse_ref,
    normed_s,
    weight_s,
    raise_s,
    base_s,
    row_sems,
    weight_sems,
    raise_sem,
    out_sem,
):
    owner = pl.program_id(0)
    core = core_ref[0]
    rows = owner_copies((mine_ref, other_ref), normed_s, row_sems)
    outs = pltpu.make_async_copy(
        whole_ref.at[:, pl.ds(QKVL + 2 * RANK, QUARTER)], out_ref, out_sem
    )
    tiles = [
        pltpu.make_async_copy(
            whole_ref.at[:, pl.ds(n * 256, 256)],
            weight_s.at[:, pl.ds(n * 256, 256)],
            weight_sems.at[n],
        )
        for n in range(QKVL // 256)
    ]
    half = pl.ds(pl.multiple_of(core * (WIDE // 2), WIDE // 2), WIDE // 2)
    raises = pltpu.make_async_copy(
        whole_ref.at[half, pl.ds(QKVL, 2 * RANK)], raise_s, raise_sem
    )

    @pl.when(owner == 0)
    def _():
        rows[0].start()
        for tile in tiles:
            tile.start()
        raises.start()
        rows[1].start()
        outs.start()
        rows[0].wait()

    @pl.when(owner == 1)
    def _():
        rows[1].wait()
        outs.wait()

    for n, tile in enumerate(tiles):

        @pl.when(owner == 0)
        def _():
            tile.wait()

        columns = slice(n * 256, (n + 1) * 256)
        base_s[:, columns] = dot(normed_s[owner, :, :WIDE], weight_s[:, columns])

    @pl.when(owner == 0)
    def _():
        raises.wait()

    low = base_s[:, 3 * HALF :].astype(BF16)
    low_ref[...] = low
    raise_q, raise_v = raising_of(raise_s)
    query = (base_s[:, :HALF] + dot(low, raise_q)).astype(BF16).astype(F32).T
    key = base_s[:, HALF : 2 * HALF].astype(BF16).astype(F32).T
    value = (base_s[:, 2 * HALF : 3 * HALF] + dot(low, raise_v)).astype(BF16).astype(F32).T
    qkv_ref[:HALF, :] = query.astype(BF16)
    qkv_ref[HALF : 2 * HALF, :] = key.astype(BF16)
    qkv_ref[2 * HALF :, :] = value.astype(BF16)

    rows_j = lax.broadcasted_iota(jnp.int32, (PACKED, PACKED), 0)
    rows_i = lax.broadcasted_iota(jnp.int32, (PACKED, PACKED), 1)
    facts = normed_s[owner, :, WIDE:].astype(F32)
    codes = jnp.where(facts[:, 1:2] > 0.5, facts[:, 0:1], -1.0)
    allowed = (facts.T[0:1, :] == codes) | (rows_j == rows_i)
    ones_rows = jnp.where(lax.broadcasted_iota(jnp.int32, (32, PACKED), 0) < 2, 1.0, 0.0)

    for h in range(FOCI):
        head = slice(h * HEAD, (h + 1) * HEAD)
        temper = soft_ref[core * FOCI + h] * (1.0 / HEAD)
        qn, _ = unit(query[head, :])
        kn, _ = unit(key[head, :])
        qs = pad_rows(qn * (temper * math.log2(math.e))).astype(BF16)
        v = jnp.concatenate([value[head, :], ones_rows], axis=0)
        scores = dot(pad_rows(kn).T.astype(BF16), qs)
        unnormed = jnp.exp2(jnp.where(allowed, scores, -1e30)).astype(BF16)
        weights_ref[h] = unnormed
        mixed = dot(v.astype(BF16), unnormed)
        inverse = 1.0 / mixed[HEAD : HEAD + 1, :]
        inverse_ref[h : h + 1, :] = inverse
        mixed_ref[head, :] = mixed[:HEAD, :] * inverse

    context_ref[...] = mixed_ref[...].T.astype(BF16).reshape(context_ref.shape)


def forward(core, soft, mine, other, whole):
    anywhere = pl.BlockSpec(memory_space=pl.ANY)
    grid = pltpu.PrefetchScalarGridSpec(
        num_scalar_prefetch=1,
        grid=(2,),
        in_specs=[
            pl.BlockSpec(memory_space=SMEM),
        ]
        + [anywhere] * 3,
        out_specs=[
            pl.BlockSpec((OWNERS, None, SLOTS * LEN, HALF), lambda o, c: (0, o, 0, 0)),
            anywhere,
            pl.BlockSpec((None, FOCI, PACKED, PACKED), lambda o, c: (o, 0, 0, 0)),
            pl.BlockSpec((None, 3 * HALF, PACKED), lambda o, c: (o, 0, 0)),
            pl.BlockSpec((None, PACKED, 2 * RANK), lambda o, c: (o, 0, 0)),
            pl.BlockSpec((None, HALF, PACKED), lambda o, c: (o, 0, 0)),
            pl.BlockSpec((None, 8, PACKED), lambda o, c: (o, 0, 0)),
        ],
        scratch_shapes=[
            pltpu.VMEM((2, PACKED, WIDE + FACTS), BF16),
            pltpu.VMEM((WIDE, QKVL), BF16),
            pltpu.VMEM((WIDE // 2, 2 * RANK), BF16),
            pltpu.VMEM((PACKED, QKVL), F32),
            pltpu.SemaphoreType.DMA((2,)),
            pltpu.SemaphoreType.DMA((QKVL // 256,)),
            pltpu.SemaphoreType.DMA,
            pltpu.SemaphoreType.DMA,
        ],
    )
    return pl.pallas_call(
        forward_kernel,
        grid_spec=grid,
        out_shape=(
            jax.ShapeDtypeStruct((OWNERS, 2, SLOTS * LEN, HALF), BF16),
            jax.ShapeDtypeStruct((WIDE, QUARTER), BF16),
            jax.ShapeDtypeStruct((2, FOCI, PACKED, PACKED), BF16),
            jax.ShapeDtypeStruct((2, 3 * HALF, PACKED), BF16),
            jax.ShapeDtypeStruct((2, PACKED, 2 * RANK), BF16),
            jax.ShapeDtypeStruct((2, HALF, PACKED), F32),
            jax.ShapeDtypeStruct((2, 8, PACKED), F32),
        ),
        compiler_params=pltpu.CompilerParams(
            vmem_limit_bytes=36 << 20, dimension_semantics=("arbitrary",)
        ),
        cost_estimate=pl.CostEstimate(
            flops=6 << 30, bytes_accessed=16 << 20, transcendentals=2 * FOCI * PACKED * PACKED
        ),
        name="forward",
    )(core, soft, mine, other, whole)


def backward_kernel(
    core_ref,
    soft_ref,
    weights_ref,
    qkv_ref,
    low_ref,
    mixed_ref,
    inverse_ref,
    mine_ref,
    other_ref,
    masked_mine_ref,
    masked_other_ref,
    whole_ref,
    out_own_ref,
    out_other_ref,
    keep_ref,
    send_ref,
    up_ref,
    normed_s,
    masked_s,
    out_s,
    tight_s,
    raise_s,
    cot_s,
    dquery_s,
    dvalue_s,
    down_s,
    up_s,
    row_sems,
    masked_sems,
    out_sems,
    raise_sem,
):
    owner = pl.program_id(0)
    core = core_ref[0]
    body = pl.ds(0, WIDE)
    rows = owner_copies((mine_ref.at[:, body], other_ref.at[:, body]), normed_s, row_sems)
    masks = owner_copies((masked_mine_ref, masked_other_ref), masked_s, masked_sems)
    half = pl.ds(pl.multiple_of(core * (WIDE // 2), WIDE // 2), WIDE // 2)
    raises = pltpu.make_async_copy(
        whole_ref.at[half, pl.ds(QKVL, 2 * RANK)], raise_s, raise_sem
    )
    outs = owner_copies(
        (out_own_ref.at[half, :], out_other_ref.at[half, :]),
        out_s,
        out_sems,
    )

    @pl.when(owner == 0)
    def _():
        masks[0].start()
        outs[0].start()
        outs[1].start()
        rows[0].start()
        raises.start()
        masks[1].start()
        rows[1].start()
        down_s[...] = jnp.zeros_like(down_s)
        up_s[...] = jnp.zeros_like(up_s)
        masks[0].wait()
        for n, out in enumerate(outs):
            out.wait()
            tall = out_s[n].astype(F32).reshape(SHARDS // 2, BLOCK, QUARTER)
            for q in range(2):
                tight = tall[:, q * UPS : (q + 1) * UPS].reshape(HALF, QUARTER)
                tight_s[n, :, q * QUARTER : (q + 1) * QUARTER] = tight.astype(BF16)

    @pl.when(owner == 1)
    def _():
        masks[1].wait()

    total = jnp.zeros((HALF, PACKED), F32)
    for n, side in enumerate((core, 1 - core)):
        columns = pl.ds(pl.multiple_of(side * (WIDE // 2), WIDE // 2), WIDE // 2)
        total = total + dot_nt(tight_s[n], masked_s[owner, :, columns])
    cot_s[...] = total.astype(BF16).astype(F32)

    ones_rows = jnp.where(lax.broadcasted_iota(jnp.int32, (32, PACKED), 0) < 2, 1.0, 0.0)
    sub = lax.broadcasted_iota(jnp.int32, (32, PACKED), 0)

    for h in range(FOCI):
        head = slice(h * HEAD, (h + 1) * HEAD)
        temper = soft_ref[core * FOCI + h] * (1.0 / HEAD)
        qn, rq = unit(qkv_ref[head, :].astype(F32))
        kn, _ = unit(qkv_ref[HALF + h * HEAD : HALF + (h + 1) * HEAD, :].astype(F32))
        value = qkv_ref[2 * HALF + h * HEAD : 2 * HALF + (h + 1) * HEAD, :].astype(F32)
        v = jnp.concatenate([value, ones_rows], axis=0)
        unnormed = weights_ref[h]
        dc = (cot_s[head, :] * inverse_ref[h : h + 1, :]).astype(BF16)
        shift = jnp.sum(dc.astype(F32) * mixed_ref[head, :], axis=0, keepdims=True)
        shift_top = shift.astype(BF16).astype(F32)
        extra = jnp.where(sub == 0, -shift_top, jnp.where(sub == 1, shift_top - shift, 0.0))
        dc = jnp.concatenate([dc, extra.astype(BF16)], axis=0)
        inner = dot(v.T.astype(BF16), dc)
        dscores = (unnormed.astype(F32) * inner).astype(BF16)
        dqn = dot(pad_rows(kn).astype(BF16), dscores)[:HEAD, :] * temper
        dq = rq * (dqn - qn * (jnp.sum(qn * dqn, axis=0, keepdims=True) * (1.0 / HEAD)))
        dquery_s[head, :] = dq.astype(BF16)
        dv = dot_nt(unnormed, dc)
        dvalue_s[head, :] = dv.T[:HEAD, :].astype(BF16)

    @pl.when(owner == 0)
    def _():
        raises.wait()
        rows[0].wait()

    @pl.when(owner == 1)
    def _():
        rows[1].wait()

    low = low_ref[...]
    raise_q, raise_v = raising_of(raise_s)
    dquery = dquery_s[...]
    dvalue = dvalue_s[...]
    lane = lax.broadcasted_iota(jnp.int32, (HALF, 2 * RANK), 1)
    up_s[...] += jnp.where(lane < RANK, dot(dquery, low), dot(dvalue, low))
    inner_t = (dot(raise_q, dquery) + dot(raise_v, dvalue)).astype(BF16)
    down_s[...] += dot(inner_t, normed_s[owner])

    @pl.when(owner == 1)
    def _():
        down = down_s[...].T.reshape(SHARDS, BLOCK, 2 * RANK)
        first = down[:, :UPS].reshape(SHARDS * UPS, 2 * RANK)
        second = down[:, UPS:].reshape(SHARDS * UPS, 2 * RANK)
        keep_ref[...] = jnp.where(core == 0, first, second)
        send_ref[...] = jnp.where(core == 0, second, first).astype(BF16)
        up_ref[...] = up_s[...]


def backward(core, soft, saved, normed, masked, whole, out_own, out_other):
    anywhere = pl.BlockSpec(memory_space=pl.ANY)
    grid = pltpu.PrefetchScalarGridSpec(
        num_scalar_prefetch=1,
        grid=(2,),
        in_specs=[
            pl.BlockSpec(memory_space=SMEM),
            pl.BlockSpec((None, FOCI, PACKED, PACKED), lambda o, c: (o, 0, 0, 0)),
            pl.BlockSpec((None, 3 * HALF, PACKED), lambda o, c: (o, 0, 0)),
            pl.BlockSpec((None, PACKED, 2 * RANK), lambda o, c: (o, 0, 0)),
            pl.BlockSpec((None, HALF, PACKED), lambda o, c: (o, 0, 0)),
            pl.BlockSpec((None, 8, PACKED), lambda o, c: (o, 0, 0)),
        ]
        + [anywhere] * 7,
        out_specs=[
            pl.BlockSpec((SHARDS * UPS, 2 * RANK), lambda o, c: (0, 0)),
            pl.BlockSpec((SHARDS * UPS, 2 * RANK), lambda o, c: (0, 0)),
            pl.BlockSpec((HALF, 2 * RANK), lambda o, c: (0, 0)),
        ],
        scratch_shapes=[
            pltpu.VMEM((2, PACKED, WIDE), BF16),
            pltpu.VMEM((2, PACKED, WIDE), BF16),
            pltpu.VMEM((2, WIDE // 2, QUARTER), BF16),
            pltpu.VMEM((2, HALF, WIDE // 2), BF16),
            pltpu.VMEM((WIDE // 2, 2 * RANK), BF16),
            pltpu.VMEM((HALF, PACKED), F32),
            pltpu.VMEM((HALF, PACKED), BF16),
            pltpu.VMEM((HALF, PACKED), BF16),
            pltpu.VMEM((2 * RANK, WIDE), F32),
            pltpu.VMEM((HALF, 2 * RANK), F32),
            pltpu.SemaphoreType.DMA((2,)),
            pltpu.SemaphoreType.DMA((2,)),
            pltpu.SemaphoreType.DMA((2,)),
            pltpu.SemaphoreType.DMA,
        ],
    )
    return pl.pallas_call(
        backward_kernel,
        grid_spec=grid,
        out_shape=(
            jax.ShapeDtypeStruct((SHARDS * UPS, 2 * RANK), F32),
            jax.ShapeDtypeStruct((SHARDS * UPS, 2 * RANK), BF16),
            jax.ShapeDtypeStruct((HALF, 2 * RANK), F32),
        ),
        compiler_params=pltpu.CompilerParams(
            vmem_limit_bytes=36 << 20, dimension_semantics=("arbitrary",)
        ),
        cost_estimate=pl.CostEstimate(flops=8 << 30, bytes_accessed=16 << 20, transcendentals=0),
        name="backward",
    )(core, soft, *saved, *normed, *masked, whole, out_own, out_other)


def combine_kernel(core_ref, keep_ref, come_ref, up_ref, parts_ref):
    down = keep_ref[...] + come_ref[...].astype(F32)
    up = up_ref[...]
    none = jnp.zeros_like(up)
    low_half = core_ref[0] == 0
    up = jnp.concatenate([jnp.where(low_half, up, none), jnp.where(low_half, none, up)], axis=0)
    shape = (SHARDS, UPS, 2 * RANK)
    parts = jnp.concatenate([down.reshape(shape), up.reshape(shape)], axis=1)
    parts_ref[...] = parts.reshape(parts_ref.shape).astype(BF16)


def combine(core, keep, come, up):
    return pl.pallas_call(
        combine_kernel,
        out_shape=jax.ShapeDtypeStruct((SHARDS * GRAD, 2 * RANK), BF16),
        in_specs=[pl.BlockSpec(memory_space=SMEM)] + [pl.BlockSpec(memory_space=VMEM)] * 3,
        out_specs=pl.BlockSpec(memory_space=VMEM),
        compiler_params=pltpu.CompilerParams(vmem_limit_bytes=8 << 20),
        name="combine",
    )(core, keep, come, up)


def finish_kernel(core_ref, owner_ref, live_ref, context_ref, x_ref, *refs):
    *out_refs, block_ref = refs
    core = core_ref[0]
    place, step = spread(slot_places(owner_ref), (ROWS, 1), 0)
    target = place * LEN + step
    slots = lax.broadcasted_iota(jnp.int32, (ROWS, PACKED), 1)
    select = jnp.where(slots == target, 1.0, 0.0).astype(BF16)
    lives, _ = spread([live_ref[p] for p in range(PANELS)], (ROWS, 1), 0)
    halves = []
    for half in range(2):
        parts = []
        for o in range(OWNERS):
            source = o // 2 * 2 + half
            first = 0 if source == o else SLOTS * LEN
            parts.append(context_ref[source, first : first + SLOTS * LEN, :])
        halves.append(dot(select, jnp.concatenate(parts, axis=0)).astype(BF16))
    for n, ref in enumerate(out_refs):
        side = core if n < 2 else 1 - core
        first = pl.multiple_of(side * (WIDE // 2) + n % 2 * QUARTER, QUARTER)
        columns = pl.ds(first, QUARTER)
        attended = dot(halves[0], ref[:HALF, :]) + dot(halves[1], ref[HALF:, :])
        added = jnp.where(step < lives, attended, 0.0)
        block_ref[:, columns] = (x_ref[:, columns].astype(F32) + added).astype(BF16)


def finish(core, owners, lives, context, x, outs):
    return pl.pallas_call(
        finish_kernel,
        out_shape=jax.ShapeDtypeStruct((ROWS, WIDE), BF16),
        in_specs=[pl.BlockSpec(memory_space=SMEM)] * 3 + [pl.BlockSpec(memory_space=VMEM)] * 6,
        out_specs=pl.BlockSpec(memory_space=VMEM),
        compiler_params=pltpu.CompilerParams(vmem_limit_bytes=40 << 20),
        cost_estimate=pl.CostEstimate(
            flops=2 * ROWS * 2 * HALF * (WIDE + PACKED), bytes_accessed=6 << 20, transcendentals=0
        ),
        name="finish",
    )(core, owners, lives, context, x, *outs)


def add_shards_kernel(part_ref, total_ref):
    total = part_ref[0].astype(F32)
    for t in range(1, SHARDS):
        total = total + part_ref[t].astype(F32)
    total = total.astype(BF16)
    for o in range(OWNERS):
        total_ref[o] = total


def add_shards(parts):
    return pl.pallas_call(
        add_shards_kernel,
        out_shape=jax.ShapeDtypeStruct((OWNERS, GRAD, 2 * RANK), BF16),
        in_specs=[pl.BlockSpec(memory_space=VMEM)],
        out_specs=pl.BlockSpec(memory_space=VMEM),
        compiler_params=pltpu.CompilerParams(vmem_limit_bytes=8 << 20),
        name="add_shards",
    )(parts)


def add_owners_kernel(part_ref, down_ref, up_ref):
    downs = [jnp.zeros((UPS, 2 * RANK), F32)] * 2
    up = jnp.zeros((UPS, 2 * RANK), F32)
    for o in range(OWNERS):
        part = part_ref[o].astype(F32)
        downs[o % 2] = downs[o % 2] + part[:UPS, :]
        up = up + part[UPS:, :]
    down = jnp.concatenate(downs, axis=0)
    for n in range(2):
        down_ref[n] = down[:, n * RANK : (n + 1) * RANK]
        up_ref[n] = up[:, n * RANK : (n + 1) * RANK]


def add_owners(parts):
    return pl.pallas_call(
        add_owners_kernel,
        out_shape=(
            jax.ShapeDtypeStruct((2, BLOCK, RANK), F32),
            jax.ShapeDtypeStruct((2, UPS, RANK), F32),
        ),
        in_specs=[pl.BlockSpec(memory_space=VMEM)],
        out_specs=(pl.BlockSpec(memory_space=VMEM),) * 2,
        compiler_params=pltpu.CompilerParams(vmem_limit_bytes=8 << 20),
        name="add_owners",
    )(parts)


def exchange(data, axis):
    return lax.all_to_all(data, axis, split_axis=0, concat_axis=0, tiled=True)


def swap_cores(data):
    pairs = [(s, s ^ 1) for s in range(OWNERS)]
    return lax.ppermute(data, "seq", pairs)


def on_device(
    encoder_timesteps,
    tile_parent_sequence,
    tile_recording_label,
    tile_valid_timesteps,
    standardize_scaling,
    triple_projector,
    final_projector,
    lowered_maps,
    raising_maps,
    focus_softness,
    result_adjoint,
):
    core = (lax.axis_index("seq") % 2).astype(jnp.int32).reshape(1)
    shard = make_shard(
        core, triple_projector, lowered_maps, jnp.swapaxes(raising_maps, 1, 2), final_projector
    )
    whole = lax.all_gather(shard, "dp", axis=0, tiled=True)

    x = encoder_timesteps.reshape(ROWS, WIDE)
    packed = pack(
        tile_parent_sequence,
        tile_recording_label,
        tile_valid_timesteps,
        x,
        standardize_scaling.reshape(1, WIDE),
    )
    packed, adjoint = lax.optimization_barrier((packed, result_adjoint.reshape(ROWS, WIDE)))
    masked = pack_masked(tile_parent_sequence, tile_valid_timesteps, adjoint)
    packed = exchange(packed, "seq")
    packed, masked = lax.optimization_barrier((packed, masked))
    masked = exchange(masked, "seq")
    normed = [part.reshape(PACKED, WIDE + FACTS) for part in (packed, swap_cores(packed))]
    context, out_own, *saved = forward(core, focus_softness, *normed, whole)
    masked, context = lax.optimization_barrier((masked, context))
    masked = [part.reshape(PACKED, WIDE) for part in (masked, swap_cores(masked))]
    out_other = swap_cores(out_own)
    keep, send, up = backward(core, focus_softness, saved, normed, masked, whole, out_own, out_other)
    context = exchange(context.reshape(OWNERS, 2 * SLOTS * LEN, HALF), "seq")
    parts = combine(core, keep, swap_cores(send), up)
    outs = []
    for part in (out_own, out_other):
        part = part.reshape(SHARDS, BLOCK, QUARTER)
        outs += [part[:, :UPS].reshape(HIDDEN, QUARTER), part[:, UPS:].reshape(HIDDEN, QUARTER)]
    parts, context = lax.optimization_barrier((parts, context))
    parts = exchange(parts.reshape(SHARDS, GRAD, 2 * RANK), "dp")
    block_out = finish(core, tile_parent_sequence, tile_valid_timesteps, context, x, outs)
    shard_down, shard_up = add_owners(exchange(add_shards(parts), "seq"))
    return block_out.reshape(encoder_timesteps.shape), shard_down, jnp.swapaxes(shard_up, 1, 2)


def solution(mesh):
    in_specs = (
        P(("dp", "seq"), None, None),
        P(("dp", "seq")),
        P(("dp", "seq")),
        P(("dp", "seq")),
        P(),
        P("dp", None),
        P("dp", None),
        P(None, "dp", None),
        P(None, None, "dp"),
        P(),
        P(("dp", "seq"), None, None),
    )
    out_specs = (P(("dp", "seq"), None, None), P(None, "dp", None), P(None, None, "dp"))
    return jax.shard_map(
        on_device, mesh=mesh, in_specs=in_specs, out_specs=out_specs, check_vma=False
    )
```

```python
import math

import jax
import jax.numpy as jnp
from jax import lax
from jax.experimental import pallas as pl
from jax.experimental.pallas import tpu as pltpu
from jax.sharding import PartitionSpec as P

EPS_NORM = 1e-05
EPS_HEAD = 1e-06
WIDE = 1536
PANELS = 16
LEN = 16
ROWS = PANELS * LEN
OWNERS = 16
SLOTS = 2
PACKED = OWNERS * SLOTS * LEN
HEAD = 96
FOCI = 4
HALF = FOCI * HEAD
RANK = 64
SHARDS = 32
BLOCK = WIDE // SHARDS
UPS = 2 * HALF // SHARDS
GRAD = 2 * UPS
HIDDEN = 2 * HALF
QUARTER = WIDE // 4
FACTS = 128
QKVL = 3 * HALF + 2 * RANK
F32 = jnp.float32
BF16 = jnp.bfloat16
SMEM = pltpu.MemorySpace.SMEM
VMEM = pltpu.MemorySpace.VMEM


def dot(a, b):
    return lax.dot_general(a, b, (((1,), (0,)), ((), ())), preferred_element_type=F32)


def dot_nt(a, b):
    return lax.dot_general(a, b, (((1,), (1,)), ((), ())), preferred_element_type=F32)


def slot_places(owner_ref):
    owners = [owner_ref[p] for p in range(PANELS)]
    places = []
    for p in range(PANELS):
        rank = jnp.int32(0)
        for q in range(p):
            rank = rank + jnp.where(owners[q] == owners[p], 1, 0)
        places.append(owners[p] * SLOTS + rank)
    return places


def spread(scalars, shape, axis):
    index = lax.broadcasted_iota(jnp.int32, shape, axis)
    panel = index // LEN
    values = jnp.zeros(shape, jnp.int32)
    for p in range(PANELS):
        values = jnp.where(panel == p, scalars[p], values)
    return values, index % LEN


def pack_kernel(owner_ref, tag_ref, live_ref, x_ref, gain_ref, packed_ref):
    place, step = spread(slot_places(owner_ref), (1, ROWS), 1)
    target = place * LEN + step
    slots = lax.broadcasted_iota(jnp.int32, (PACKED, ROWS), 0)
    select = jnp.where(slots == target, 1.0, 0.0).astype(BF16)
    values = x_ref[...].astype(F32)
    centred = values - jnp.mean(values, axis=-1, keepdims=True)
    scaled = centred * lax.rsqrt(jnp.mean(centred * centred, axis=-1, keepdims=True) + EPS_NORM)
    normed = (scaled * gain_ref[...]).astype(BF16)
    packed_ref[:, :, :WIDE] = dot(select, normed).astype(BF16).reshape(OWNERS, SLOTS * LEN, WIDE)
    tags, step = spread([tag_ref[p] for p in range(PANELS)], (ROWS, FACTS), 0)
    lives, _ = spread([live_ref[p] for p in range(PANELS)], (ROWS, FACTS), 0)
    lane = lax.broadcasted_iota(jnp.int32, (ROWS, FACTS), 1)
    alive = jnp.where(step < lives, 1, 0)
    facts = jnp.where(lane == 0, tags, jnp.where(lane == 1, alive, 0)).astype(F32).astype(BF16)
    packed_ref[:, :, WIDE:] = dot(select, facts).astype(BF16).reshape(OWNERS, SLOTS * LEN, FACTS)


def pack(owners, tags, lives, x, gain):
    return pl.pallas_call(
        pack_kernel,
        out_shape=jax.ShapeDtypeStruct((OWNERS, SLOTS * LEN, WIDE + FACTS), BF16),
        in_specs=[pl.BlockSpec(memory_space=SMEM)] * 3 + [pl.BlockSpec(memory_space=VMEM)] * 2,
        out_specs=pl.BlockSpec(memory_space=VMEM),
        compiler_params=pltpu.CompilerParams(vmem_limit_bytes=32 << 20),
        cost_estimate=pl.CostEstimate(
            flops=2 * PACKED * ROWS * WIDE, bytes_accessed=4 * PACKED * WIDE, transcendentals=0
        ),
        name="pack",
    )(owners, tags, lives, x, gain)


def shard_kernel(core_ref, triple_ref, lowered_ref, raising_ref, final_ref, shard_ref):
    core = core_ref[0]
    for n in range(3):
        first = pl.multiple_of(n * HIDDEN + core * HALF, HALF)
        shard_ref[:, n * HALF : (n + 1) * HALF] = triple_ref[:, pl.ds(first, HALF)]
    lowered = [lowered_ref[n].astype(F32) for n in range(2)]
    shard_ref[:, 3 * HALF : QKVL] = jnp.concatenate(lowered, axis=1).astype(BF16)
    raising = jnp.concatenate([raising_ref[n].astype(F32) for n in range(2)], axis=1)
    shard_ref[:, QKVL : QKVL + 2 * RANK] = pad_rows(raising, BLOCK).astype(BF16)
    quarters = []
    for q in range(2):
        first = pl.multiple_of(core * (WIDE // 2) + q * QUARTER, QUARTER)
        quarters.append(final_ref[:, pl.ds(first, QUARTER)].astype(F32))
    shard_ref[:, QKVL + 2 * RANK :] = jnp.concatenate(quarters, axis=0).astype(BF16)


def make_shard(core, triple, lowered, raising, final):
    return pl.pallas_call(
        shard_kernel,
        out_shape=jax.ShapeDtypeStruct((BLOCK, QKVL + 2 * RANK + QUARTER), BF16),
        in_specs=[pl.BlockSpec(memory_space=SMEM)] + [pl.BlockSpec(memory_space=VMEM)] * 4,
        out_specs=pl.BlockSpec(memory_space=VMEM),
        compiler_params=pltpu.CompilerParams(vmem_limit_bytes=60 << 20),
        name="make_shard",
    )(core, triple, lowered, raising, final)


def pack_masked_kernel(owner_ref, live_ref, adjoint_ref, packed_ref):
    place, step = spread(slot_places(owner_ref), (1, ROWS), 1)
    target = place * LEN + step
    slots = lax.broadcasted_iota(jnp.int32, (PACKED, ROWS), 0)
    select = jnp.where(slots == target, 1.0, 0.0).astype(BF16)
    lives, step = spread([live_ref[p] for p in range(PANELS)], (ROWS, 1), 0)
    masked = jnp.where(step < lives, adjoint_ref[...].astype(F32), 0.0).astype(BF16)
    packed_ref[...] = dot(select, masked).astype(BF16).reshape(packed_ref.shape)


def pack_masked(owners, lives, adjoint):
    return pl.pallas_call(
        pack_masked_kernel,
        out_shape=jax.ShapeDtypeStruct((OWNERS, SLOTS * LEN, WIDE), BF16),
        in_specs=[pl.BlockSpec(memory_space=SMEM)] * 2 + [pl.BlockSpec(memory_space=VMEM)],
        out_specs=pl.BlockSpec(memory_space=VMEM),
        compiler_params=pltpu.CompilerParams(vmem_limit_bytes=32 << 20),
        cost_estimate=pl.CostEstimate(
            flops=2 * PACKED * ROWS * WIDE, bytes_accessed=4 * PACKED * WIDE, transcendentals=0
        ),
        name="pack_masked",
    )(owners, lives, adjoint)


def pad_rows(values, rows=128):
    return jnp.concatenate([values, jnp.zeros((rows - values.shape[0], values.shape[1]), values.dtype)], axis=0)


def owner_copies(sources, landing, sems):
    return [pltpu.make_async_copy(source, landing.at[o], sems.at[o]) for o, source in enumerate(sources)]


def raising_of(raise_s):
    tall = raise_s[...].astype(F32).reshape(SHARDS // 2, BLOCK, 2 * RANK)[:, :UPS]
    raising = tall.reshape(HALF, 2 * RANK).T
    row = lax.broadcasted_iota(jnp.int32, raising.shape, 0)
    raise_q = jnp.where(row < RANK, raising, 0.0).astype(BF16)
    raise_v = jnp.where(row < RANK, 0.0, raising).astype(BF16)
    return raise_q, raise_v


def unit(values):
    scale = lax.rsqrt(jnp.sum(values * values, axis=0, keepdims=True) * (1.0 / HEAD) + EPS_HEAD)
    return values * scale, scale


def forward_kernel(
    core_ref,
    soft_ref,
    mine_ref,
    other_ref,
    whole_ref,
    context_ref,
    out_ref,
    weights_ref,
    qkv_ref,
    low_ref,
    mixed_ref,
    inverse_ref,
    normed_s,
    weight_s,
    raise_s,
    base_s,
    row_sems,
    weight_sems,
    raise_sem,
    out_sem,
):
    owner = pl.program_id(0)
    core = core_ref[0]
    rows = owner_copies((mine_ref, other_ref), normed_s, row_sems)
    outs = pltpu.make_async_copy(
        whole_ref.at[:, pl.ds(QKVL + 2 * RANK, QUARTER)], out_ref, out_sem
    )
    tiles = [
        pltpu.make_async_copy(
            whole_ref.at[:, pl.ds(n * 256, 256)],
            weight_s.at[:, pl.ds(n * 256, 256)],
            weight_sems.at[n],
        )
        for n in range(QKVL // 256)
    ]
    half = pl.ds(pl.multiple_of(core * (WIDE // 2), WIDE // 2), WIDE // 2)
    raises = pltpu.make_async_copy(
        whole_ref.at[half, pl.ds(QKVL, 2 * RANK)], raise_s, raise_sem
    )

    @pl.when(owner == 0)
    def _():
        rows[0].start()
        for tile in tiles:
            tile.start()
        raises.start()
        rows[1].start()
        outs.start()
        rows[0].wait()

    @pl.when(owner == 1)
    def _():
        rows[1].wait()
        outs.wait()

    for n, tile in enumerate(tiles):

        @pl.when(owner == 0)
        def _():
            tile.wait()

        columns = slice(n * 256, (n + 1) * 256)
        base_s[:, columns] = dot(normed_s[owner, :, :WIDE], weight_s[:, columns])

    @pl.when(owner == 0)
    def _():
        raises.wait()

    low = base_s[:, 3 * HALF :].astype(BF16)
    low_ref[...] = low
    raise_q, raise_v = raising_of(raise_s)
    query = (base_s[:, :HALF] + dot(low, raise_q)).astype(BF16).astype(F32).T
    key = base_s[:, HALF : 2 * HALF].astype(BF16).astype(F32).T
    value = (base_s[:, 2 * HALF : 3 * HALF] + dot(low, raise_v)).astype(BF16).astype(F32).T
    qkv_ref[:HALF, :] = query.astype(BF16)
    qkv_ref[HALF : 2 * HALF, :] = key.astype(BF16)
    qkv_ref[2 * HALF :, :] = value.astype(BF16)

    rows_j = lax.broadcasted_iota(jnp.int32, (PACKED, PACKED), 0)
    rows_i = lax.broadcasted_iota(jnp.int32, (PACKED, PACKED), 1)
    facts = normed_s[owner, :, WIDE:].astype(F32)
    codes = jnp.where(facts[:, 1:2] > 0.5, facts[:, 0:1], -1.0)
    allowed = (facts.T[0:1, :] == codes) | (rows_j == rows_i)
    ones_rows = jnp.where(lax.broadcasted_iota(jnp.int32, (32, PACKED), 0) < 2, 1.0, 0.0)

    for h in range(FOCI):
        head = slice(h * HEAD, (h + 1) * HEAD)
        temper = soft_ref[core * FOCI + h] * (1.0 / HEAD)
        qn, _ = unit(query[head, :])
        kn, _ = unit(key[head, :])
        qs = pad_rows(qn * (temper * math.log2(math.e))).astype(BF16)
        v = jnp.concatenate([value[head, :], ones_rows], axis=0)
        scores = dot(pad_rows(kn).T.astype(BF16), qs)
        unnormed = jnp.exp2(jnp.where(allowed, scores, -1e30)).astype(BF16)
        weights_ref[h] = unnormed
        mixed = dot(v.astype(BF16), unnormed)
        inverse = 1.0 / mixed[HEAD : HEAD + 1, :]
        inverse_ref[h : h + 1, :] = inverse
        mixed_ref[head, :] = mixed[:HEAD, :] * inverse

    context_ref[...] = mixed_ref[...].T.astype(BF16).reshape(context_ref.shape)


def forward(core, soft, mine, other, whole):
    anywhere = pl.BlockSpec(memory_space=pl.ANY)
    grid = pltpu.PrefetchScalarGridSpec(
        num_scalar_prefetch=1,
        grid=(2,),
        in_specs=[
            pl.BlockSpec(memory_space=SMEM),
        ]
        + [anywhere] * 3,
        out_specs=[
            pl.BlockSpec((OWNERS, None, SLOTS * LEN, HALF), lambda o, c: (0, o, 0, 0)),
            anywhere,
            pl.BlockSpec((None, FOCI, PACKED, PACKED), lambda o, c: (o, 0, 0, 0)),
            pl.BlockSpec((None, 3 * HALF, PACKED), lambda o, c: (o, 0, 0)),
            pl.BlockSpec((None, PACKED, 2 * RANK), lambda o, c: (o, 0, 0)),
            pl.BlockSpec((None, HALF, PACKED), lambda o, c: (o, 0, 0)),
            pl.BlockSpec((None, 8, PACKED), lambda o, c: (o, 0, 0)),
        ],
        scratch_shapes=[
            pltpu.VMEM((2, PACKED, WIDE + FACTS), BF16),
            pltpu.VMEM((WIDE, QKVL), BF16),
            pltpu.VMEM((WIDE // 2, 2 * RANK), BF16),
            pltpu.VMEM((PACKED, QKVL), F32),
            pltpu.SemaphoreType.DMA((2,)),
            pltpu.SemaphoreType.DMA((QKVL // 256,)),
            pltpu.SemaphoreType.DMA,
            pltpu.SemaphoreType.DMA,
        ],
    )
    return pl.pallas_call(
        forward_kernel,
        grid_spec=grid,
        out_shape=(
            jax.ShapeDtypeStruct((OWNERS, 2, SLOTS * LEN, HALF), BF16),
            jax.ShapeDtypeStruct((WIDE, QUARTER), BF16),
            jax.ShapeDtypeStruct((2, FOCI, PACKED, PACKED), BF16),
            jax.ShapeDtypeStruct((2, 3 * HALF, PACKED), BF16),
            jax.ShapeDtypeStruct((2, PACKED, 2 * RANK), BF16),
            jax.ShapeDtypeStruct((2, HALF, PACKED), F32),
            jax.ShapeDtypeStruct((2, 8, PACKED), F32),
        ),
        compiler_params=pltpu.CompilerParams(
            vmem_limit_bytes=60 << 20, dimension_semantics=("arbitrary",)
        ),
        cost_estimate=pl.CostEstimate(
            flops=6 << 30, bytes_accessed=16 << 20, transcendentals=2 * FOCI * PACKED * PACKED
        ),
        name="forward",
    )(core, soft, mine, other, whole)


def backward_kernel(
    core_ref,
    soft_ref,
    weights_ref,
    qkv_ref,
    low_ref,
    mixed_ref,
    inverse_ref,
    mine_ref,
    other_ref,
    masked_mine_ref,
    masked_other_ref,
    whole_ref,
    out_own_ref,
    out_other_ref,
    keep_ref,
    send_ref,
    up_ref,
    normed_s,
    masked_s,
    out_s,
    tight_s,
    raise_s,
    cot_s,
    dquery_s,
    dvalue_s,
    down_s,
    up_s,
    row_sems,
    masked_sems,
    out_sems,
    raise_sem,
):
    owner = pl.program_id(0)
    core = core_ref[0]
    body = pl.ds(0, WIDE)
    rows = owner_copies((mine_ref.at[:, body], other_ref.at[:, body]), normed_s, row_sems)
    masks = owner_copies((masked_mine_ref, masked_other_ref), masked_s, masked_sems)
    half = pl.ds(pl.multiple_of(core * (WIDE // 2), WIDE // 2), WIDE // 2)
    raises = pltpu.make_async_copy(
        whole_ref.at[half, pl.ds(QKVL, 2 * RANK)], raise_s, raise_sem
    )
    outs = owner_copies(
        (out_own_ref.at[half, :], out_other_ref.at[half, :]),
        out_s,
        out_sems,
    )

    @pl.when(owner == 0)
    def _():
        masks[0].start()
        outs[0].start()
        outs[1].start()
        rows[0].start()
        raises.start()
        masks[1].start()
        rows[1].start()
        down_s[...] = jnp.zeros_like(down_s)
        up_s[...] = jnp.zeros_like(up_s)
        masks[0].wait()
        for n, out in enumerate(outs):
            out.wait()
            tall = out_s[n].astype(F32).reshape(SHARDS // 2, BLOCK, QUARTER)
            for q in range(2):
                tight = tall[:, q * UPS : (q + 1) * UPS].reshape(HALF, QUARTER)
                tight_s[n, :, q * QUARTER : (q + 1) * QUARTER] = tight.astype(BF16)

    @pl.when(owner == 1)
    def _():
        masks[1].wait()

    total = jnp.zeros((HALF, PACKED), F32)
    for n, side in enumerate((core, 1 - core)):
        columns = pl.ds(pl.multiple_of(side * (WIDE // 2), WIDE // 2), WIDE // 2)
        total = total + dot_nt(tight_s[n], masked_s[owner, :, columns])
    cot_s[...] = total.astype(BF16).astype(F32)

    ones_rows = jnp.where(lax.broadcasted_iota(jnp.int32, (32, PACKED), 0) < 2, 1.0, 0.0)
    sub = lax.broadcasted_iota(jnp.int32, (32, PACKED), 0)

    for h in range(FOCI):
        head = slice(h * HEAD, (h + 1) * HEAD)
        temper = soft_ref[core * FOCI + h] * (1.0 / HEAD)
        qn, rq = unit(qkv_ref[head, :].astype(F32))
        kn, _ = unit(qkv_ref[HALF + h * HEAD : HALF + (h + 1) * HEAD, :].astype(F32))
        value = qkv_ref[2 * HALF + h * HEAD : 2 * HALF + (h + 1) * HEAD, :].astype(F32)
        v = jnp.concatenate([value, ones_rows], axis=0)
        unnormed = weights_ref[h]
        dc = (cot_s[head, :] * inverse_ref[h : h + 1, :]).astype(BF16)
        shift = jnp.sum(dc.astype(F32) * mixed_ref[head, :], axis=0, keepdims=True)
        shift_top = shift.astype(BF16).astype(F32)
        extra = jnp.where(sub == 0, -shift_top, jnp.where(sub == 1, shift_top - shift, 0.0))
        dc = jnp.concatenate([dc, extra.astype(BF16)], axis=0)
        inner = dot(v.T.astype(BF16), dc)
        dscores = (unnormed.astype(F32) * inner).astype(BF16)
        dqn = dot(pad_rows(kn).astype(BF16), dscores)[:HEAD, :] * temper
        dq = rq * (dqn - qn * (jnp.sum(qn * dqn, axis=0, keepdims=True) * (1.0 / HEAD)))
        dquery_s[head, :] = dq.astype(BF16)
        dv = dot_nt(unnormed, dc)
        dvalue_s[head, :] = dv.T[:HEAD, :].astype(BF16)

    @pl.when(owner == 0)
    def _():
        raises.wait()
        rows[0].wait()

    @pl.when(owner == 1)
    def _():
        rows[1].wait()

    low = low_ref[...]
    raise_q, raise_v = raising_of(raise_s)
    dquery = dquery_s[...]
    dvalue = dvalue_s[...]
    lane = lax.broadcasted_iota(jnp.int32, (HALF, 2 * RANK), 1)
    up_s[...] += jnp.where(lane < RANK, dot(dquery, low), dot(dvalue, low))
    inner_t = (dot(raise_q, dquery) + dot(raise_v, dvalue)).astype(BF16)
    down_s[...] += dot(inner_t, normed_s[owner])

    @pl.when(owner == 1)
    def _():
        down = down_s[...].T.reshape(SHARDS, BLOCK, 2 * RANK)
        first = down[:, :UPS].reshape(SHARDS * UPS, 2 * RANK)
        second = down[:, UPS:].reshape(SHARDS * UPS, 2 * RANK)
        keep_ref[...] = jnp.where(core == 0, first, second)
        send_ref[...] = jnp.where(core == 0, second, first).astype(BF16)
        up_ref[...] = up_s[...]


def backward(core, soft, saved, normed, masked, whole, out_own, out_other):
    anywhere = pl.BlockSpec(memory_space=pl.ANY)
    grid = pltpu.PrefetchScalarGridSpec(
        num_scalar_prefetch=1,
        grid=(2,),
        in_specs=[
            pl.BlockSpec(memory_space=SMEM),
            pl.BlockSpec((None, FOCI, PACKED, PACKED), lambda o, c: (o, 0, 0, 0)),
            pl.BlockSpec((None, 3 * HALF, PACKED), lambda o, c: (o, 0, 0)),
            pl.BlockSpec((None, PACKED, 2 * RANK), lambda o, c: (o, 0, 0)),
            pl.BlockSpec((None, HALF, PACKED), lambda o, c: (o, 0, 0)),
            pl.BlockSpec((None, 8, PACKED), lambda o, c: (o, 0, 0)),
        ]
        + [anywhere] * 7,
        out_specs=[
            pl.BlockSpec((SHARDS * UPS, 2 * RANK), lambda o, c: (0, 0)),
            pl.BlockSpec((SHARDS * UPS, 2 * RANK), lambda o, c: (0, 0)),
            pl.BlockSpec((HALF, 2 * RANK), lambda o, c: (0, 0)),
        ],
        scratch_shapes=[
            pltpu.VMEM((2, PACKED, WIDE), BF16),
            pltpu.VMEM((2, PACKED, WIDE), BF16),
            pltpu.VMEM((2, WIDE // 2, QUARTER), BF16),
            pltpu.VMEM((2, HALF, WIDE // 2), BF16),
            pltpu.VMEM((WIDE // 2, 2 * RANK), BF16),
            pltpu.VMEM((HALF, PACKED), F32),
            pltpu.VMEM((HALF, PACKED), BF16),
            pltpu.VMEM((HALF, PACKED), BF16),
            pltpu.VMEM((2 * RANK, WIDE), F32),
            pltpu.VMEM((HALF, 2 * RANK), F32),
            pltpu.SemaphoreType.DMA((2,)),
            pltpu.SemaphoreType.DMA((2,)),
            pltpu.SemaphoreType.DMA((2,)),
            pltpu.SemaphoreType.DMA,
        ],
    )
    return pl.pallas_call(
        backward_kernel,
        grid_spec=grid,
        out_shape=(
            jax.ShapeDtypeStruct((SHARDS * UPS, 2 * RANK), F32),
            jax.ShapeDtypeStruct((SHARDS * UPS, 2 * RANK), BF16),
            jax.ShapeDtypeStruct((HALF, 2 * RANK), F32),
        ),
        compiler_params=pltpu.CompilerParams(
            vmem_limit_bytes=60 << 20, dimension_semantics=("arbitrary",)
        ),
        cost_estimate=pl.CostEstimate(flops=8 << 30, bytes_accessed=16 << 20, transcendentals=0),
        name="backward",
    )(core, soft, *saved, *normed, *masked, whole, out_own, out_other)


def combine_kernel(core_ref, keep_ref, come_ref, up_ref, parts_ref):
    down = keep_ref[...] + come_ref[...].astype(F32)
    up = up_ref[...]
    none = jnp.zeros_like(up)
    low_half = core_ref[0] == 0
    up = jnp.concatenate([jnp.where(low_half, up, none), jnp.where(low_half, none, up)], axis=0)
    shape = (SHARDS, UPS, 2 * RANK)
    parts = jnp.concatenate([down.reshape(shape), up.reshape(shape)], axis=1)
    parts_ref[...] = parts.reshape(parts_ref.shape).astype(BF16)


def combine(core, keep, come, up):
    return pl.pallas_call(
        combine_kernel,
        out_shape=jax.ShapeDtypeStruct((SHARDS * GRAD, 2 * RANK), BF16),
        in_specs=[pl.BlockSpec(memory_space=SMEM)] + [pl.BlockSpec(memory_space=VMEM)] * 3,
        out_specs=pl.BlockSpec(memory_space=VMEM),
        compiler_params=pltpu.CompilerParams(vmem_limit_bytes=8 << 20),
        name="combine",
    )(core, keep, come, up)


def finish_kernel(core_ref, owner_ref, live_ref, context_ref, x_ref, *refs):
    *out_refs, block_ref = refs
    core = core_ref[0]
    place, step = spread(slot_places(owner_ref), (ROWS, 1), 0)
    target = place * LEN + step
    slots = lax.broadcasted_iota(jnp.int32, (ROWS, PACKED), 1)
    select = jnp.where(slots == target, 1.0, 0.0).astype(BF16)
    lives, _ = spread([live_ref[p] for p in range(PANELS)], (ROWS, 1), 0)
    halves = []
    for half in range(2):
        parts = []
        for o in range(OWNERS):
            source = o // 2 * 2 + half
            first = 0 if source == o else SLOTS * LEN
            parts.append(context_ref[source, first : first + SLOTS * LEN, :])
        halves.append(dot(select, jnp.concatenate(parts, axis=0)).astype(BF16))
    for n, ref in enumerate(out_refs):
        side = core if n < 2 else 1 - core
        first = pl.multiple_of(side * (WIDE // 2) + n % 2 * QUARTER, QUARTER)
        columns = pl.ds(first, QUARTER)
        attended = dot(halves[0], ref[:HALF, :]) + dot(halves[1], ref[HALF:, :])
        added = jnp.where(step < lives, attended, 0.0)
        block_ref[:, columns] = (x_ref[:, columns].astype(F32) + added).astype(BF16)


def finish(core, owners, lives, context, x, outs):
    return pl.pallas_call(
        finish_kernel,
        out_shape=jax.ShapeDtypeStruct((ROWS, WIDE), BF16),
        in_specs=[pl.BlockSpec(memory_space=SMEM)] * 3 + [pl.BlockSpec(memory_space=VMEM)] * 6,
        out_specs=pl.BlockSpec(memory_space=VMEM),
        compiler_params=pltpu.CompilerParams(vmem_limit_bytes=40 << 20),
        cost_estimate=pl.CostEstimate(
            flops=2 * ROWS * 2 * HALF * (WIDE + PACKED), bytes_accessed=6 << 20, transcendentals=0
        ),
        name="finish",
    )(core, owners, lives, context, x, *outs)


def add_shards_kernel(part_ref, total_ref):
    total = part_ref[0].astype(F32)
    for t in range(1, SHARDS):
        total = total + part_ref[t].astype(F32)
    total = total.astype(BF16)
    for o in range(OWNERS):
        total_ref[o] = total


def add_shards(parts):
    return pl.pallas_call(
        add_shards_kernel,
        out_shape=jax.ShapeDtypeStruct((OWNERS, GRAD, 2 * RANK), BF16),
        in_specs=[pl.BlockSpec(memory_space=VMEM)],
        out_specs=pl.BlockSpec(memory_space=VMEM),
        compiler_params=pltpu.CompilerParams(vmem_limit_bytes=8 << 20),
        name="add_shards",
    )(parts)


def add_owners_kernel(part_ref, down_ref, up_ref):
    downs = [jnp.zeros((UPS, 2 * RANK), F32)] * 2
    up = jnp.zeros((UPS, 2 * RANK), F32)
    for o in range(OWNERS):
        part = part_ref[o].astype(F32)
        downs[o % 2] = downs[o % 2] + part[:UPS, :]
        up = up + part[UPS:, :]
    down = jnp.concatenate(downs, axis=0)
    for n in range(2):
        down_ref[n] = down[:, n * RANK : (n + 1) * RANK]
        up_ref[n] = up[:, n * RANK : (n + 1) * RANK]


def add_owners(parts):
    return pl.pallas_call(
        add_owners_kernel,
        out_shape=(
            jax.ShapeDtypeStruct((2, BLOCK, RANK), F32),
            jax.ShapeDtypeStruct((2, UPS, RANK), F32),
        ),
        in_specs=[pl.BlockSpec(memory_space=VMEM)],
        out_specs=(pl.BlockSpec(memory_space=VMEM),) * 2,
        compiler_params=pltpu.CompilerParams(vmem_limit_bytes=8 << 20),
        name="add_owners",
    )(parts)


def exchange(data, axis):
    return lax.all_to_all(data, axis, split_axis=0, concat_axis=0, tiled=True)


def swap_cores(data):
    pairs = [(s, s ^ 1) for s in range(OWNERS)]
    return lax.ppermute(data, "seq", pairs)


def on_device(
    encoder_timesteps,
    tile_parent_sequence,
    tile_recording_label,
    tile_valid_timesteps,
    standardize_scaling,
    triple_projector,
    final_projector,
    lowered_maps,
    raising_maps,
    focus_softness,
    result_adjoint,
):
    core = (lax.axis_index("seq") % 2).astype(jnp.int32).reshape(1)
    shard = make_shard(
        core, triple_projector, lowered_maps, jnp.swapaxes(raising_maps, 1, 2), final_projector
    )
    whole = lax.all_gather(shard, "dp", axis=0, tiled=True)

    x = encoder_timesteps.reshape(ROWS, WIDE)
    packed = pack(
        tile_parent_sequence,
        tile_recording_label,
        tile_valid_timesteps,
        x,
        standardize_scaling.reshape(1, WIDE),
    )
    packed, adjoint = lax.optimization_barrier((packed, result_adjoint.reshape(ROWS, WIDE)))
    masked = pack_masked(tile_parent_sequence, tile_valid_timesteps, adjoint)
    packed = exchange(packed, "seq")
    packed, masked = lax.optimization_barrier((packed, masked))
    masked = exchange(masked, "seq")
    normed = [part.reshape(PACKED, WIDE + FACTS) for part in (packed, swap_cores(packed))]
    context, out_own, *saved = forward(core, focus_softness, *normed, whole)
    masked, context = lax.optimization_barrier((masked, context))
    masked = [part.reshape(PACKED, WIDE) for part in (masked, swap_cores(masked))]
    out_other = swap_cores(out_own)
    keep, send, up = backward(core, focus_softness, saved, normed, masked, whole, out_own, out_other)
    context = exchange(context.reshape(OWNERS, 2 * SLOTS * LEN, HALF), "seq")
    parts = combine(core, keep, swap_cores(send), up)
    outs = []
    for part in (out_own, out_other):
        part = part.reshape(SHARDS, BLOCK, QUARTER)
        outs += [part[:, :UPS].reshape(HIDDEN, QUARTER), part[:, UPS:].reshape(HIDDEN, QUARTER)]
    parts, context = lax.optimization_barrier((parts, context))
    parts = exchange(parts.reshape(SHARDS, GRAD, 2 * RANK), "dp")
    block_out = finish(core, tile_parent_sequence, tile_valid_timesteps, context, x, outs)
    shard_down, shard_up = add_owners(exchange(add_shards(parts), "seq"))
    return block_out.reshape(encoder_timesteps.shape), shard_down, jnp.swapaxes(shard_up, 1, 2)


def solution(mesh):
    in_specs = (
        P(("dp", "seq"), None, None),
        P(("dp", "seq")),
        P(("dp", "seq")),
        P(("dp", "seq")),
        P(),
        P("dp", None),
        P("dp", None),
        P(None, "dp", None),
        P(None, None, "dp"),
        P(),
        P(("dp", "seq"), None, None),
    )
    out_specs = (P(("dp", "seq"), None, None), P(None, "dp", None), P(None, None, "dp"))
    return jax.shard_map(
        on_device, mesh=mesh, in_specs=in_specs, out_specs=out_specs, check_vma=False
    )
```

```python
import math

import jax
import jax.numpy as jnp
from jax import lax
from jax.experimental import pallas as pl
from jax.experimental.pallas import tpu as pltpu
from jax.sharding import PartitionSpec as P

EPS_NORM = 1e-05
EPS_HEAD = 1e-06
WIDE = 1536
PANELS = 16
LEN = 16
ROWS = PANELS * LEN
OWNERS = 16
SLOTS = 2
PACKED = OWNERS * SLOTS * LEN
HEAD = 96
FOCI = 4
HALF = FOCI * HEAD
RANK = 64
SHARDS = 32
BLOCK = WIDE // SHARDS
UPS = 2 * HALF // SHARDS
GRAD = 2 * UPS
HIDDEN = 2 * HALF
QUARTER = WIDE // 4
FACTS = 128
QKVL = 3 * HALF + 2 * RANK
F32 = jnp.float32
BF16 = jnp.bfloat16
SMEM = pltpu.MemorySpace.SMEM
VMEM = pltpu.MemorySpace.VMEM


def dot(a, b):
    return lax.dot_general(a, b, (((1,), (0,)), ((), ())), preferred_element_type=F32)


def dot_nt(a, b):
    return lax.dot_general(a, b, (((1,), (1,)), ((), ())), preferred_element_type=F32)


def slot_places(owner_ref):
    owners = [owner_ref[p] for p in range(PANELS)]
    places = []
    for p in range(PANELS):
        rank = jnp.int32(0)
        for q in range(p):
            rank = rank + jnp.where(owners[q] == owners[p], 1, 0)
        places.append(owners[p] * SLOTS + rank)
    return places


def spread(scalars, shape, axis):
    index = lax.broadcasted_iota(jnp.int32, shape, axis)
    panel = index // LEN
    values = jnp.zeros(shape, jnp.int32)
    for p in range(PANELS):
        values = jnp.where(panel == p, scalars[p], values)
    return values, index % LEN


def pack_kernel(owner_ref, tag_ref, live_ref, x_ref, gain_ref, packed_ref):
    place, step = spread(slot_places(owner_ref), (1, ROWS), 1)
    target = place * LEN + step
    slots = lax.broadcasted_iota(jnp.int32, (PACKED, ROWS), 0)
    select = jnp.where(slots == target, 1.0, 0.0).astype(BF16)
    values = x_ref[...].astype(F32)
    centred = values - jnp.mean(values, axis=-1, keepdims=True)
    scaled = centred * lax.rsqrt(jnp.mean(centred * centred, axis=-1, keepdims=True) + EPS_NORM)
    normed = (scaled * gain_ref[...]).astype(BF16)
    packed_ref[:, :, :WIDE] = dot(select, normed).astype(BF16).reshape(OWNERS, SLOTS * LEN, WIDE)
    tags, step = spread([tag_ref[p] for p in range(PANELS)], (ROWS, FACTS), 0)
    lives, _ = spread([live_ref[p] for p in range(PANELS)], (ROWS, FACTS), 0)
    lane = lax.broadcasted_iota(jnp.int32, (ROWS, FACTS), 1)
    alive = jnp.where(step < lives, 1, 0)
    facts = jnp.where(lane == 0, tags, jnp.where(lane == 1, alive, 0)).astype(F32).astype(BF16)
    packed_ref[:, :, WIDE:] = dot(select, facts).astype(BF16).reshape(OWNERS, SLOTS * LEN, FACTS)


def pack(owners, tags, lives, x, gain):
    return pl.pallas_call(
        pack_kernel,
        out_shape=jax.ShapeDtypeStruct((OWNERS, SLOTS * LEN, WIDE + FACTS), BF16),
        in_specs=[pl.BlockSpec(memory_space=SMEM)] * 3 + [pl.BlockSpec(memory_space=VMEM)] * 2,
        out_specs=pl.BlockSpec(memory_space=VMEM),
        compiler_params=pltpu.CompilerParams(vmem_limit_bytes=32 << 20),
        cost_estimate=pl.CostEstimate(
            flops=2 * PACKED * ROWS * WIDE, bytes_accessed=4 * PACKED * WIDE, transcendentals=0
        ),
        name="pack",
    )(owners, tags, lives, x, gain)


def shard_kernel(core_ref, triple_ref, lowered_ref, raising_ref, final_ref, shard_ref):
    core = core_ref[0]
    for n in range(3):
        first = pl.multiple_of(n * HIDDEN + core * HALF, HALF)
        shard_ref[:, n * HALF : (n + 1) * HALF] = triple_ref[:, pl.ds(first, HALF)]
    lowered = [lowered_ref[n].astype(F32) for n in range(2)]
    shard_ref[:, 3 * HALF : QKVL] = jnp.concatenate(lowered, axis=1).astype(BF16)
    raising = jnp.concatenate([raising_ref[n].astype(F32) for n in range(2)], axis=1)
    shard_ref[:, QKVL : QKVL + 2 * RANK] = pad_rows(raising, BLOCK).astype(BF16)
    quarters = []
    for q in range(2):
        first = pl.multiple_of(core * (WIDE // 2) + q * QUARTER, QUARTER)
        quarters.append(final_ref[:, pl.ds(first, QUARTER)].astype(F32))
    shard_ref[:, QKVL + 2 * RANK :] = jnp.concatenate(quarters, axis=0).astype(BF16)


def make_shard(core, triple, lowered, raising, final):
    return pl.pallas_call(
        shard_kernel,
        out_shape=jax.ShapeDtypeStruct((BLOCK, QKVL + 2 * RANK + QUARTER), BF16),
        in_specs=[pl.BlockSpec(memory_space=SMEM)] + [pl.BlockSpec(memory_space=VMEM)] * 4,
        out_specs=pl.BlockSpec(memory_space=VMEM),
        compiler_params=pltpu.CompilerParams(vmem_limit_bytes=60 << 20),
        name="make_shard",
    )(core, triple, lowered, raising, final)


def pack_masked_kernel(owner_ref, live_ref, adjoint_ref, packed_ref):
    place, step = spread(slot_places(owner_ref), (1, ROWS), 1)
    target = place * LEN + step
    slots = lax.broadcasted_iota(jnp.int32, (PACKED, ROWS), 0)
    select = jnp.where(slots == target, 1.0, 0.0).astype(BF16)
    lives, step = spread([live_ref[p] for p in range(PANELS)], (ROWS, 1), 0)
    masked = jnp.where(step < lives, adjoint_ref[...].astype(F32), 0.0).astype(BF16)
    packed_ref[...] = dot(select, masked).astype(BF16).reshape(packed_ref.shape)


def pack_masked(owners, lives, adjoint):
    return pl.pallas_call(
        pack_masked_kernel,
        out_shape=jax.ShapeDtypeStruct((OWNERS, SLOTS * LEN, WIDE), BF16),
        in_specs=[pl.BlockSpec(memory_space=SMEM)] * 2 + [pl.BlockSpec(memory_space=VMEM)],
        out_specs=pl.BlockSpec(memory_space=VMEM),
        compiler_params=pltpu.CompilerParams(vmem_limit_bytes=32 << 20),
        cost_estimate=pl.CostEstimate(
            flops=2 * PACKED * ROWS * WIDE, bytes_accessed=4 * PACKED * WIDE, transcendentals=0
        ),
        name="pack_masked",
    )(owners, lives, adjoint)


def pad_rows(values, rows=128):
    return jnp.concatenate([values, jnp.zeros((rows - values.shape[0], values.shape[1]), values.dtype)], axis=0)


def owner_copies(sources, landing, sems):
    return [pltpu.make_async_copy(source, landing.at[o], sems.at[o]) for o, source in enumerate(sources)]


def raising_of(raise_s):
    tall = raise_s[...].astype(F32).reshape(SHARDS // 2, BLOCK, 2 * RANK)[:, :UPS]
    raising = tall.reshape(HALF, 2 * RANK).T
    row = lax.broadcasted_iota(jnp.int32, raising.shape, 0)
    raise_q = jnp.where(row < RANK, raising, 0.0).astype(BF16)
    raise_v = jnp.where(row < RANK, 0.0, raising).astype(BF16)
    return raise_q, raise_v


def unit(values):
    scale = lax.rsqrt(jnp.sum(values * values, axis=0, keepdims=True) * (1.0 / HEAD) + EPS_HEAD)
    return values * scale, scale


def forward_kernel(
    core_ref,
    soft_ref,
    mine_ref,
    other_ref,
    whole_ref,
    context_ref,
    out_ref,
    weights_ref,
    qkv_ref,
    low_ref,
    mixed_ref,
    inverse_ref,
    normed_s,
    weight_s,
    raise_s,
    base_s,
    row_sems,
    weight_sems,
    raise_sem,
    out_sem,
):
    owner = pl.program_id(0)
    core = core_ref[0]
    rows = owner_copies((mine_ref, other_ref), normed_s, row_sems)
    outs = pltpu.make_async_copy(
        whole_ref.at[:, pl.ds(QKVL + 2 * RANK, QUARTER)], out_ref, out_sem
    )
    tiles = [
        pltpu.make_async_copy(
            whole_ref.at[:, pl.ds(n * 256, 256)],
            weight_s.at[:, pl.ds(n * 256, 256)],
            weight_sems.at[n],
        )
        for n in range(QKVL // 256)
    ]
    half = pl.ds(pl.multiple_of(core * (WIDE // 2), WIDE // 2), WIDE // 2)
    raises = pltpu.make_async_copy(
        whole_ref.at[half, pl.ds(QKVL, 2 * RANK)], raise_s, raise_sem
    )

    @pl.when(owner == 0)
    def _():
        rows[0].start()
        for tile in tiles:
            tile.start()
        raises.start()
        rows[1].start()
        outs.start()
        rows[0].wait()

    @pl.when(owner == 1)
    def _():
        rows[1].wait()
        outs.wait()

    for n, tile in enumerate(tiles):

        @pl.when(owner == 0)
        def _():
            tile.wait()

        columns = slice(n * 256, (n + 1) * 256)
        base_s[:, columns] = dot(normed_s[owner, :, :WIDE], weight_s[:, columns])

    @pl.when(owner == 0)
    def _():
        raises.wait()

    low = base_s[:, 3 * HALF :].astype(BF16)
    low_ref[...] = low
    raise_q, raise_v = raising_of(raise_s)
    query = (base_s[:, :HALF] + dot(low, raise_q)).astype(BF16).astype(F32).T
    key = base_s[:, HALF : 2 * HALF].astype(BF16).astype(F32).T
    value = (base_s[:, 2 * HALF : 3 * HALF] + dot(low, raise_v)).astype(BF16).astype(F32).T
    qkv_ref[:HALF, :] = query.astype(BF16)
    qkv_ref[HALF : 2 * HALF, :] = key.astype(BF16)
    qkv_ref[2 * HALF :, :] = value.astype(BF16)

    rows_j = lax.broadcasted_iota(jnp.int32, (PACKED, PACKED), 0)
    rows_i = lax.broadcasted_iota(jnp.int32, (PACKED, PACKED), 1)
    facts = normed_s[owner, :, WIDE:].astype(F32)
    codes = jnp.where(facts[:, 1:2] > 0.5, facts[:, 0:1], -1.0)
    allowed = (facts.T[0:1, :] == codes) | (rows_j == rows_i)
    ones_rows = jnp.where(lax.broadcasted_iota(jnp.int32, (32, PACKED), 0) < 2, 1.0, 0.0)

    for h in range(FOCI):
        head = slice(h * HEAD, (h + 1) * HEAD)
        temper = soft_ref[core * FOCI + h] * (1.0 / HEAD)
        qn, _ = unit(query[head, :])
        kn, _ = unit(key[head, :])
        qs = pad_rows(qn * (temper * math.log2(math.e))).astype(BF16)
        v = jnp.concatenate([value[head, :], ones_rows], axis=0)
        scores = dot(pad_rows(kn).T.astype(BF16), qs)
        unnormed = jnp.exp2(jnp.where(allowed, scores, -1e30)).astype(BF16)
        weights_ref[h] = unnormed
        mixed = dot(v.astype(BF16), unnormed)
        inverse = 1.0 / mixed[HEAD : HEAD + 1, :]
        inverse_ref[h : h + 1, :] = inverse
        mixed_ref[head, :] = mixed[:HEAD, :] * inverse

    context_ref[...] = mixed_ref[...].T.astype(BF16).reshape(context_ref.shape)


def forward(core, soft, mine, other, whole):
    anywhere = pl.BlockSpec(memory_space=pl.ANY)
    grid = pltpu.PrefetchScalarGridSpec(
        num_scalar_prefetch=1,
        grid=(2,),
        in_specs=[
            pl.BlockSpec(memory_space=SMEM),
        ]
        + [anywhere] * 3,
        out_specs=[
            pl.BlockSpec((OWNERS, None, SLOTS * LEN, HALF), lambda o, c: (0, o, 0, 0)),
            pl.BlockSpec((WIDE, QUARTER), lambda o, c: (0, 0)),
            pl.BlockSpec((None, FOCI, PACKED, PACKED), lambda o, c: (o, 0, 0, 0)),
            pl.BlockSpec((None, 3 * HALF, PACKED), lambda o, c: (o, 0, 0)),
            pl.BlockSpec((None, PACKED, 2 * RANK), lambda o, c: (o, 0, 0)),
            pl.BlockSpec((None, HALF, PACKED), lambda o, c: (o, 0, 0)),
            pl.BlockSpec((None, 8, PACKED), lambda o, c: (o, 0, 0)),
        ],
        scratch_shapes=[
            pltpu.VMEM((2, PACKED, WIDE + FACTS), BF16),
            pltpu.VMEM((WIDE, QKVL), BF16),
            pltpu.VMEM((WIDE // 2, 2 * RANK), BF16),
            pltpu.VMEM((PACKED, QKVL), F32),
            pltpu.SemaphoreType.DMA((2,)),
            pltpu.SemaphoreType.DMA((QKVL // 256,)),
            pltpu.SemaphoreType.DMA,
            pltpu.SemaphoreType.DMA,
        ],
    )
    return pl.pallas_call(
        forward_kernel,
        grid_spec=grid,
        out_shape=(
            jax.ShapeDtypeStruct((OWNERS, 2, SLOTS * LEN, HALF), BF16),
            jax.ShapeDtypeStruct((WIDE, QUARTER), BF16),
            jax.ShapeDtypeStruct((2, FOCI, PACKED, PACKED), BF16),
            jax.ShapeDtypeStruct((2, 3 * HALF, PACKED), BF16),
            jax.ShapeDtypeStruct((2, PACKED, 2 * RANK), BF16),
            jax.ShapeDtypeStruct((2, HALF, PACKED), F32),
            jax.ShapeDtypeStruct((2, 8, PACKED), F32),
        ),
        compiler_params=pltpu.CompilerParams(
            vmem_limit_bytes=60 << 20, dimension_semantics=("arbitrary",)
        ),
        cost_estimate=pl.CostEstimate(
            flops=6 << 30, bytes_accessed=16 << 20, transcendentals=2 * FOCI * PACKED * PACKED
        ),
        name="forward",
    )(core, soft, mine, other, whole)


def backward_kernel(
    core_ref,
    soft_ref,
    weights_ref,
    qkv_ref,
    low_ref,
    mixed_ref,
    inverse_ref,
    mine_ref,
    other_ref,
    masked_mine_ref,
    masked_other_ref,
    whole_ref,
    out_own_ref,
    out_other_ref,
    keep_ref,
    send_ref,
    up_ref,
    normed_s,
    masked_s,
    out_s,
    tight_s,
    raise_s,
    cot_s,
    dquery_s,
    dvalue_s,
    down_s,
    up_s,
    row_sems,
    masked_sems,
    out_sems,
    raise_sem,
):
    owner = pl.program_id(0)
    core = core_ref[0]
    body = pl.ds(0, WIDE)
    rows = owner_copies((mine_ref.at[:, body], other_ref.at[:, body]), normed_s, row_sems)
    masks = owner_copies((masked_mine_ref, masked_other_ref), masked_s, masked_sems)
    half = pl.ds(pl.multiple_of(core * (WIDE // 2), WIDE // 2), WIDE // 2)
    raises = pltpu.make_async_copy(
        whole_ref.at[half, pl.ds(QKVL, 2 * RANK)], raise_s, raise_sem
    )
    outs = owner_copies(
        (out_own_ref.at[half, :], out_other_ref.at[half, :]),
        out_s,
        out_sems,
    )

    @pl.when(owner == 0)
    def _():
        masks[0].start()
        outs[0].start()
        outs[1].start()
        rows[0].start()
        raises.start()
        masks[1].start()
        rows[1].start()
        down_s[...] = jnp.zeros_like(down_s)
        up_s[...] = jnp.zeros_like(up_s)
        masks[0].wait()
        for n, out in enumerate(outs):
            out.wait()
            tall = out_s[n].astype(F32).reshape(SHARDS // 2, BLOCK, QUARTER)
            for q in range(2):
                tight = tall[:, q * UPS : (q + 1) * UPS].reshape(HALF, QUARTER)
                tight_s[n, :, q * QUARTER : (q + 1) * QUARTER] = tight.astype(BF16)

    @pl.when(owner == 1)
    def _():
        masks[1].wait()

    total = jnp.zeros((HALF, PACKED), F32)
    for n, side in enumerate((core, 1 - core)):
        columns = pl.ds(pl.multiple_of(side * (WIDE // 2), WIDE // 2), WIDE // 2)
        total = total + dot_nt(tight_s[n], masked_s[owner, :, columns])
    cot_s[...] = total.astype(BF16).astype(F32)

    ones_rows = jnp.where(lax.broadcasted_iota(jnp.int32, (32, PACKED), 0) < 2, 1.0, 0.0)
    sub = lax.broadcasted_iota(jnp.int32, (32, PACKED), 0)

    for h in range(FOCI):
        head = slice(h * HEAD, (h + 1) * HEAD)
        temper = soft_ref[core * FOCI + h] * (1.0 / HEAD)
        qn, rq = unit(qkv_ref[head, :].astype(F32))
        kn, _ = unit(qkv_ref[HALF + h * HEAD : HALF + (h + 1) * HEAD, :].astype(F32))
        value = qkv_ref[2 * HALF + h * HEAD : 2 * HALF + (h + 1) * HEAD, :].astype(F32)
        v = jnp.concatenate([value, ones_rows], axis=0)
        unnormed = weights_ref[h]
        dc = (cot_s[head, :] * inverse_ref[h : h + 1, :]).astype(BF16)
        shift = jnp.sum(dc.astype(F32) * mixed_ref[head, :], axis=0, keepdims=True)
        shift_top = shift.astype(BF16).astype(F32)
        extra = jnp.where(sub == 0, -shift_top, jnp.where(sub == 1, shift_top - shift, 0.0))
        dc = jnp.concatenate([dc, extra.astype(BF16)], axis=0)
        inner = dot(v.T.astype(BF16), dc)
        dscores = (unnormed.astype(F32) * inner).astype(BF16)
        dqn = dot(pad_rows(kn).astype(BF16), dscores)[:HEAD, :] * temper
        dq = rq * (dqn - qn * (jnp.sum(qn * dqn, axis=0, keepdims=True) * (1.0 / HEAD)))
        dquery_s[head, :] = dq.astype(BF16)
        dv = dot_nt(unnormed, dc)
        dvalue_s[head, :] = dv.T[:HEAD, :].astype(BF16)

    @pl.when(owner == 0)
    def _():
        raises.wait()
        rows[0].wait()

    @pl.when(owner == 1)
    def _():
        rows[1].wait()

    low = low_ref[...]
    raise_q, raise_v = raising_of(raise_s)
    dquery = dquery_s[...]
    dvalue = dvalue_s[...]
    lane = lax.broadcasted_iota(jnp.int32, (HALF, 2 * RANK), 1)
    up_s[...] += jnp.where(lane < RANK, dot(dquery, low), dot(dvalue, low))
    inner_t = (dot(raise_q, dquery) + dot(raise_v, dvalue)).astype(BF16)
    down_s[...] += dot(inner_t, normed_s[owner])

    @pl.when(owner == 1)
    def _():
        down = down_s[...].T.reshape(SHARDS, BLOCK, 2 * RANK)
        first = down[:, :UPS].reshape(SHARDS * UPS, 2 * RANK)
        second = down[:, UPS:].reshape(SHARDS * UPS, 2 * RANK)
        keep_ref[...] = jnp.where(core == 0, first, second)
        send_ref[...] = jnp.where(core == 0, second, first).astype(BF16)
        up_ref[...] = up_s[...]


def backward(core, soft, saved, normed, masked, whole, out_own, out_other):
    anywhere = pl.BlockSpec(memory_space=pl.ANY)
    grid = pltpu.PrefetchScalarGridSpec(
        num_scalar_prefetch=1,
        grid=(2,),
        in_specs=[
            pl.BlockSpec(memory_space=SMEM),
            pl.BlockSpec((None, FOCI, PACKED, PACKED), lambda o, c: (o, 0, 0, 0)),
            pl.BlockSpec((None, 3 * HALF, PACKED), lambda o, c: (o, 0, 0)),
            pl.BlockSpec((None, PACKED, 2 * RANK), lambda o, c: (o, 0, 0)),
            pl.BlockSpec((None, HALF, PACKED), lambda o, c: (o, 0, 0)),
            pl.BlockSpec((None, 8, PACKED), lambda o, c: (o, 0, 0)),
        ]
        + [anywhere] * 7,
        out_specs=[
            pl.BlockSpec((SHARDS * UPS, 2 * RANK), lambda o, c: (0, 0)),
            pl.BlockSpec((SHARDS * UPS, 2 * RANK), lambda o, c: (0, 0)),
            pl.BlockSpec((HALF, 2 * RANK), lambda o, c: (0, 0)),
        ],
        scratch_shapes=[
            pltpu.VMEM((2, PACKED, WIDE), BF16),
            pltpu.VMEM((2, PACKED, WIDE), BF16),
            pltpu.VMEM((2, WIDE // 2, QUARTER), BF16),
            pltpu.VMEM((2, HALF, WIDE // 2), BF16),
            pltpu.VMEM((WIDE // 2, 2 * RANK), BF16),
            pltpu.VMEM((HALF, PACKED), F32),
            pltpu.VMEM((HALF, PACKED), BF16),
            pltpu.VMEM((HALF, PACKED), BF16),
            pltpu.VMEM((2 * RANK, WIDE), F32),
            pltpu.VMEM((HALF, 2 * RANK), F32),
            pltpu.SemaphoreType.DMA((2,)),
            pltpu.SemaphoreType.DMA((2,)),
            pltpu.SemaphoreType.DMA((2,)),
            pltpu.SemaphoreType.DMA,
        ],
    )
    return pl.pallas_call(
        backward_kernel,
        grid_spec=grid,
        out_shape=(
            jax.ShapeDtypeStruct((SHARDS * UPS, 2 * RANK), F32),
            jax.ShapeDtypeStruct((SHARDS * UPS, 2 * RANK), BF16),
            jax.ShapeDtypeStruct((HALF, 2 * RANK), F32),
        ),
        compiler_params=pltpu.CompilerParams(
            vmem_limit_bytes=48 << 20, dimension_semantics=("arbitrary",)
        ),
        cost_estimate=pl.CostEstimate(flops=8 << 30, bytes_accessed=16 << 20, transcendentals=0),
        name="backward",
    )(core, soft, *saved, *normed, *masked, whole, out_own, out_other)


def combine_kernel(core_ref, keep_ref, come_ref, up_ref, parts_ref):
    down = keep_ref[...] + come_ref[...].astype(F32)
    up = up_ref[...]
    none = jnp.zeros_like(up)
    low_half = core_ref[0] == 0
    up = jnp.concatenate([jnp.where(low_half, up, none), jnp.where(low_half, none, up)], axis=0)
    shape = (SHARDS, UPS, 2 * RANK)
    parts = jnp.concatenate([down.reshape(shape), up.reshape(shape)], axis=1)
    parts_ref[...] = parts.reshape(parts_ref.shape).astype(BF16)


def combine(core, keep, come, up):
    return pl.pallas_call(
        combine_kernel,
        out_shape=jax.ShapeDtypeStruct((SHARDS * GRAD, 2 * RANK), BF16),
        in_specs=[pl.BlockSpec(memory_space=SMEM)] + [pl.BlockSpec(memory_space=VMEM)] * 3,
        out_specs=pl.BlockSpec(memory_space=VMEM),
        compiler_params=pltpu.CompilerParams(vmem_limit_bytes=8 << 20),
        name="combine",
    )(core, keep, come, up)


def finish_kernel(core_ref, owner_ref, live_ref, context_ref, x_ref, *refs):
    *out_refs, block_ref = refs
    core = core_ref[0]
    place, step = spread(slot_places(owner_ref), (ROWS, 1), 0)
    target = place * LEN + step
    slots = lax.broadcasted_iota(jnp.int32, (ROWS, PACKED), 1)
    select = jnp.where(slots == target, 1.0, 0.0).astype(BF16)
    lives, _ = spread([live_ref[p] for p in range(PANELS)], (ROWS, 1), 0)
    halves = []
    for half in range(2):
        parts = []
        for o in range(OWNERS):
            source = o // 2 * 2 + half
            first = 0 if source == o else SLOTS * LEN
            parts.append(context_ref[source, first : first + SLOTS * LEN, :])
        halves.append(dot(select, jnp.concatenate(parts, axis=0)).astype(BF16))
    for n, ref in enumerate(out_refs):
        side = core if n < 2 else 1 - core
        first = pl.multiple_of(side * (WIDE // 2) + n % 2 * QUARTER, QUARTER)
        columns = pl.ds(first, QUARTER)
        attended = dot(halves[0], ref[:HALF, :]) + dot(halves[1], ref[HALF:, :])
        added = jnp.where(step < lives, attended, 0.0)
        block_ref[:, columns] = (x_ref[:, columns].astype(F32) + added).astype(BF16)


def finish(core, owners, lives, context, x, outs):
    return pl.pallas_call(
        finish_kernel,
        out_shape=jax.ShapeDtypeStruct((ROWS, WIDE), BF16),
        in_specs=[pl.BlockSpec(memory_space=SMEM)] * 3 + [pl.BlockSpec(memory_space=VMEM)] * 6,
        out_specs=pl.BlockSpec(memory_space=VMEM),
        compiler_params=pltpu.CompilerParams(vmem_limit_bytes=40 << 20),
        cost_estimate=pl.CostEstimate(
            flops=2 * ROWS * 2 * HALF * (WIDE + PACKED), bytes_accessed=6 << 20, transcendentals=0
        ),
        name="finish",
    )(core, owners, lives, context, x, *outs)


def add_shards_kernel(part_ref, total_ref):
    total = part_ref[0].astype(F32)
    for t in range(1, SHARDS):
        total = total + part_ref[t].astype(F32)
    total = total.astype(BF16)
    for o in range(OWNERS):
        total_ref[o] = total


def add_shards(parts):
    return pl.pallas_call(
        add_shards_kernel,
        out_shape=jax.ShapeDtypeStruct((OWNERS, GRAD, 2 * RANK), BF16),
        in_specs=[pl.BlockSpec(memory_space=VMEM)],
        out_specs=pl.BlockSpec(memory_space=VMEM),
        compiler_params=pltpu.CompilerParams(vmem_limit_bytes=8 << 20),
        name="add_shards",
    )(parts)


def add_owners_kernel(part_ref, down_ref, up_ref):
    downs = [jnp.zeros((UPS, 2 * RANK), F32)] * 2
    up = jnp.zeros((UPS, 2 * RANK), F32)
    for o in range(OWNERS):
        part = part_ref[o].astype(F32)
        downs[o % 2] = downs[o % 2] + part[:UPS, :]
        up = up + part[UPS:, :]
    down = jnp.concatenate(downs, axis=0)
    for n in range(2):
        down_ref[n] = down[:, n * RANK : (n + 1) * RANK]
        up_ref[n] = up[:, n * RANK : (n + 1) * RANK]


def add_owners(parts):
    return pl.pallas_call(
        add_owners_kernel,
        out_shape=(
            jax.ShapeDtypeStruct((2, BLOCK, RANK), F32),
            jax.ShapeDtypeStruct((2, UPS, RANK), F32),
        ),
        in_specs=[pl.BlockSpec(memory_space=VMEM)],
        out_specs=(pl.BlockSpec(memory_space=VMEM),) * 2,
        compiler_params=pltpu.CompilerParams(vmem_limit_bytes=8 << 20),
        name="add_owners",
    )(parts)


def exchange(data, axis):
    return lax.all_to_all(data, axis, split_axis=0, concat_axis=0, tiled=True)


def swap_cores(data):
    pairs = [(s, s ^ 1) for s in range(OWNERS)]
    return lax.ppermute(data, "seq", pairs)


def on_device(
    encoder_timesteps,
    tile_parent_sequence,
    tile_recording_label,
    tile_valid_timesteps,
    standardize_scaling,
    triple_projector,
    final_projector,
    lowered_maps,
    raising_maps,
    focus_softness,
    result_adjoint,
):
    core = (lax.axis_index("seq") % 2).astype(jnp.int32).reshape(1)
    shard = make_shard(
        core, triple_projector, lowered_maps, jnp.swapaxes(raising_maps, 1, 2), final_projector
    )
    whole = lax.all_gather(shard, "dp", axis=0, tiled=True)

    x = encoder_timesteps.reshape(ROWS, WIDE)
    packed = pack(
        tile_parent_sequence,
        tile_recording_label,
        tile_valid_timesteps,
        x,
        standardize_scaling.reshape(1, WIDE),
    )
    packed, adjoint = lax.optimization_barrier((packed, result_adjoint.reshape(ROWS, WIDE)))
    masked = pack_masked(tile_parent_sequence, tile_valid_timesteps, adjoint)
    packed = exchange(packed, "seq")
    packed, masked = lax.optimization_barrier((packed, masked))
    masked = exchange(masked, "seq")
    normed = [part.reshape(PACKED, WIDE + FACTS) for part in (packed, swap_cores(packed))]
    context, out_own, *saved = forward(core, focus_softness, *normed, whole)
    masked, context = lax.optimization_barrier((masked, context))
    masked = [part.reshape(PACKED, WIDE) for part in (masked, swap_cores(masked))]
    out_other = swap_cores(out_own)
    keep, send, up = backward(core, focus_softness, saved, normed, masked, whole, out_own, out_other)
    context = exchange(context.reshape(OWNERS, 2 * SLOTS * LEN, HALF), "seq")
    parts = combine(core, keep, swap_cores(send), up)
    outs = []
    for part in (out_own, out_other):
        part = part.reshape(SHARDS, BLOCK, QUARTER)
        outs += [part[:, :UPS].reshape(HIDDEN, QUARTER), part[:, UPS:].reshape(HIDDEN, QUARTER)]
    parts, context = lax.optimization_barrier((parts, context))
    parts = exchange(parts.reshape(SHARDS, GRAD, 2 * RANK), "dp")
    block_out = finish(core, tile_parent_sequence, tile_valid_timesteps, context, x, outs)
    shard_down, shard_up = add_owners(exchange(add_shards(parts), "seq"))
    return block_out.reshape(encoder_timesteps.shape), shard_down, jnp.swapaxes(shard_up, 1, 2)


def solution(mesh):
    in_specs = (
        P(("dp", "seq"), None, None),
        P(("dp", "seq")),
        P(("dp", "seq")),
        P(("dp", "seq")),
        P(),
        P("dp", None),
        P("dp", None),
        P(None, "dp", None),
        P(None, None, "dp"),
        P(),
        P(("dp", "seq"), None, None),
    )
    out_specs = (P(("dp", "seq"), None, None), P(None, "dp", None), P(None, None, "dp"))
    return jax.shard_map(
        on_device, mesh=mesh, in_specs=in_specs, out_specs=out_specs, check_vma=False
    )
```

```python
import math

import jax
import jax.numpy as jnp
from jax import lax
from jax.experimental import pallas as pl
from jax.experimental.pallas import tpu as pltpu
from jax.sharding import PartitionSpec as P

EPS_NORM = 1e-05
EPS_HEAD = 1e-06
WIDE = 1536
PANELS = 16
LEN = 16
ROWS = PANELS * LEN
OWNERS = 16
SLOTS = 2
PACKED = OWNERS * SLOTS * LEN
HEAD = 96
FOCI = 4
HALF = FOCI * HEAD
RANK = 64
SHARDS = 32
BLOCK = WIDE // SHARDS
UPS = 2 * HALF // SHARDS
GRAD = 2 * UPS
HIDDEN = 2 * HALF
QUARTER = WIDE // 4
FACTS = 128
QKVL = 3 * HALF + 2 * RANK
F32 = jnp.float32
BF16 = jnp.bfloat16
SMEM = pltpu.MemorySpace.SMEM
VMEM = pltpu.MemorySpace.VMEM


def dot(a, b):
    return lax.dot_general(a, b, (((1,), (0,)), ((), ())), preferred_element_type=F32)


def dot_nt(a, b):
    return lax.dot_general(a, b, (((1,), (1,)), ((), ())), preferred_element_type=F32)


def slot_places(owner_ref):
    owners = [owner_ref[p] for p in range(PANELS)]
    places = []
    for p in range(PANELS):
        rank = jnp.int32(0)
        for q in range(p):
            rank = rank + jnp.where(owners[q] == owners[p], 1, 0)
        places.append(owners[p] * SLOTS + rank)
    return places


def spread(scalars, shape, axis):
    index = lax.broadcasted_iota(jnp.int32, shape, axis)
    panel = index // LEN
    values = jnp.zeros(shape, jnp.int32)
    for p in range(PANELS):
        values = jnp.where(panel == p, scalars[p], values)
    return values, index % LEN


def pack_kernel(owner_ref, tag_ref, live_ref, x_ref, gain_ref, packed_ref):
    place, step = spread(slot_places(owner_ref), (1, ROWS), 1)
    target = place * LEN + step
    slots = lax.broadcasted_iota(jnp.int32, (PACKED, ROWS), 0)
    select = jnp.where(slots == target, 1.0, 0.0).astype(BF16)
    values = x_ref[...].astype(F32)
    centred = values - jnp.mean(values, axis=-1, keepdims=True)
    scaled = centred * lax.rsqrt(jnp.mean(centred * centred, axis=-1, keepdims=True) + EPS_NORM)
    normed = (scaled * gain_ref[...]).astype(BF16)
    packed_ref[:, :, :WIDE] = dot(select, normed).astype(BF16).reshape(OWNERS, SLOTS * LEN, WIDE)
    tags, step = spread([tag_ref[p] for p in range(PANELS)], (ROWS, FACTS), 0)
    lives, _ = spread([live_ref[p] for p in range(PANELS)], (ROWS, FACTS), 0)
    lane = lax.broadcasted_iota(jnp.int32, (ROWS, FACTS), 1)
    alive = jnp.where(step < lives, 1, 0)
    facts = jnp.where(lane == 0, tags, jnp.where(lane == 1, alive, 0)).astype(F32).astype(BF16)
    packed_ref[:, :, WIDE:] = dot(select, facts).astype(BF16).reshape(OWNERS, SLOTS * LEN, FACTS)


def pack(owners, tags, lives, x, gain):
    return pl.pallas_call(
        pack_kernel,
        out_shape=jax.ShapeDtypeStruct((OWNERS, SLOTS * LEN, WIDE + FACTS), BF16),
        in_specs=[pl.BlockSpec(memory_space=SMEM)] * 3 + [pl.BlockSpec(memory_space=VMEM)] * 2,
        out_specs=pl.BlockSpec(memory_space=VMEM),
        compiler_params=pltpu.CompilerParams(vmem_limit_bytes=32 << 20),
        cost_estimate=pl.CostEstimate(
            flops=2 * PACKED * ROWS * WIDE, bytes_accessed=4 * PACKED * WIDE, transcendentals=0
        ),
        name="pack",
    )(owners, tags, lives, x, gain)


def shard_kernel(core_ref, triple_ref, lowered_ref, raising_ref, final_ref, shard_ref):
    core = core_ref[0]
    for n in range(3):
        first = pl.multiple_of(n * HIDDEN + core * HALF, HALF)
        shard_ref[:, n * HALF : (n + 1) * HALF] = triple_ref[:, pl.ds(first, HALF)]
    lowered = [lowered_ref[n].astype(F32) for n in range(2)]
    shard_ref[:, 3 * HALF : QKVL] = jnp.concatenate(lowered, axis=1).astype(BF16)
    raising = jnp.concatenate([raising_ref[n].astype(F32) for n in range(2)], axis=1)
    shard_ref[:, QKVL : QKVL + 2 * RANK] = pad_rows(raising, BLOCK).astype(BF16)
    quarters = []
    for q in range(2):
        first = pl.multiple_of(core * (WIDE // 2) + q * QUARTER, QUARTER)
        quarters.append(final_ref[:, pl.ds(first, QUARTER)].astype(F32))
    shard_ref[:, QKVL + 2 * RANK :] = jnp.concatenate(quarters, axis=0).astype(BF16)


def make_shard(core, triple, lowered, raising, final):
    return pl.pallas_call(
        shard_kernel,
        out_shape=jax.ShapeDtypeStruct((BLOCK, QKVL + 2 * RANK + QUARTER), BF16),
        in_specs=[pl.BlockSpec(memory_space=SMEM)] + [pl.BlockSpec(memory_space=VMEM)] * 4,
        out_specs=pl.BlockSpec(memory_space=VMEM),
        compiler_params=pltpu.CompilerParams(vmem_limit_bytes=60 << 20),
        name="make_shard",
    )(core, triple, lowered, raising, final)


def pack_masked_kernel(owner_ref, live_ref, adjoint_ref, packed_ref):
    place, step = spread(slot_places(owner_ref), (1, ROWS), 1)
    target = place * LEN + step
    slots = lax.broadcasted_iota(jnp.int32, (PACKED, ROWS), 0)
    select = jnp.where(slots == target, 1.0, 0.0).astype(BF16)
    lives, step = spread([live_ref[p] for p in range(PANELS)], (ROWS, 1), 0)
    masked = jnp.where(step < lives, adjoint_ref[...].astype(F32), 0.0).astype(BF16)
    packed_ref[...] = dot(select, masked).astype(BF16).reshape(packed_ref.shape)


def pack_masked(owners, lives, adjoint):
    return pl.pallas_call(
        pack_masked_kernel,
        out_shape=jax.ShapeDtypeStruct((OWNERS, SLOTS * LEN, WIDE), BF16),
        in_specs=[pl.BlockSpec(memory_space=SMEM)] * 2 + [pl.BlockSpec(memory_space=VMEM)],
        out_specs=pl.BlockSpec(memory_space=VMEM),
        compiler_params=pltpu.CompilerParams(vmem_limit_bytes=32 << 20),
        cost_estimate=pl.CostEstimate(
            flops=2 * PACKED * ROWS * WIDE, bytes_accessed=4 * PACKED * WIDE, transcendentals=0
        ),
        name="pack_masked",
    )(owners, lives, adjoint)


def pad_rows(values, rows=128):
    return jnp.concatenate([values, jnp.zeros((rows - values.shape[0], values.shape[1]), values.dtype)], axis=0)


def owner_copies(sources, landing, sems):
    return [pltpu.make_async_copy(source, landing.at[o], sems.at[o]) for o, source in enumerate(sources)]


def raising_of(raise_s):
    tall = raise_s[...].astype(F32).reshape(SHARDS // 2, BLOCK, 2 * RANK)[:, :UPS]
    raising = tall.reshape(HALF, 2 * RANK).T
    row = lax.broadcasted_iota(jnp.int32, raising.shape, 0)
    raise_q = jnp.where(row < RANK, raising, 0.0).astype(BF16)
    raise_v = jnp.where(row < RANK, 0.0, raising).astype(BF16)
    return raise_q, raise_v


def unit(values):
    scale = lax.rsqrt(jnp.sum(values * values, axis=0, keepdims=True) * (1.0 / HEAD) + EPS_HEAD)
    return values * scale, scale


def forward_kernel(
    core_ref,
    soft_ref,
    mine_ref,
    other_ref,
    whole_ref,
    context_ref,
    out_ref,
    weights_ref,
    qkv_ref,
    low_ref,
    mixed_ref,
    inverse_ref,
    normed_s,
    weight_s,
    raise_s,
    base_s,
    row_sems,
    weight_sems,
    raise_sem,
    out_sem,
):
    owner = pl.program_id(0)
    core = core_ref[0]
    rows = owner_copies((mine_ref, other_ref), normed_s, row_sems)
    outs = pltpu.make_async_copy(
        whole_ref.at[:, pl.ds(QKVL + 2 * RANK, QUARTER)], out_ref, out_sem
    )
    tiles = [
        pltpu.make_async_copy(
            whole_ref.at[:, pl.ds(n * 256, 256)],
            weight_s.at[:, pl.ds(n * 256, 256)],
            weight_sems.at[n],
        )
        for n in range(QKVL // 256)
    ]
    half = pl.ds(pl.multiple_of(core * (WIDE // 2), WIDE // 2), WIDE // 2)
    raises = pltpu.make_async_copy(
        whole_ref.at[half, pl.ds(QKVL, 2 * RANK)], raise_s, raise_sem
    )

    @pl.when(owner == 0)
    def _():
        rows[0].start()
        for tile in tiles:
            tile.start()
        raises.start()
        rows[1].start()
        outs.start()
        rows[0].wait()

    @pl.when(owner == 1)
    def _():
        rows[1].wait()
        outs.wait()

    for n, tile in enumerate(tiles):

        @pl.when(owner == 0)
        def _():
            tile.wait()

        columns = slice(n * 256, (n + 1) * 256)
        base_s[:, columns] = dot(normed_s[owner, :, :WIDE], weight_s[:, columns])

    @pl.when(owner == 0)
    def _():
        raises.wait()

    low = base_s[:, 3 * HALF :].astype(BF16)
    low_ref[...] = low
    raise_q, raise_v = raising_of(raise_s)
    query = (base_s[:, :HALF] + dot(low, raise_q)).astype(BF16).astype(F32).T
    key = base_s[:, HALF : 2 * HALF].astype(BF16).astype(F32).T
    value = (base_s[:, 2 * HALF : 3 * HALF] + dot(low, raise_v)).astype(BF16).astype(F32).T
    qkv_ref[:HALF, :] = query.astype(BF16)
    qkv_ref[HALF : 2 * HALF, :] = key.astype(BF16)
    qkv_ref[2 * HALF :, :] = value.astype(BF16)

    rows_j = lax.broadcasted_iota(jnp.int32, (PACKED, PACKED), 0)
    rows_i = lax.broadcasted_iota(jnp.int32, (PACKED, PACKED), 1)
    facts = normed_s[owner, :, WIDE:].astype(F32)
    codes = jnp.where(facts[:, 1:2] > 0.5, facts[:, 0:1], -1.0)
    allowed = (facts.T[0:1, :] == codes) | (rows_j == rows_i)
    ones_rows = jnp.where(lax.broadcasted_iota(jnp.int32, (32, PACKED), 0) < 2, 1.0, 0.0)

    for h in range(FOCI):
        head = slice(h * HEAD, (h + 1) * HEAD)
        temper = soft_ref[core * FOCI + h] * (1.0 / HEAD)
        qn, _ = unit(query[head, :])
        kn, _ = unit(key[head, :])
        qs = pad_rows(qn * (temper * math.log2(math.e))).astype(BF16)
        v = jnp.concatenate([value[head, :], ones_rows], axis=0)
        scores = dot(pad_rows(kn).T.astype(BF16), qs)
        unnormed = jnp.exp2(jnp.where(allowed, scores, -1e30)).astype(BF16)
        weights_ref[h] = unnormed
        mixed = dot(v.astype(BF16), unnormed)
        inverse = 1.0 / mixed[HEAD : HEAD + 1, :]
        inverse_ref[h : h + 1, :] = inverse
        mixed_ref[head, :] = mixed[:HEAD, :] * inverse

    context_ref[...] = mixed_ref[...].T.astype(BF16).reshape(context_ref.shape)


def forward(core, soft, mine, other, whole):
    anywhere = pl.BlockSpec(memory_space=pl.ANY)
    grid = pltpu.PrefetchScalarGridSpec(
        num_scalar_prefetch=1,
        grid=(2,),
        in_specs=[
            pl.BlockSpec(memory_space=SMEM),
        ]
        + [anywhere] * 3,
        out_specs=[
            pl.BlockSpec((OWNERS, None, SLOTS * LEN, HALF), lambda o, c: (0, o, 0, 0)),
            pl.BlockSpec((WIDE, QUARTER), lambda o, c: (0, 0)),
            pl.BlockSpec((None, FOCI, PACKED, PACKED), lambda o, c: (o, 0, 0, 0)),
            pl.BlockSpec((None, 3 * HALF, PACKED), lambda o, c: (o, 0, 0)),
            pl.BlockSpec((None, PACKED, 2 * RANK), lambda o, c: (o, 0, 0)),
            pl.BlockSpec((None, HALF, PACKED), lambda o, c: (o, 0, 0)),
            pl.BlockSpec((None, 8, PACKED), lambda o, c: (o, 0, 0)),
        ],
        scratch_shapes=[
            pltpu.VMEM((2, PACKED, WIDE + FACTS), BF16),
            pltpu.VMEM((WIDE, QKVL), BF16),
            pltpu.VMEM((WIDE // 2, 2 * RANK), BF16),
            pltpu.VMEM((PACKED, QKVL), F32),
            pltpu.SemaphoreType.DMA((2,)),
            pltpu.SemaphoreType.DMA((QKVL // 256,)),
            pltpu.SemaphoreType.DMA,
            pltpu.SemaphoreType.DMA,
        ],
    )
    return pl.pallas_call(
        forward_kernel,
        grid_spec=grid,
        out_shape=(
            jax.ShapeDtypeStruct((OWNERS, 2, SLOTS * LEN, HALF), BF16),
            jax.ShapeDtypeStruct((WIDE, QUARTER), BF16),
            jax.ShapeDtypeStruct((2, FOCI, PACKED, PACKED), BF16),
            jax.ShapeDtypeStruct((2, 3 * HALF, PACKED), BF16),
            jax.ShapeDtypeStruct((2, PACKED, 2 * RANK), BF16),
            jax.ShapeDtypeStruct((2, HALF, PACKED), F32),
            jax.ShapeDtypeStruct((2, 8, PACKED), F32),
        ),
        compiler_params=pltpu.CompilerParams(
            vmem_limit_bytes=60 << 20, dimension_semantics=("arbitrary",)
        ),
        cost_estimate=pl.CostEstimate(
            flops=6 << 30, bytes_accessed=16 << 20, transcendentals=2 * FOCI * PACKED * PACKED
        ),
        name="forward",
    )(core, soft, mine, other, whole)


def backward_kernel(
    core_ref,
    soft_ref,
    weights_ref,
    qkv_ref,
    low_ref,
    mixed_ref,
    inverse_ref,
    mine_ref,
    other_ref,
    masked_mine_ref,
    masked_other_ref,
    whole_ref,
    out_own_ref,
    out_other_ref,
    keep_ref,
    send_ref,
    up_ref,
    normed_s,
    masked_s,
    out_s,
    tight_s,
    raise_s,
    cot_s,
    dquery_s,
    dvalue_s,
    down_s,
    up_s,
    row_sems,
    masked_sems,
    out_sems,
    raise_sem,
):
    owner = pl.program_id(0)
    core = core_ref[0]
    body = pl.ds(0, WIDE)
    rows = owner_copies((mine_ref.at[:, body], other_ref.at[:, body]), normed_s, row_sems)
    masks = owner_copies((masked_mine_ref, masked_other_ref), masked_s, masked_sems)
    half = pl.ds(pl.multiple_of(core * (WIDE // 2), WIDE // 2), WIDE // 2)
    raises = pltpu.make_async_copy(
        whole_ref.at[half, pl.ds(QKVL, 2 * RANK)], raise_s, raise_sem
    )
    outs = owner_copies(
        (out_own_ref.at[half, :], out_other_ref.at[half, :]),
        out_s,
        out_sems,
    )

    @pl.when(owner == 0)
    def _():
        masks[0].start()
        outs[0].start()
        outs[1].start()
        rows[0].start()
        raises.start()
        masks[1].start()
        rows[1].start()
        down_s[...] = jnp.zeros_like(down_s)
        up_s[...] = jnp.zeros_like(up_s)
        masks[0].wait()
        for n, out in enumerate(outs):
            out.wait()
            tall = out_s[n].astype(F32).reshape(SHARDS // 2, BLOCK, QUARTER)
            for q in range(2):
                tight = tall[:, q * UPS : (q + 1) * UPS].reshape(HALF, QUARTER)
                tight_s[n, :, q * QUARTER : (q + 1) * QUARTER] = tight.astype(BF16)

    @pl.when(owner == 1)
    def _():
        masks[1].wait()

    total = jnp.zeros((HALF, PACKED), F32)
    for n, side in enumerate((core, 1 - core)):
        columns = pl.ds(pl.multiple_of(side * (WIDE // 2), WIDE // 2), WIDE // 2)
        total = total + dot_nt(tight_s[n], masked_s[owner, :, columns])
    cot_s[...] = total.astype(BF16).astype(F32)

    ones_rows = jnp.where(lax.broadcasted_iota(jnp.int32, (32, PACKED), 0) < 2, 1.0, 0.0)
    sub = lax.broadcasted_iota(jnp.int32, (32, PACKED), 0)

    for h in range(FOCI):
        head = slice(h * HEAD, (h + 1) * HEAD)
        temper = soft_ref[core * FOCI + h] * (1.0 / HEAD)
        qn, rq = unit(qkv_ref[head, :].astype(F32))
        kn, _ = unit(qkv_ref[HALF + h * HEAD : HALF + (h + 1) * HEAD, :].astype(F32))
        value = qkv_ref[2 * HALF + h * HEAD : 2 * HALF + (h + 1) * HEAD, :].astype(F32)
        v = jnp.concatenate([value, ones_rows], axis=0)
        unnormed = weights_ref[h]
        dc = (cot_s[head, :] * inverse_ref[h : h + 1, :]).astype(BF16)
        shift = jnp.sum(dc.astype(F32) * mixed_ref[head, :], axis=0, keepdims=True)
        shift_top = shift.astype(BF16).astype(F32)
        extra = jnp.where(sub == 0, -shift_top, jnp.where(sub == 1, shift_top - shift, 0.0))
        dc = jnp.concatenate([dc, extra.astype(BF16)], axis=0)
        inner = dot(v.T.astype(BF16), dc)
        dscores = (unnormed.astype(F32) * inner).astype(BF16)
        dqn = dot(pad_rows(kn).astype(BF16), dscores)[:HEAD, :] * temper
        dq = rq * (dqn - qn * (jnp.sum(qn * dqn, axis=0, keepdims=True) * (1.0 / HEAD)))
        dquery_s[head, :] = dq.astype(BF16)
        dv = dot_nt(unnormed, dc)
        dvalue_s[head, :] = dv.T[:HEAD, :].astype(BF16)

    @pl.when(owner == 0)
    def _():
        raises.wait()
        rows[0].wait()

    @pl.when(owner == 1)
    def _():
        rows[1].wait()

    low = low_ref[...]
    raise_q, raise_v = raising_of(raise_s)
    dquery = dquery_s[...]
    dvalue = dvalue_s[...]
    lane = lax.broadcasted_iota(jnp.int32, (HALF, 2 * RANK), 1)
    up_s[...] += jnp.where(lane < RANK, dot(dquery, low), dot(dvalue, low))
    inner_t = (dot(raise_q, dquery) + dot(raise_v, dvalue)).astype(BF16)
    down_s[...] += dot(inner_t, normed_s[owner])

    @pl.when(owner == 1)
    def _():
        down = down_s[...].T.reshape(SHARDS, BLOCK, 2 * RANK)
        first = down[:, :UPS].reshape(SHARDS * UPS, 2 * RANK)
        second = down[:, UPS:].reshape(SHARDS * UPS, 2 * RANK)
        keep_ref[...] = jnp.where(core == 0, first, second)
        send_ref[...] = jnp.where(core == 0, second, first).astype(BF16)
        up_ref[...] = up_s[...]


def backward(core, soft, saved, normed, masked, whole, out_own, out_other):
    anywhere = pl.BlockSpec(memory_space=pl.ANY)
    grid = pltpu.PrefetchScalarGridSpec(
        num_scalar_prefetch=1,
        grid=(2,),
        in_specs=[
            pl.BlockSpec(memory_space=SMEM),
            pl.BlockSpec((None, FOCI, PACKED, PACKED), lambda o, c: (o, 0, 0, 0)),
            pl.BlockSpec((None, 3 * HALF, PACKED), lambda o, c: (o, 0, 0)),
            pl.BlockSpec((None, PACKED, 2 * RANK), lambda o, c: (o, 0, 0)),
            pl.BlockSpec((None, HALF, PACKED), lambda o, c: (o, 0, 0)),
            pl.BlockSpec((None, 8, PACKED), lambda o, c: (o, 0, 0)),
        ]
        + [anywhere] * 7,
        out_specs=[
            pl.BlockSpec((SHARDS * UPS, 2 * RANK), lambda o, c: (0, 0)),
            pl.BlockSpec((SHARDS * UPS, 2 * RANK), lambda o, c: (0, 0)),
            pl.BlockSpec((HALF, 2 * RANK), lambda o, c: (0, 0)),
        ],
        scratch_shapes=[
            pltpu.VMEM((2, PACKED, WIDE), BF16),
            pltpu.VMEM((2, PACKED, WIDE), BF16),
            pltpu.VMEM((2, WIDE // 2, QUARTER), BF16),
            pltpu.VMEM((2, HALF, WIDE // 2), BF16),
            pltpu.VMEM((WIDE // 2, 2 * RANK), BF16),
            pltpu.VMEM((HALF, PACKED), F32),
            pltpu.VMEM((HALF, PACKED), BF16),
            pltpu.VMEM((HALF, PACKED), BF16),
            pltpu.VMEM((2 * RANK, WIDE), F32),
            pltpu.VMEM((HALF, 2 * RANK), F32),
            pltpu.SemaphoreType.DMA((2,)),
            pltpu.SemaphoreType.DMA((2,)),
            pltpu.SemaphoreType.DMA((2,)),
            pltpu.SemaphoreType.DMA,
        ],
    )
    return pl.pallas_call(
        backward_kernel,
        grid_spec=grid,
        out_shape=(
            jax.ShapeDtypeStruct((SHARDS * UPS, 2 * RANK), F32),
            jax.ShapeDtypeStruct((SHARDS * UPS, 2 * RANK), BF16),
            jax.ShapeDtypeStruct((HALF, 2 * RANK), F32),
        ),
        compiler_params=pltpu.CompilerParams(
            vmem_limit_bytes=59 << 20, dimension_semantics=("arbitrary",)
        ),
        cost_estimate=pl.CostEstimate(flops=8 << 30, bytes_accessed=16 << 20, transcendentals=0),
        name="backward",
    )(core, soft, *saved, *normed, *masked, whole, out_own, out_other)


def combine_kernel(core_ref, keep_ref, come_ref, up_ref, parts_ref):
    down = keep_ref[...] + come_ref[...].astype(F32)
    up = up_ref[...]
    none = jnp.zeros_like(up)
    low_half = core_ref[0] == 0
    up = jnp.concatenate([jnp.where(low_half, up, none), jnp.where(low_half, none, up)], axis=0)
    shape = (SHARDS, UPS, 2 * RANK)
    parts = jnp.concatenate([down.reshape(shape), up.reshape(shape)], axis=1)
    parts_ref[...] = parts.reshape(parts_ref.shape).astype(BF16)


def combine(core, keep, come, up):
    return pl.pallas_call(
        combine_kernel,
        out_shape=jax.ShapeDtypeStruct((SHARDS * GRAD, 2 * RANK), BF16),
        in_specs=[pl.BlockSpec(memory_space=SMEM)] + [pl.BlockSpec(memory_space=VMEM)] * 3,
        out_specs=pl.BlockSpec(memory_space=VMEM),
        compiler_params=pltpu.CompilerParams(vmem_limit_bytes=8 << 20),
        name="combine",
    )(core, keep, come, up)


def finish_kernel(core_ref, owner_ref, live_ref, context_ref, x_ref, *refs):
    *out_refs, block_ref = refs
    core = core_ref[0]
    place, step = spread(slot_places(owner_ref), (ROWS, 1), 0)
    target = place * LEN + step
    slots = lax.broadcasted_iota(jnp.int32, (ROWS, PACKED), 1)
    select = jnp.where(slots == target, 1.0, 0.0).astype(BF16)
    lives, _ = spread([live_ref[p] for p in range(PANELS)], (ROWS, 1), 0)
    halves = []
    for half in range(2):
        parts = []
        for o in range(OWNERS):
            source = o // 2 * 2 + half
            first = 0 if source == o else SLOTS * LEN
            parts.append(context_ref[source, first : first + SLOTS * LEN, :])
        halves.append(dot(select, jnp.concatenate(parts, axis=0)).astype(BF16))
    for n, ref in enumerate(out_refs):
        side = core if n < 2 else 1 - core
        first = pl.multiple_of(side * (WIDE // 2) + n % 2 * QUARTER, QUARTER)
        columns = pl.ds(first, QUARTER)
        attended = dot(halves[0], ref[:HALF, :]) + dot(halves[1], ref[HALF:, :])
        added = jnp.where(step < lives, attended, 0.0)
        block_ref[:, columns] = (x_ref[:, columns].astype(F32) + added).astype(BF16)


def finish(core, owners, lives, context, x, outs):
    return pl.pallas_call(
        finish_kernel,
        out_shape=jax.ShapeDtypeStruct((ROWS, WIDE), BF16),
        in_specs=[pl.BlockSpec(memory_space=SMEM)] * 3 + [pl.BlockSpec(memory_space=VMEM)] * 6,
        out_specs=pl.BlockSpec(memory_space=VMEM),
        compiler_params=pltpu.CompilerParams(vmem_limit_bytes=40 << 20),
        cost_estimate=pl.CostEstimate(
            flops=2 * ROWS * 2 * HALF * (WIDE + PACKED), bytes_accessed=6 << 20, transcendentals=0
        ),
        name="finish",
    )(core, owners, lives, context, x, *outs)


def add_shards_kernel(part_ref, total_ref):
    total = part_ref[0].astype(F32)
    for t in range(1, SHARDS):
        total = total + part_ref[t].astype(F32)
    total = total.astype(BF16)
    for o in range(OWNERS):
        total_ref[o] = total


def add_shards(parts):
    return pl.pallas_call(
        add_shards_kernel,
        out_shape=jax.ShapeDtypeStruct((OWNERS, GRAD, 2 * RANK), BF16),
        in_specs=[pl.BlockSpec(memory_space=VMEM)],
        out_specs=pl.BlockSpec(memory_space=VMEM),
        compiler_params=pltpu.CompilerParams(vmem_limit_bytes=8 << 20),
        name="add_shards",
    )(parts)


def add_owners_kernel(part_ref, down_ref, up_ref):
    downs = [jnp.zeros((UPS, 2 * RANK), F32)] * 2
    up = jnp.zeros((UPS, 2 * RANK), F32)
    for o in range(OWNERS):
        part = part_ref[o].astype(F32)
        downs[o % 2] = downs[o % 2] + part[:UPS, :]
        up = up + part[UPS:, :]
    down = jnp.concatenate(downs, axis=0)
    for n in range(2):
        down_ref[n] = down[:, n * RANK : (n + 1) * RANK]
        up_ref[n] = up[:, n * RANK : (n + 1) * RANK]


def add_owners(parts):
    return pl.pallas_call(
        add_owners_kernel,
        out_shape=(
            jax.ShapeDtypeStruct((2, BLOCK, RANK), F32),
            jax.ShapeDtypeStruct((2, UPS, RANK), F32),
        ),
        in_specs=[pl.BlockSpec(memory_space=VMEM)],
        out_specs=(pl.BlockSpec(memory_space=VMEM),) * 2,
        compiler_params=pltpu.CompilerParams(vmem_limit_bytes=8 << 20),
        name="add_owners",
    )(parts)


def exchange(data, axis):
    return lax.all_to_all(data, axis, split_axis=0, concat_axis=0, tiled=True)


def swap_cores(data):
    pairs = [(s, s ^ 1) for s in range(OWNERS)]
    return lax.ppermute(data, "seq", pairs)


def on_device(
    encoder_timesteps,
    tile_parent_sequence,
    tile_recording_label,
    tile_valid_timesteps,
    standardize_scaling,
    triple_projector,
    final_projector,
    lowered_maps,
    raising_maps,
    focus_softness,
    result_adjoint,
):
    core = (lax.axis_index("seq") % 2).astype(jnp.int32).reshape(1)
    shard = make_shard(
        core, triple_projector, lowered_maps, jnp.swapaxes(raising_maps, 1, 2), final_projector
    )
    whole = lax.all_gather(shard, "dp", axis=0, tiled=True)

    x = encoder_timesteps.reshape(ROWS, WIDE)
    packed = pack(
        tile_parent_sequence,
        tile_recording_label,
        tile_valid_timesteps,
        x,
        standardize_scaling.reshape(1, WIDE),
    )
    packed, adjoint = lax.optimization_barrier((packed, result_adjoint.reshape(ROWS, WIDE)))
    masked = pack_masked(tile_parent_sequence, tile_valid_timesteps, adjoint)
    packed = exchange(packed, "seq")
    packed, masked = lax.optimization_barrier((packed, masked))
    masked = exchange(masked, "seq")
    normed = [part.reshape(PACKED, WIDE + FACTS) for part in (packed, swap_cores(packed))]
    context, out_own, *saved = forward(core, focus_softness, *normed, whole)
    masked, context = lax.optimization_barrier((masked, context))
    masked = [part.reshape(PACKED, WIDE) for part in (masked, swap_cores(masked))]
    out_other = swap_cores(out_own)
    keep, send, up = backward(core, focus_softness, saved, normed, masked, whole, out_own, out_other)
    context = exchange(context.reshape(OWNERS, 2 * SLOTS * LEN, HALF), "seq")
    parts = combine(core, keep, swap_cores(send), up)
    outs = []
    for part in (out_own, out_other):
        part = part.reshape(SHARDS, BLOCK, QUARTER)
        outs += [part[:, :UPS].reshape(HIDDEN, QUARTER), part[:, UPS:].reshape(HIDDEN, QUARTER)]
    parts, context = lax.optimization_barrier((parts, context))
    parts = exchange(parts.reshape(SHARDS, GRAD, 2 * RANK), "dp")
    block_out = finish(core, tile_parent_sequence, tile_valid_timesteps, context, x, outs)
    shard_down, shard_up = add_owners(exchange(add_shards(parts), "seq"))
    return block_out.reshape(encoder_timesteps.shape), shard_down, jnp.swapaxes(shard_up, 1, 2)


def solution(mesh):
    in_specs = (
        P(("dp", "seq"), None, None),
        P(("dp", "seq")),
        P(("dp", "seq")),
        P(("dp", "seq")),
        P(),
        P("dp", None),
        P("dp", None),
        P(None, "dp", None),
        P(None, None, "dp"),
        P(),
        P(("dp", "seq"), None, None),
    )
    out_specs = (P(("dp", "seq"), None, None), P(None, "dp", None), P(None, None, "dp"))
    return jax.shard_map(
        on_device, mesh=mesh, in_specs=in_specs, out_specs=out_specs, check_vma=False
    )
```
